32 devices in a mesh: grp: 4 (over y, core), dev: 8 (over z, x).
Axes of the slice: x: 2, y: 2, z: 4, core: 2. Of those that a mesh axis runs over, the one named last changes fastest.
Arguments:
- row_panel: bfloat16 [8, 512, 512], P('grp', 'dev'), may hold values from -3 to 3
- col_near: bfloat16 [32, 512, 512], P('dev', 'grp'), may hold values from -3 to 3
- col_far: bfloat16 [32, 2, 48, 512], P('dev', None, 'grp'), may hold values from -0.4375 to 0.4375
- near_tiles: bfloat16 [256, 512, 512], P(('grp', 'dev')), may hold values from -6 to 6
- near_rows: int32 [32, 8], P(('grp', 'dev')), may hold values from 0 to 1, as said below
- near_cols: int32 [32, 8], replicated, may hold values from 0 to 31, as said below
- far_tiles: bfloat16 [256, 2, 48, 512], P(('grp', 'dev')), may hold values from -6 to 6
- far_rows: int32 [32, 8], P(('grp', 'dev')), may hold values from 0 to 1, as said below
- far_cols: int32 [32, 8], replicated, may hold values from 0 to 31, as said below
Outputs:
- near_out: bfloat16 [256, 512, 512], P(('grp', 'dev'))
- far_out: bfloat16 [256, 48, 512], P(('grp', 'dev'))
The draws below stay inside these ranges and needn't reach their ends.
Inputs may be any that keep to these rules, and one draw needn't show every extreme that they name: `near_rows`: for every row group and every slot s, the 8 devices of the group hold in their near slot s every near tile of that group whose column lies in bucket s (columns s * 4 to (s + 1) * 4 - 1), each exactly once. near_cols[f, s] lies in bucket s, from s * 4 to (s + 1) * 4 - 1. `far_rows`: for every row group and every slot s, the 8 devices of the group hold in their far slot s every far tile of that group whose column lies in bucket s, each exactly once. far_cols[f, s] lies in bucket s, from s * 4 to (s + 1) * 4 - 1.
All inputs are finite; a program needn't handle non-finite values.
Results may differ from the reference program's by a relative error of at most 0.001.
Values may be sent and summed in bfloat16 or wider, within the bound.
No kernel may reach another device: no remote copies, remote signals or barrier semaphores. Data moves between devices by JAX's collectives and lax.ppermute only.
A program may use at most 128 MiB of HBM per device.

```python
import jax
import jax.numpy as jnp
from jax import lax

B = 512
R = 48
ROW_GRP = 2
NEAR_COLS = 32
FAR_COLS = 32
ROWS = 8
N_GRP = 4
N_DEV = 8
DEVICES = 32


def slot_tables(key, salt):
    key = jax.random.fold_in(key, salt)
    scores = jax.random.randint(key, (N_GRP, N_DEV, N_DEV), 0, 1 << 20) * N_DEV + jnp.arange(N_DEV, dtype=jnp.int32)
    order = jnp.argsort(scores, axis=-1).astype(jnp.int32)
    order = jnp.transpose(order, (0, 2, 1))
    per_bucket = N_DEV // ROW_GRP
    buckets = jnp.arange(N_DEV, dtype=jnp.int32)
    rows = order // per_bucket
    cols = buckets * per_bucket + order % per_bucket
    return (rows.reshape(DEVICES, N_DEV).astype(jnp.int32), cols.reshape(DEVICES, N_DEV).astype(jnp.int32))


def draw_near_rows(key, part):
    return slot_tables(key, 11)[0]


def draw_near_cols(key, part):
    return slot_tables(key, 11)[1]


def draw_far_rows(key, part):
    return slot_tables(key, 23)[0]


def draw_far_cols(key, part):
    return slot_tables(key, 23)[1]


def block_levels(stream_key, dims, cuts, smallest, largest):
    level, own = 1.0, jax.random.fold_in(stream_key, 6)
    for axis_at, parts in cuts:
        steps = jnp.exp(jax.random.uniform(jax.random.fold_in(own, axis_at), (parts,), jnp.float32, smallest / len(cuts), largest / len(cuts)))
        level = level * jnp.repeat(steps, dims[axis_at] // parts).reshape([-1 if axis == axis_at else 1 for axis in range(len(dims))])
    return level


def noise(key, extent, deviation, most, split=(), kind=jnp.bfloat16):
    entries = jax.random.normal(key, extent, jnp.float32) * deviation
    if len(split) > 0:
        entries = block_levels(key, extent, split, -0.22, 0.18) * entries
    return jnp.clip(entries, min=-most, max=most).astype(kind)


def setup_inputs(seed: int = 0) -> dict:
    key_of = jax.random.split(jax.random.key(seed), 10)
    row_panel = noise(key_of[0], (ROWS, B, B), (B ** -0.25), 3.0, ((0, 4), (1, 8)))
    col_near = noise(key_of[1], (NEAR_COLS, B, B), (B ** -0.25), 3.0, ((0, 8), (1, 4)))
    col_far = noise(key_of[2], (FAR_COLS, 2, R, B), (0.8 * R ** -0.25 * B ** -0.375), 0.4375, ((0, 8), (2, 4)))
    near_tiles = noise(key_of[3], (DEVICES * N_DEV, B, B), 1.0, 6.0, ((0, 32),))
    near_rows = draw_near_rows(jax.random.fold_in(key_of[9], 71), 0)
    near_cols = draw_near_cols(jax.random.fold_in(key_of[9], 71), 0)
    far_tiles = noise(key_of[6], (DEVICES * N_DEV, 2, R, B), 1.0, 6.0, ((0, 32),))
    far_rows = draw_far_rows(jax.random.fold_in(key_of[9], 71), 0)
    far_cols = draw_far_cols(jax.random.fold_in(key_of[9], 71), 0)
    return {"row_panel": row_panel, "col_near": col_near, "col_far": col_far, "near_tiles": near_tiles, "near_rows": near_rows, "near_cols": near_cols, "far_tiles": far_tiles, "far_rows": far_rows, "far_cols": far_cols}


def slab_rows(local_rows):
    devices = local_rows.shape[0]
    groups = jnp.arange(devices, dtype=jnp.int32) // N_DEV
    return (groups[:, None] * ROW_GRP + local_rows).astype(jnp.int32).reshape(-1)


def reference(row_panel, col_near, col_far, near_tiles, near_rows, near_cols, far_tiles, far_rows, far_cols):
    near_index = slab_rows(near_rows)
    far_index = slab_rows(far_rows)

    def near_one(items):
        tile, row_id, col_id = items
        left = lax.dynamic_index_in_dim(row_panel, row_id, 0, keepdims=False).astype(jnp.float32)
        right = lax.dynamic_index_in_dim(col_near, col_id, 0, keepdims=False).astype(jnp.float32)
        product = jnp.dot(left, right.T, precision=lax.Precision.HIGHEST)
        return (tile.astype(jnp.float32) - product).astype(jnp.bfloat16)

    def far_one(items):
        tile, row_id, col_id = items
        left = lax.dynamic_index_in_dim(row_panel, row_id, 0, keepdims=False).astype(jnp.float32)
        factors = lax.dynamic_index_in_dim(col_far, col_id, 0, keepdims=False)
        basis = tile[0].astype(jnp.float32)
        x_trans = jnp.dot(basis, left, precision=lax.Precision.HIGHEST)
        small = jnp.dot(factors[1].astype(jnp.float32), x_trans.T, precision=lax.Precision.HIGHEST)
        update = jnp.dot(small.T, factors[0].astype(jnp.float32), precision=lax.Precision.HIGHEST)
        return (tile[1].astype(jnp.float32) - update).astype(jnp.bfloat16)

    near_out = lax.map(near_one, (near_tiles, near_index, near_cols.reshape(-1).astype(jnp.int32)), batch_size=16)
    far_out = lax.map(far_one, (far_tiles, far_index, far_cols.reshape(-1).astype(jnp.int32)), batch_size=16)
    return near_out, far_out
```

```python
import jax
import jax.numpy as jnp
from jax import lax
from jax.sharding import Mesh, PartitionSpec as P

OUTER = 4
PLANE = ("gy", "core", "inner")


def shards(
    row_panel, col_near, col_far, near_tiles, near_rows, near_cols, far_tiles, far_rows, far_cols
):
    inner_size = lax.axis_size("inner")
    outer_size = lax.axis_size("outer")
    groups = lax.axis_size("gy") * lax.axis_size("core")
    dev_count = inner_size * outer_size
    per_bucket = col_near.shape[0]
    outer, inner = lax.axis_index("outer"), lax.axis_index("inner")
    order = col_near.shape[2]
    quarter = col_near.shape[1]
    rank = col_far.shape[2] * groups

    def wanted(cols):
        table = cols.reshape(groups, outer_size, inner_size, outer_size, inner_size)
        table = lax.dynamic_index_in_dim(table, outer, 1, keepdims=False)
        table = lax.dynamic_index_in_dim(table, inner, 3, keepdims=False)
        return table.reshape(groups * inner_size, outer_size) % per_bucket

    line = jnp.arange(outer_size, dtype=jnp.int32) * per_bucket
    near_line = lax.all_gather(col_near, "outer", axis=0, tiled=True)
    near_send = jnp.take(near_line, wanted(near_cols) + line, axis=0)
    near_got = lax.all_to_all(near_send, PLANE, split_axis=0, concat_axis=0, tiled=True)

    far_line = lax.all_gather(col_far, "outer", axis=0, tiled=True)
    far_send = jnp.take(far_line, wanted(far_cols) + line, axis=0)
    far_got = lax.all_to_all(far_send, PLANE, split_axis=0, concat_axis=0, tiled=True)

    row_tiles = lax.all_gather(row_panel, ("outer", "inner"), axis=1, tiled=True)

    near_got = near_got.reshape(groups, inner_size, outer_size, quarter, order)
    near_panel = jnp.transpose(near_got, (2, 1, 0, 3, 4)).reshape(dev_count, order, order)
    far_got = far_got.reshape(groups, inner_size, outer_size, 2, rank // groups, order)
    far_panel = jnp.transpose(far_got, (2, 1, 3, 0, 4, 5)).reshape(dev_count, 2, rank, order)

    near_left = jnp.take(row_tiles, near_rows[0], axis=0)
    near_product = jnp.einsum(
        "sik,sjk->sij", near_left, near_panel, preferred_element_type=jnp.float32
    )
    near_out = (near_tiles.astype(jnp.float32) - near_product).astype(jnp.bfloat16)
    far_left = jnp.take(row_tiles, far_rows[0], axis=0)
    basis = far_tiles[:, 0]
    x_trans = jnp.einsum("sqi,sik->sqk", basis, far_left, preferred_element_type=jnp.float32)
    small = jnp.einsum(
        "sak,sqk->saq",
        far_panel[:, 1].astype(jnp.float32),
        x_trans,
        precision=lax.Precision.HIGHEST,
    )
    update = jnp.einsum(
        "saq,saj->sqj", small, far_panel[:, 0].astype(jnp.float32), precision=lax.Precision.HIGHEST
    )
    far_out = (far_tiles[:, 1].astype(jnp.float32) - update).astype(jnp.bfloat16)
    return (near_out, far_out)


def solution(mesh):
    groups, dev_count = mesh.shape["grp"], mesh.shape["dev"]
    fine = Mesh(
        mesh.devices.reshape(groups // 2, 2, OUTER, dev_count // OUTER),
        ("gy", "core", "outer", "inner"),
    )
    grp, dev = ("gy", "core"), ("outer", "inner")
    every = grp + dev
    placed = (
        P(grp, dev, None),
        P(dev, grp, None),
        P(dev, None, grp, None),
        P(every, None, None),
        P(every, None),
        P(),
        P(every, None, None, None),
        P(every, None),
        P(),
    )
    return jax.shard_map(
        shards,
        mesh=fine,
        in_specs=placed,
        out_specs=(P(every, None, None), P(every, None, None)),
        check_vma=False,
    )
```

```python
import functools

import jax
import jax.numpy as jnp
from jax import lax
from jax.experimental import pallas as pl
from jax.experimental.pallas import tpu as pltpu
from jax.sharding import Mesh, PartitionSpec as P

OUTER = 4
PLANE = ("gy", "core", "inner")
ROW_ALIGN = 16
VMEM_LIMIT = 48 * 1024 * 1024


def pack_kernel(dims, meta, near_cols, far_cols, *refs):
    groups, inner_size, per_bucket, quarter, far_rows, row_count = dims
    sources, (out, rows_out, sems) = refs[:-3], refs[-3:]
    which, outer, inner, bucket_outer = meta[0], meta[1], meta[2], meta[3]
    bucket = bucket_outer * inner_size + inner
    far_at = per_bucket * quarter
    rows_at = far_at + per_bucket * far_rows
    for k, source in enumerate(sources):

        @pl.when(which == k)
        def _(source=source):
            copies = []
            for g in range(groups):
                for x in range(inner_size):
                    at = g * inner_size + x
                    device = (g * OUTER + outer) * inner_size + x
                    near = near_cols[device, bucket] - bucket * per_bucket
                    far = far_cols[device, bucket] - bucket * per_bucket
                    copies.append(
                        pltpu.make_async_copy(
                            source.at[pl.ds(pl.multiple_of(near * quarter, ROW_ALIGN), quarter)],
                            out.at[at, pl.ds(0, quarter)],
                            sems.at[2 * at],
                        )
                    )
                    copies.append(
                        pltpu.make_async_copy(
                            source.at[
                                pl.ds(pl.multiple_of(far_at + far * far_rows, ROW_ALIGN), far_rows)
                            ],
                            out.at[at, pl.ds(quarter, far_rows)],
                            sems.at[2 * at + 1],
                        )
                    )
            copies.append(
                pltpu.make_async_copy(
                    source.at[pl.ds(rows_at, row_count)],
                    rows_out,
                    sems.at[2 * groups * inner_size],
                )
            )
            for copy in copies:
                copy.start()
            for copy in copies:
                copy.wait()


def pack(dims, meta, near_cols, far_cols, sources):
    groups, inner_size, per_bucket, quarter, far_rows, row_count = dims
    order = sources[0].shape[1]
    wanted = groups * inner_size
    moved = wanted * (quarter + far_rows) * order * 2
    return pl.pallas_call(
        functools.partial(pack_kernel, dims),
        grid_spec=pltpu.PrefetchScalarGridSpec(
            num_scalar_prefetch=3,
            grid=(),
            in_specs=[pl.BlockSpec(memory_space=pl.ANY)] * len(sources),
            out_specs=[pl.BlockSpec(memory_space=pl.ANY)] * 2,
            scratch_shapes=[pltpu.SemaphoreType.DMA((2 * wanted + 1,))],
        ),
        out_shape=[
            jax.ShapeDtypeStruct((wanted, quarter + far_rows, order), jnp.bfloat16),
            jax.ShapeDtypeStruct((row_count, order), jnp.bfloat16),
        ],
        cost_estimate=pl.CostEstimate(flops=0, bytes_accessed=2 * moved, transcendentals=0),
    )(meta, near_cols, far_cols, *sources)


def split_dot(exact, wide, dimensions):
    high = wide.astype(jnp.bfloat16)
    low = (wide - high.astype(jnp.float32)).astype(jnp.bfloat16)
    return lax.dot_general(
        exact, high, dimensions, preferred_element_type=jnp.float32
    ) + lax.dot_general(exact, low, dimensions, preferred_element_type=jnp.float32)


def update_kernel(dims, meta, near_rows, far_rows, near_tile, far_tile, *refs):
    groups, inner_size, quarter, far_half, shard = dims
    got = refs[:OUTER]
    shards_in = refs[OUTER : OUTER + OUTER * inner_size]
    near_out, far_out, lefts, panel, factor_p, factor_q = refs[OUTER + OUTER * inner_size :]
    row_group = lefts.shape[0]
    inner = meta[OUTER]
    step = pl.program_id(0)
    chunk = step // inner_size
    x = step % inner_size

    @pl.when(step == 0)
    def _():
        for n in range(OUTER):
            for k in range(inner_size):
                owner = meta[n] * inner_size + (inner + k) % inner_size
                for r in range(row_group):
                    lefts[r, pl.ds(pl.multiple_of(owner * shard, ROW_ALIGN), shard), :] = shards_in[
                        n * inner_size + k
                    ][r * shard : (r + 1) * shard, :]

    for n in range(OUTER):

        @pl.when(chunk == n)
        def _(n=n):
            for g in range(groups):
                at = g * inner_size + x
                panel[g * quarter : (g + 1) * quarter, :] = got[n][at, 0:quarter, :]
                middle = quarter + far_half
                factor_p[g * far_half : (g + 1) * far_half, :] = got[n][at, quarter:middle, :]
                factor_q[g * far_half : (g + 1) * far_half, :] = got[n][
                    at, middle : middle + far_half, :
                ]

    slot = meta[chunk] * inner_size + x
    across = (((1,), (1,)), ((), ()))
    product = lax.dot_general(
        lefts[near_rows[slot]], panel[...], across, preferred_element_type=jnp.float32
    )
    near_out[0] = (near_tile[0].astype(jnp.float32) - product).astype(jnp.bfloat16)
    x_trans = jnp.dot(
        far_tile[0, 0], lefts[far_rows[slot]], preferred_element_type=jnp.float32
    )
    small = split_dot(factor_q[...], x_trans, across)
    update = split_dot(factor_p[...], small, (((0,), (0,)), ((), ())))
    far_out[0] = (far_tile[0, 1].astype(jnp.float32) - update.T).astype(jnp.bfloat16)


def update(dims, meta, near_rows, far_rows, near_tiles, far_tiles, got, shards_in):
    groups, inner_size, quarter, far_half, shard = dims
    slots, order = near_tiles.shape[0], near_tiles.shape[1]
    rank = far_tiles.shape[2]

    def at_slot(*rest):
        def index(step, meta, near_rows, far_rows):
            return (meta[step // inner_size] * inner_size + step % inner_size,) + rest

        return index

    whole = pl.BlockSpec(memory_space=pltpu.VMEM)
    row_group = shards_in[0].shape[0] // shard
    return pl.pallas_call(
        functools.partial(update_kernel, dims),
        grid_spec=pltpu.PrefetchScalarGridSpec(
            num_scalar_prefetch=3,
            grid=(slots,),
            in_specs=[
                pl.BlockSpec((1, order, order), at_slot(0, 0)),
                pl.BlockSpec((1, 2, rank, order), at_slot(0, 0, 0)),
            ]
            + [whole] * (len(got) + len(shards_in)),
            out_specs=[
                pl.BlockSpec((1, order, order), at_slot(0, 0)),
                pl.BlockSpec((1, rank, order), at_slot(0, 0)),
            ],
            scratch_shapes=[
                pltpu.VMEM((row_group, order, order), jnp.bfloat16),
                pltpu.VMEM((order, order), jnp.bfloat16),
                pltpu.VMEM((groups * far_half, order), jnp.bfloat16),
                pltpu.VMEM((groups * far_half, order), jnp.bfloat16),
            ],
        ),
        out_shape=[
            jax.ShapeDtypeStruct(near_tiles.shape, jnp.bfloat16),
            jax.ShapeDtypeStruct((slots, rank, order), jnp.bfloat16),
        ],
        compiler_params=pltpu.CompilerParams(vmem_limit_bytes=VMEM_LIMIT),
        cost_estimate=pl.CostEstimate(
            flops=2 * slots * order * order * (order + 4 * rank),
            bytes_accessed=3 * slots * order * order * 2,
            transcendentals=0,
        ),
    )(meta, near_rows, far_rows, near_tiles, far_tiles, *got, *shards_in)


def shards(
    row_panel, col_near, col_far, near_tiles, near_rows, near_cols, far_tiles, far_rows, far_cols
):
    inner_size = lax.axis_size("inner")
    groups = lax.axis_size("gy") * lax.axis_size("core")
    outer, inner = lax.axis_index("outer"), lax.axis_index("inner")
    per_bucket, quarter, order = col_near.shape
    row_group, shard = row_panel.shape[:2]
    far_part = col_far.shape[2]
    far_half = -(-far_part // ROW_ALIGN) * ROW_ALIGN
    row_count = row_group * shard

    far_padded = jnp.pad(col_far, ((0, 0), (0, 0), (0, far_half - far_part), (0, 0)))
    own = jnp.concatenate(
        [
            col_near.reshape(per_bucket * quarter, order),
            far_padded.reshape(per_bucket * 2 * far_half, order),
            row_panel.reshape(row_count, order),
        ],
        axis=0,
    )

    def along(value, pairs):
        return lax.ppermute(value, "outer", pairs)

    up1 = along(own, [(0, 1), (1, 2), (2, 3)])
    down1 = along(own, [(3, 2), (2, 1), (1, 0)])
    up2 = along(up1, [(1, 2), (2, 3)])
    down2 = along(down1, [(2, 1), (1, 0)])
    relay = jnp.where(outer == 1, down2, up2)
    last = along(relay, [(1, 0), (2, 3)])

    def choose(*by_outer):
        return jnp.asarray(by_outer, jnp.int32)[outer]

    plan = [
        ((own,), jnp.int32(0), outer),
        ((up1, down1), choose(1, 0, 0, 0), choose(1, 0, 1, 2)),
        ((up2, down1, down2), choose(2, 1, 1, 0), choose(2, 2, 3, 1)),
        ((last, down2, up2), choose(0, 1, 2, 0), choose(3, 3, 0, 0)),
    ]
    dims = (groups, inner_size, per_bucket, quarter, 2 * far_half, row_count)
    got, shards_in = [], []
    for sources, which, bucket_outer in plan:
        meta = jnp.stack([which, outer, inner, bucket_outer])
        send, rows = pack(dims, meta, near_cols, far_cols, sources)
        got.append(lax.all_to_all(send, PLANE, split_axis=0, concat_axis=0, tiled=True))
        shards_in.append(rows)
        for k in range(1, inner_size):
            turn = [((i + k) % inner_size, i) for i in range(inner_size)]
            shards_in.append(lax.ppermute(rows, "inner", turn))
    meta = jnp.stack([bucket_outer for _, _, bucket_outer in plan] + [inner])
    return tuple(
        update(
            (groups, inner_size, quarter, far_half, shard),
            meta,
            near_rows[0],
            far_rows[0],
            near_tiles,
            far_tiles,
            got,
            shards_in,
        )
    )


def solution(mesh):
    groups, dev_count = mesh.shape["grp"], mesh.shape["dev"]
    fine = Mesh(
        mesh.devices.reshape(groups // 2, 2, OUTER, dev_count // OUTER),
        ("gy", "core", "outer", "inner"),
    )
    grp, dev = ("gy", "core"), ("outer", "inner")
    every = grp + dev
    placed = (
        P(grp, dev, None),
        P(dev, grp, None),
        P(dev, None, grp, None),
        P(every, None, None),
        P(every, None),
        P(),
        P(every, None, None, None),
        P(every, None),
        P(),
    )
    return jax.shard_map(
        shards,
        mesh=fine,
        in_specs=placed,
        out_specs=(P(every, None, None), P(every, None, None)),
        check_vma=False,
    )
```

```python
import functools

import jax
import jax.numpy as jnp
from jax import lax
from jax.experimental import pallas as pl
from jax.experimental.pallas import tpu as pltpu
from jax.sharding import Mesh, PartitionSpec as P

OUTER = 4
PLANE = ("gy", "core", "inner")
ROW_ALIGN = 16
VMEM_LIMIT = 40 * 1024 * 1024
CHUNK_OWNER = ((0, 1, 2, 3), (1, 0, 1, 2), (2, 2, 3, 1), (3, 3, 0, 0))
CHUNK_SOURCE = ((0, 0, 0, 0), (1, 0, 0, 0), (2, 1, 1, 0), (0, 1, 1, 0))
VMEM = pl.BlockSpec(memory_space=pltpu.VMEM)
SMEM = pl.BlockSpec(memory_space=pltpu.SMEM)


class Sizes:
    def __init__(self, groups, inner, per_bucket, quarter, far_half, shard):
        self.groups, self.inner, self.per_bucket = groups, inner, per_bucket
        self.quarter, self.far_half, self.shard = quarter, far_half, shard
        self.far = 2 * far_half
        self.slots = OUTER * inner
        self.wanted = groups * inner
        self.stride = 2 * self.wanted + 2
        self.near_rows_at = OUTER * self.stride
        self.far_rows_at = self.near_rows_at + self.slots
        self.inner_at = self.far_rows_at + self.slots
        self.table = self.inner_at + 1

    def owner_at(self, n):
        return n * self.stride + 2 * self.wanted

    def source_at(self, n):
        return n * self.stride + 2 * self.wanted + 1


def by_position(values, position):
    result = jnp.int32(values[0])
    for k in range(1, len(values)):
        result = jnp.where(position == k, jnp.int32(values[k]), result)
    return result


def table_kernel(sizes, place, near_cols, far_cols, near_rows, far_rows, table):
    outer, inner = place[0], place[1]
    table[sizes.inner_at] = inner
    for n in range(OUTER):
        owner = by_position(CHUNK_OWNER[n], outer)
        table[sizes.owner_at(n)] = owner
        table[sizes.source_at(n)] = by_position(CHUNK_SOURCE[n], outer)
        bucket = owner * sizes.inner + inner
        for g in range(sizes.groups):
            for x in range(sizes.inner):
                at = g * sizes.inner + x
                device = (g * OUTER + outer) * sizes.inner + x
                first = bucket * sizes.per_bucket
                table[n * sizes.stride + at] = near_cols[bucket, device] - first
                table[n * sizes.stride + sizes.wanted + at] = far_cols[bucket, device] - first
    for s in range(sizes.slots):
        table[sizes.near_rows_at + s] = near_rows[0, s]
        table[sizes.far_rows_at + s] = far_rows[0, s]


def make_table(sizes, place, near_cols, far_cols, near_rows, far_rows):
    return pl.pallas_call(
        functools.partial(table_kernel, sizes),
        in_specs=[SMEM] * 5,
        out_specs=SMEM,
        out_shape=jax.ShapeDtypeStruct((sizes.table,), jnp.int32),
    )(place, near_cols.T, far_cols.T, near_rows, far_rows)


def pack_kernel(sizes, n, table, *refs):
    sources, out = refs[:-1], refs[-1]
    quarter, far = sizes.quarter, sizes.far
    far_at = sizes.per_bucket * quarter
    for k, source in enumerate(sources):

        @pl.when(table[sizes.source_at(n)] == k)
        def _(source=source):
            for at in range(sizes.wanted):
                near_pick = table[n * sizes.stride + at] * quarter
                far_pick = far_at + table[n * sizes.stride + sizes.wanted + at] * far
                out[at, 0:quarter, :] = source[
                    pl.ds(pl.multiple_of(near_pick, ROW_ALIGN), quarter), :
                ]
                out[at, quarter : quarter + far, :] = source[
                    pl.ds(pl.multiple_of(far_pick, ROW_ALIGN), far), :
                ]


def pack(sizes, n, table, sources):
    order = sources[0].shape[1]
    shape = (sizes.wanted, sizes.quarter + sizes.far, order)
    return pl.pallas_call(
        functools.partial(pack_kernel, sizes, n),
        in_specs=[SMEM] + [VMEM] * len(sources),
        out_specs=VMEM,
        out_shape=jax.ShapeDtypeStruct(shape, jnp.bfloat16),
        compiler_params=pltpu.CompilerParams(vmem_limit_bytes=VMEM_LIMIT),
        cost_estimate=pl.CostEstimate(
            flops=0, bytes_accessed=4 * shape[0] * shape[1] * shape[2], transcendentals=0
        ),
    )(table, *sources)


def lefts_kernel(sizes, table, *refs):
    parts, lefts = refs[:-1], refs[-1]
    shard = sizes.shard
    inner = table[sizes.inner_at]
    for k, part in enumerate(parts):
        x = lax.rem(inner + k, sizes.inner)
        for z in range(OUTER):
            at = pl.multiple_of((z * sizes.inner + x) * shard, ROW_ALIGN)
            for r in range(lefts.shape[0]):
                lefts[r, pl.ds(at, shard), :] = part[z, r]


def make_lefts(sizes, table, parts):
    row_group, shard, order = parts[0].shape[1:]
    return pl.pallas_call(
        functools.partial(lefts_kernel, sizes),
        in_specs=[SMEM] + [VMEM] * len(parts),
        out_specs=VMEM,
        out_shape=jax.ShapeDtypeStruct((row_group, order, order), jnp.bfloat16),
        compiler_params=pltpu.CompilerParams(vmem_limit_bytes=VMEM_LIMIT),
    )(table, *parts)


def update_kernel(sizes, n, table, near_tile, far_tile, lefts, got, *refs):
    near_out, far_out, panel, factor_p, factor_q = refs[-5:]
    x = pl.program_id(0)
    slot = table[sizes.owner_at(n)] * sizes.inner + x
    quarter, half = sizes.quarter, sizes.far_half
    for g in range(sizes.groups):
        at = g * sizes.inner + x
        panel[g * quarter : (g + 1) * quarter, :] = got[at, 0:quarter, :]
        factor_p[g * half : (g + 1) * half, :] = got[at, quarter : quarter + half, :]
        factor_q[g * half : (g + 1) * half, :] = got[at, quarter + half : quarter + 2 * half, :]
    across = (((1,), (1,)), ((), ()))
    product = lax.dot_general(
        lefts[table[sizes.near_rows_at + slot]],
        panel[...],
        across,
        preferred_element_type=jnp.float32,
    )
    near_out[0] = (near_tile[0].astype(jnp.float32) - product).astype(jnp.bfloat16)

    def halves(value):
        high = value.astype(jnp.bfloat16)
        return high, (value - high.astype(jnp.float32)).astype(jnp.bfloat16)

    x_trans = jnp.dot(
        far_tile[0, 0],
        lefts[table[sizes.far_rows_at + slot]],
        preferred_element_type=jnp.float32,
    )
    factors = factor_q[...]
    small = sum(
        lax.dot_general(part, factors, across, preferred_element_type=jnp.float32)
        for part in halves(x_trans)
    )
    factors = factor_p[...]
    change = sum(
        jnp.dot(part, factors, preferred_element_type=jnp.float32) for part in halves(small)
    )
    far_out[0] = (far_tile[0, 1].astype(jnp.float32) - change).astype(jnp.bfloat16)


def update(sizes, n, table, near_tiles, far_tiles, lefts, got, before):
    slots, order = near_tiles.shape[:2]
    rank = far_tiles.shape[2]

    def at_slot(*rest):
        return lambda x, table: (table[sizes.owner_at(n)] * sizes.inner + x,) + rest

    whole = pl.BlockSpec(memory_space=pltpu.VMEM)
    kept = pl.BlockSpec(memory_space=pl.ANY)
    return pl.pallas_call(
        functools.partial(update_kernel, sizes, n),
        grid_spec=pltpu.PrefetchScalarGridSpec(
            num_scalar_prefetch=1,
            grid=(sizes.inner,),
            in_specs=[
                pl.BlockSpec((1, order, order), at_slot(0, 0)),
                pl.BlockSpec((1, 2, rank, order), at_slot(0, 0, 0)),
                whole,
                whole,
            ]
            + [kept] * len(before),
            out_specs=[
                pl.BlockSpec((1, order, order), at_slot(0, 0)),
                pl.BlockSpec((1, rank, order), at_slot(0, 0)),
            ],
            scratch_shapes=[
                pltpu.VMEM((order, order), jnp.bfloat16),
                pltpu.VMEM((sizes.groups * sizes.far_half, order), jnp.bfloat16),
                pltpu.VMEM((sizes.groups * sizes.far_half, order), jnp.bfloat16),
            ],
        ),
        out_shape=[
            jax.ShapeDtypeStruct(near_tiles.shape, jnp.bfloat16),
            jax.ShapeDtypeStruct((slots, rank, order), jnp.bfloat16),
        ],
        input_output_aliases={5 + k: k for k in range(len(before))},
        compiler_params=pltpu.CompilerParams(vmem_limit_bytes=VMEM_LIMIT),
        cost_estimate=pl.CostEstimate(
            flops=2 * sizes.inner * order * order * (order + 4 * rank),
            bytes_accessed=4 * sizes.inner * order * order * 2,
            transcendentals=0,
        ),
    )(table, near_tiles, far_tiles, lefts, got, *before)


def shards(
    row_panel, col_near, col_far, near_tiles, near_rows, near_cols, far_tiles, far_rows, far_cols
):
    inner_size = lax.axis_size("inner")
    groups = lax.axis_size("gy") * lax.axis_size("core")
    outer, inner = lax.axis_index("outer"), lax.axis_index("inner")
    per_bucket, quarter, order = col_near.shape
    row_group, shard = row_panel.shape[:2]
    far_part = col_far.shape[2]
    far_half = -(-far_part // ROW_ALIGN) * ROW_ALIGN
    sizes = Sizes(groups, inner_size, per_bucket, quarter, far_half, shard)

    rows_line = lax.all_to_all(
        jnp.broadcast_to(row_panel, (OUTER,) + row_panel.shape),
        "outer",
        split_axis=0,
        concat_axis=0,
        tiled=True,
    )
    far_padded = jnp.pad(col_far, ((0, 0), (0, 0), (0, far_half - far_part), (0, 0)))
    own = jnp.concatenate(
        [
            col_near.reshape(per_bucket * quarter, order),
            far_padded.reshape(per_bucket * 2 * far_half, order),
        ],
        axis=0,
    )

    def along(value, pairs):
        return lax.ppermute(value, "outer", pairs)

    up1 = along(own, [(0, 1), (1, 2), (2, 3)])
    down1 = along(own, [(3, 2), (2, 1), (1, 0)])
    up2 = along(up1, [(1, 2), (2, 3)])
    down2 = along(down1, [(2, 1), (1, 0)])
    relay = jnp.where(outer == 1, down2, up2)
    last = along(relay, [(1, 0), (2, 3)])
    chunks = [(own,), (up1, down1), (up2, down1, down2), (last, relay)]

    row_parts = [rows_line]
    for k in range(1, inner_size):
        turn = [((i + k) % inner_size, i) for i in range(inner_size)]
        row_parts.append(lax.ppermute(rows_line, "inner", turn))

    table = make_table(
        sizes, jnp.stack([outer, inner]), near_cols, far_cols, near_rows, far_rows
    )
    lefts = make_lefts(sizes, table, row_parts)
    outs = ()
    for n, sources in enumerate(chunks):
        send = pack(sizes, n, table, sources)
        got = lax.all_to_all(send, PLANE, split_axis=0, concat_axis=0, tiled=True)
        outs = update(sizes, n, table, near_tiles, far_tiles, lefts, got, outs)
    return tuple(outs)


def solution(mesh):
    groups, dev_count = mesh.shape["grp"], mesh.shape["dev"]
    fine = Mesh(
        mesh.devices.reshape(groups // 2, 2, OUTER, dev_count // OUTER),
        ("gy", "core", "outer", "inner"),
    )
    grp, dev = ("gy", "core"), ("outer", "inner")
    every = grp + dev
    placed = (
        P(grp, dev, None),
        P(dev, grp, None),
        P(dev, None, grp, None),
        P(every, None, None),
        P(every, None),
        P(),
        P(every, None, None, None),
        P(every, None),
        P(),
    )
    return jax.shard_map(
        shards,
        mesh=fine,
        in_specs=placed,
        out_specs=(P(every, None, None), P(every, None, None)),
        check_vma=False,
    )
```

```python
import functools

import jax
import jax.numpy as jnp
from jax import lax
from jax.experimental import pallas as pl
from jax.experimental.pallas import tpu as pltpu
from jax.sharding import Mesh, PartitionSpec as P

OUTER = 4
PLANE = ("gy", "core", "inner")
ROW_ALIGN = 16
FAR_ALIGN = 8
LANES = 128
VMEM_LIMIT = 16 * 1024 * 1024
UPDATE_VMEM = 56 * 1024 * 1024
CHUNK_OWNER = ((0, 1, 2, 3), (1, 0, 1, 2), (2, 2, 3, 1), (3, 3, 0, 0))
CHUNK_SOURCE = ((0, 0, 0, 0), (1, 0, 0, 0), (2, 1, 1, 0), (0, 1, 1, 0))
CHUNK_SOURCES = (("own",), ("up1", "down1"), ("up2", "down1", "down2"), ("last", "relay"))
PACK_FLOPS = 10**12
TOKEN = jax.ShapeDtypeStruct((8, LANES), jnp.float32)
VMEM = pl.BlockSpec(memory_space=pltpu.VMEM)
SMEM = pl.BlockSpec(memory_space=pltpu.SMEM)
KEPT = pl.BlockSpec(memory_space=pl.ANY)
HBM = pl.BlockSpec(memory_space=pltpu.HBM)


class Sizes:
    def __init__(self, groups, inner, per_bucket, quarter, far, shard):
        self.groups, self.inner, self.per_bucket = groups, inner, per_bucket
        self.quarter, self.far, self.shard = quarter, far, shard
        self.far_all = -(-groups * far // LANES) * LANES
        self.slots = OUTER * inner
        self.wanted = groups * inner
        self.stride = 2 * self.wanted + 2
        self.near_rows_at = OUTER * self.stride
        self.far_rows_at = self.near_rows_at + self.slots
        self.inner_at = self.far_rows_at + self.slots
        self.outer_at = self.inner_at + 1
        self.table = self.outer_at + 1

    def owner_at(self, n):
        return n * self.stride + 2 * self.wanted

    def source_at(self, n):
        return n * self.stride + 2 * self.wanted + 1


def by_position(values, position):
    result = jnp.int32(values[0])
    for k in range(1, len(values)):
        result = jnp.where(position == k, jnp.int32(values[k]), result)
    return result


def table_kernel(sizes, place, near_cols, far_cols, near_rows, far_rows, table):
    outer, inner = place[0], place[1]
    table[sizes.inner_at] = inner
    table[sizes.outer_at] = outer
    for n in range(OUTER):
        owner = by_position(CHUNK_OWNER[n], outer)
        table[sizes.owner_at(n)] = owner
        table[sizes.source_at(n)] = by_position(CHUNK_SOURCE[n], outer)
        bucket = owner * sizes.inner + inner
        for g in range(sizes.groups):
            for x in range(sizes.inner):
                at = g * sizes.inner + x
                device = (g * OUTER + outer) * sizes.inner + x
                first = bucket * sizes.per_bucket
                table[n * sizes.stride + at] = near_cols[bucket, device] - first
                table[n * sizes.stride + sizes.wanted + at] = far_cols[bucket, device] - first
    for s in range(sizes.slots):
        table[sizes.near_rows_at + s] = near_rows[0, s]
        table[sizes.far_rows_at + s] = far_rows[0, s]


def make_table(sizes, place, near_cols, far_cols, near_rows, far_rows):
    return pl.pallas_call(
        functools.partial(table_kernel, sizes),
        in_specs=[SMEM] * 5,
        out_specs=SMEM,
        out_shape=jax.ShapeDtypeStruct((sizes.table,), jnp.int32),
    )(place, near_cols.T, far_cols.T, near_rows, far_rows)


def pack_kernel(sizes, n, table, *refs):
    count = len(CHUNK_SOURCES[n])
    sources, out = refs[:count], refs[-1]
    quarter, far = sizes.quarter, sizes.far
    far_at = sizes.per_bucket * quarter
    for k, source in enumerate(sources):

        @pl.when(table[sizes.source_at(n)] == k)
        def _(source=source):
            for at in range(sizes.wanted):
                near_pick = table[n * sizes.stride + at] * quarter
                out[at, 0:quarter, :] = source[
                    pl.ds(pl.multiple_of(near_pick, ROW_ALIGN), quarter), :
                ]
                far_pick = table[n * sizes.stride + sizes.wanted + at]
                picked = source[far_at : far_at + far, :]
                for j in range(1, sizes.per_bucket):
                    other = source[far_at + j * far : far_at + (j + 1) * far, :]
                    picked = jnp.where(far_pick == j, other, picked)
                out[at, quarter : quarter + far, :] = picked


def pack(sizes, n, table, sources, after):
    order = sources[0].shape[1]
    shape = (sizes.wanted, sizes.quarter + sizes.far, order)
    return pl.pallas_call(
        functools.partial(pack_kernel, sizes, n),
        in_specs=[SMEM] + [VMEM] * len(sources) + [KEPT] * len(after),
        out_specs=VMEM,
        out_shape=jax.ShapeDtypeStruct(shape, jnp.bfloat16),
        compiler_params=pltpu.CompilerParams(vmem_limit_bytes=VMEM_LIMIT),
        cost_estimate=pl.CostEstimate(
            flops=PACK_FLOPS, bytes_accessed=0, transcendentals=0
        ),
    )(table, *sources, *after)


def half_kernel(sizes, table, *refs):
    parts, half, token = refs[:-2], refs[-2], refs[-1]
    token[...] = jnp.zeros_like(token)
    for k, part in enumerate(parts):
        half[lax.rem(table[sizes.outer_at] + OUTER - k, OUTER)] = part[...]


def make_half(sizes, table, parts):
    return pl.pallas_call(
        functools.partial(half_kernel, sizes),
        in_specs=[SMEM] + [VMEM] * len(parts),
        out_specs=[VMEM, VMEM],
        out_shape=[jax.ShapeDtypeStruct((OUTER,) + parts[0].shape, jnp.bfloat16), TOKEN],
        compiler_params=pltpu.CompilerParams(vmem_limit_bytes=VMEM_LIMIT),
        cost_estimate=pl.CostEstimate(flops=0, bytes_accessed=0, transcendentals=0),
    )(table, *parts)


def lefts_kernel(sizes, table, *refs):
    parts, lefts = refs[:-1], refs[-1]
    shard = sizes.shard
    inner = table[sizes.inner_at]
    for k, part in enumerate(parts):
        x = lax.rem(inner + k, sizes.inner)
        for z in range(OUTER):
            at = pl.multiple_of((z * sizes.inner + x) * shard, ROW_ALIGN)
            for r in range(lefts.shape[0]):
                lefts[r, pl.ds(at, shard), :] = part[z, r]


def make_lefts(sizes, table, parts):
    row_group, shard, order = parts[0].shape[1:]
    return pl.pallas_call(
        functools.partial(lefts_kernel, sizes),
        in_specs=[SMEM] + [VMEM] * len(parts),
        out_specs=VMEM,
        out_shape=jax.ShapeDtypeStruct((row_group, order, order), jnp.bfloat16),
        compiler_params=pltpu.CompilerParams(vmem_limit_bytes=VMEM_LIMIT),
        cost_estimate=pl.CostEstimate(flops=0, bytes_accessed=0, transcendentals=0),
    )(table, *parts)


def halves(value):
    high = value.astype(jnp.bfloat16)
    return high, (value - high.astype(jnp.float32)).astype(jnp.bfloat16)


def update_kernel(sizes, n, table, near_tiles, far_tiles, lefts, got, *refs):
    near_out, far_out, token, near, far_in, near_done, far_done, panel, factors, sems = refs[-10:]
    quarter, far = sizes.quarter, sizes.far
    first = table[sizes.owner_at(n)] * sizes.inner
    loads = []
    for x in range(sizes.inner):
        loads.append(
            (
                pltpu.make_async_copy(near_tiles.at[first + x], near.at[x], sems.at[0, x]),
                pltpu.make_async_copy(far_tiles.at[first + x], far_in.at[x], sems.at[1, x]),
            )
        )
        for load in loads[x]:
            load.start()
    token[...] = jnp.zeros_like(token)
    filled = sizes.groups * far
    if filled < sizes.far_all:
        factors[filled:, :] = jnp.zeros_like(factors[filled:, :])
    across = (((1,), (1,)), ((), ()))
    stores = []
    for x in range(sizes.inner):
        for g in range(sizes.groups):
            at = g * sizes.inner + x
            panel[g * quarter : (g + 1) * quarter, :] = got[at, 0:quarter, :]
            factors[g * far : (g + 1) * far, :] = got[at, quarter : quarter + far, :]
        product = lax.dot_general(
            lefts[table[sizes.near_rows_at + first + x]],
            panel[...],
            across,
            preferred_element_type=jnp.float32,
        )
        for load in loads[x]:
            load.wait()
        near_done[x] = (near[x].astype(jnp.float32) - product).astype(jnp.bfloat16)
        stores.append(
            pltpu.make_async_copy(near_done.at[x], near_out.at[first + x], sems.at[2, x])
        )
        stores[-1].start()
        x_trans = jnp.dot(
            far_in[x, 0],
            lefts[table[sizes.far_rows_at + first + x]],
            preferred_element_type=jnp.float32,
        )
        pairs = factors[...]
        small = sum(
            lax.dot_general(part, pairs, across, preferred_element_type=jnp.float32)
            for part in halves(x_trans)
        )
        turned = pltpu.roll(small, sizes.far_all - 1, 1)
        lane = lax.broadcasted_iota(jnp.int32, turned.shape, 1)
        turned = jnp.where(lane % 2 == 0, turned, 0.0)
        change = sum(
            jnp.dot(part, pairs, preferred_element_type=jnp.float32) for part in halves(turned)
        )
        far_done[x] = (far_in[x, 1].astype(jnp.float32) - change).astype(jnp.bfloat16)
        stores.append(
            pltpu.make_async_copy(far_done.at[x], far_out.at[first + x], sems.at[3, x])
        )
        stores[-1].start()
    for store in stores:
        store.wait()


def update(sizes, n, table, near_tiles, far_tiles, lefts, got, before):
    slots, order = near_tiles.shape[:2]
    rank = far_tiles.shape[2]
    return pl.pallas_call(
        functools.partial(update_kernel, sizes, n),
        in_specs=[SMEM, HBM, HBM, VMEM, VMEM] + [HBM] * len(before),
        out_specs=[HBM, HBM, VMEM],
        scratch_shapes=[
            pltpu.VMEM((sizes.inner, order, order), jnp.bfloat16),
            pltpu.VMEM((sizes.inner, 2, rank, order), jnp.bfloat16),
            pltpu.VMEM((sizes.inner, order, order), jnp.bfloat16),
            pltpu.VMEM((sizes.inner, rank, order), jnp.bfloat16),
            pltpu.VMEM((order, order), jnp.bfloat16),
            pltpu.VMEM((sizes.far_all, order), jnp.bfloat16),
            pltpu.SemaphoreType.DMA((4, sizes.inner)),
        ],
        out_shape=[
            jax.ShapeDtypeStruct(near_tiles.shape, jnp.bfloat16),
            jax.ShapeDtypeStruct((slots, rank, order), jnp.bfloat16),
            TOKEN,
        ],
        input_output_aliases={5 + k: k for k in range(len(before))},
        compiler_params=pltpu.CompilerParams(vmem_limit_bytes=UPDATE_VMEM),
        cost_estimate=pl.CostEstimate(flops=0, bytes_accessed=0, transcendentals=0),
    )(table, near_tiles, far_tiles, lefts, got, *before)


def shards(
    row_panel, col_near, col_far, near_tiles, near_rows, near_cols, far_tiles, far_rows, far_cols
):
    inner_size = lax.axis_size("inner")
    groups = lax.axis_size("gy") * lax.axis_size("core")
    outer, inner = lax.axis_index("outer"), lax.axis_index("inner")
    per_bucket, quarter, order = col_near.shape
    row_group, shard = row_panel.shape[:2]
    far_pairs = jnp.swapaxes(col_far, 1, 2).reshape(per_bucket, -1, order)
    far = -(-far_pairs.shape[1] // FAR_ALIGN) * FAR_ALIGN
    far_pairs = jnp.pad(far_pairs, ((0, 0), (0, far - far_pairs.shape[1]), (0, 0)))
    sizes = Sizes(groups, inner_size, per_bucket, quarter, far, shard)

    def along(value, pairs):
        return lax.ppermute(value, "outer", pairs)

    parts = [row_panel]
    for k in range(1, OUTER):
        parts.append(along(row_panel, [(i, (i + k) % OUTER) for i in range(OUTER)]))

    own = jnp.concatenate(
        [col_near.reshape(per_bucket * quarter, order), far_pairs.reshape(per_bucket * far, order)],
        axis=0,
    )
    held = {"own": own}
    held["up1"] = along(own, [(0, 1), (1, 2), (2, 3)])
    held["down1"] = along(own, [(3, 2), (2, 1), (1, 0)])
    held["up2"] = along(held["up1"], [(1, 2), (2, 3)])
    held["down2"] = along(held["down1"], [(2, 1), (1, 0)])
    held["relay"] = jnp.where(outer == 1, held["down2"], held["up2"])
    held["last"] = along(held["relay"], [(1, 0), (2, 3)])

    table = make_table(
        sizes, jnp.stack([outer, inner]), near_cols, far_cols, near_rows, far_rows
    )
    half, half_token = make_half(sizes, table, parts)
    halves = [half]
    for k in range(1, inner_size):
        turn = [((i + k) % inner_size, i) for i in range(inner_size)]
        halves.append(lax.ppermute(half, "inner", turn))
    lefts = make_lefts(sizes, table, halves)

    outs, tokens = (), []
    for n in range(OUTER):
        sources = [held[name] for name in CHUNK_SOURCES[n]]
        after = [half_token] if n == 1 else (tokens[n - 2 : n - 1] if n else [])
        send = pack(sizes, n, table, sources, after)
        got = lax.all_to_all(send, PLANE, split_axis=0, concat_axis=0, tiled=True)
        *outs, token = update(sizes, n, table, near_tiles, far_tiles, lefts, got, outs)
        tokens.append(token)
    return tuple(outs)


def solution(mesh):
    groups, dev_count = mesh.shape["grp"], mesh.shape["dev"]
    fine = Mesh(
        mesh.devices.reshape(groups // 2, 2, OUTER, dev_count // OUTER),
        ("gy", "core", "outer", "inner"),
    )
    grp, dev = ("gy", "core"), ("outer", "inner")
    every = grp + dev
    placed = (
        P(grp, dev, None),
        P(dev, grp, None),
        P(dev, None, grp, None),
        P(every, None, None),
        P(every, None),
        P(),
        P(every, None, None, None),
        P(every, None),
        P(),
    )
    return jax.shard_map(
        shards,
        mesh=fine,
        in_specs=placed,
        out_specs=(P(every, None, None), P(every, None, None)),
        check_vma=False,
    )
```

```python
import functools

import jax
import jax.numpy as jnp
from jax import lax
from jax.experimental import pallas as pl
from jax.experimental.pallas import tpu as pltpu
from jax.sharding import Mesh, PartitionSpec as P

OUTER = 4
PLANE = ("gy", "core", "inner")
ROW_ALIGN = 16
FAR_ALIGN = 8
LANES = 128
VMEM_LIMIT = 16 * 1024 * 1024
CHUNK_OWNER = ((0, 1, 2, 3), (1, 0, 3, 2), (2, 2, 1, 1), (3, 3, 0, 0))
CHUNK_SOURCE = ((0, 0, 0, 0), (0, 0, 0, 0), (1, 0, 0, 1), (1, 0, 0, 1))
CHUNK_SOURCES = (("own",), ("pair",), ("middle", "pass2"), ("cross", "pass3"))
PACK_FLOPS = 10**10
UPDATE_FLOPS = 3 * 10**9
VMEM = pl.BlockSpec(memory_space=pltpu.VMEM)
SMEM = pl.BlockSpec(memory_space=pltpu.SMEM)
KEPT = pl.BlockSpec(memory_space=pl.ANY)


class Sizes:
    def __init__(self, groups, inner, per_bucket, quarter, far, shard):
        self.groups, self.inner, self.per_bucket = groups, inner, per_bucket
        self.quarter, self.far, self.shard = quarter, far, shard
        self.far_all = -(-groups * far // LANES) * LANES
        self.slots = OUTER * inner
        self.wanted = groups * inner
        self.stride = 2 * self.wanted + 2
        self.near_rows_at = OUTER * self.stride
        self.far_rows_at = self.near_rows_at + self.slots
        self.inner_at = self.far_rows_at + self.slots
        self.outer_at = self.inner_at + 1
        self.table = self.outer_at + 1

    def owner_at(self, n):
        return n * self.stride + 2 * self.wanted

    def source_at(self, n):
        return n * self.stride + 2 * self.wanted + 1


def by_position(values, position):
    result = jnp.int32(values[0])
    for k in range(1, len(values)):
        result = jnp.where(position == k, jnp.int32(values[k]), result)
    return result


def fill_table(sizes, place, near_cols, far_cols, near_rows, far_rows, table):
    outer, inner = place[0], place[1]
    table[sizes.inner_at] = inner
    table[sizes.outer_at] = outer
    for n in range(OUTER):
        owner = by_position(CHUNK_OWNER[n], outer)
        table[sizes.owner_at(n)] = owner
        table[sizes.source_at(n)] = by_position(CHUNK_SOURCE[n], outer)
        bucket = owner * sizes.inner + inner
        for g in range(sizes.groups):
            for x in range(sizes.inner):
                at = g * sizes.inner + x
                device = (g * OUTER + outer) * sizes.inner + x
                first = bucket * sizes.per_bucket
                table[n * sizes.stride + at] = near_cols[bucket, device] - first
                table[n * sizes.stride + sizes.wanted + at] = far_cols[bucket, device] - first
    for s in range(sizes.slots):
        table[sizes.near_rows_at + s] = near_rows[0, s]
        table[sizes.far_rows_at + s] = far_rows[0, s]


def pack_from(sizes, n, table, source, out):
    quarter, far = sizes.quarter, sizes.far
    far_at = sizes.per_bucket * quarter
    for at in range(sizes.wanted):
        near_pick = table[n * sizes.stride + at] * quarter
        out[at, 0:quarter, :] = source[pl.ds(pl.multiple_of(near_pick, ROW_ALIGN), quarter), :]
        far_pick = table[n * sizes.stride + sizes.wanted + at]
        picked = source[far_at : far_at + far, :]
        for j in range(1, sizes.per_bucket):
            other = source[far_at + j * far : far_at + (j + 1) * far, :]
            picked = jnp.where(far_pick == j, other, picked)
        out[at, quarter : quarter + far, :] = picked


def first_kernel(sizes, place, near_cols, far_cols, near_rows, far_rows, near, pairs, *outs):
    table, own, out = outs
    fill_table(sizes, place, near_cols, far_cols, near_rows, far_rows, table)
    quarter, far = sizes.quarter, sizes.far
    far_at = sizes.per_bucket * quarter
    for j in range(sizes.per_bucket):
        own[j * quarter : (j + 1) * quarter, :] = near[j]
        own[far_at + j * far : far_at + (j + 1) * far, :] = pairs[j]
    pack_from(sizes, 0, table, own, out)


def send_shape(sizes, order):
    return jax.ShapeDtypeStruct((sizes.wanted, sizes.quarter + sizes.far, order), jnp.bfloat16)


def first(sizes, place, near_cols, far_cols, near_rows, far_rows, near, pairs):
    order = near.shape[2]
    rows = sizes.per_bucket * (sizes.quarter + sizes.far)
    return pl.pallas_call(
        functools.partial(first_kernel, sizes),
        in_specs=[SMEM] * 5 + [VMEM] * 2,
        out_specs=[SMEM, VMEM, VMEM],
        out_shape=[
            jax.ShapeDtypeStruct((sizes.table,), jnp.int32),
            jax.ShapeDtypeStruct((rows, order), jnp.bfloat16),
            send_shape(sizes, order),
        ],
        compiler_params=pltpu.CompilerParams(vmem_limit_bytes=VMEM_LIMIT),
        cost_estimate=pl.CostEstimate(flops=0, bytes_accessed=0, transcendentals=0),
    )(place, near_cols.T, far_cols.T, near_rows, far_rows, near, pairs)


def pack_kernel(sizes, n, table, *refs):
    sources, out = refs[: len(CHUNK_SOURCES[n])], refs[-1]
    for k, source in enumerate(sources):

        @pl.when(table[sizes.source_at(n)] == k)
        def _(source=source):
            pack_from(sizes, n, table, source, out)


def pack(sizes, n, table, sources, after):
    return pl.pallas_call(
        functools.partial(pack_kernel, sizes, n),
        in_specs=[SMEM] + [VMEM] * len(sources) + [KEPT] * len(after),
        out_specs=VMEM,
        out_shape=send_shape(sizes, sources[0].shape[1]),
        compiler_params=pltpu.CompilerParams(vmem_limit_bytes=VMEM_LIMIT),
        cost_estimate=pl.CostEstimate(flops=PACK_FLOPS, bytes_accessed=0, transcendentals=0),
    )(table, *sources, *after)


def rows_kernel(after, *refs):
    parts, out, token = refs[:-2], refs[-2], refs[-1]
    for k, part in enumerate(parts):
        out[k] = part[...]
    token[...] = jnp.zeros_like(token)


def join_rows(parts, after):
    return pl.pallas_call(
        rows_kernel,
        in_specs=[KEPT] + [VMEM] * len(parts),
        out_specs=[VMEM, VMEM],
        out_shape=[
            jax.ShapeDtypeStruct((len(parts),) + parts[0].shape, jnp.bfloat16),
            jax.ShapeDtypeStruct((8, LANES), jnp.float32),
        ],
        compiler_params=pltpu.CompilerParams(vmem_limit_bytes=VMEM_LIMIT),
        cost_estimate=pl.CostEstimate(flops=PACK_FLOPS, bytes_accessed=0, transcendentals=0),
    )(after, *parts)


def lefts_kernel(sizes, table, *refs):
    parts, lefts = refs[:-1], refs[-1]
    shard = sizes.shard
    inner, outer = table[sizes.inner_at], table[sizes.outer_at]
    for step, part in enumerate(parts):
        z = lax.rem(outer + OUTER - step, OUTER)
        for k in range(sizes.inner):
            x = lax.rem(inner + k, sizes.inner)
            at = pl.multiple_of((z * sizes.inner + x) * shard, ROW_ALIGN)
            for r in range(lefts.shape[0]):
                lefts[r, pl.ds(at, shard), :] = part[k, r]


def make_lefts(sizes, table, parts):
    row_group, shard, order = parts[0].shape[1:]
    return pl.pallas_call(
        functools.partial(lefts_kernel, sizes),
        in_specs=[SMEM] + [VMEM] * len(parts),
        out_specs=VMEM,
        out_shape=jax.ShapeDtypeStruct((row_group, order, order), jnp.bfloat16),
        compiler_params=pltpu.CompilerParams(vmem_limit_bytes=VMEM_LIMIT),
        cost_estimate=pl.CostEstimate(flops=0, bytes_accessed=0, transcendentals=0),
    )(table, *parts)


def halves(value):
    high = value.astype(jnp.bfloat16)
    return high, (value - high.astype(jnp.float32)).astype(jnp.bfloat16)


def update_kernel(sizes, n, table, near_tile, far_tile, lefts, got, *refs):
    near_out, far_out, panel, factors = refs[-4:]
    x = pl.program_id(0)
    slot = table[sizes.owner_at(n)] * sizes.inner + x
    quarter, far = sizes.quarter, sizes.far
    for g in range(sizes.groups):
        at = g * sizes.inner + x
        panel[g * quarter : (g + 1) * quarter, :] = got[at, 0:quarter, :]
        factors[g * far : (g + 1) * far, :] = got[at, quarter : quarter + far, :]
    filled = sizes.groups * far
    if filled < sizes.far_all:
        factors[filled:, :] = jnp.zeros_like(factors[filled:, :])
    across = (((1,), (1,)), ((), ()))
    product = lax.dot_general(
        lefts[table[sizes.near_rows_at + slot]],
        panel[...],
        across,
        preferred_element_type=jnp.float32,
    )
    near_out[0] = (near_tile[0].astype(jnp.float32) - product).astype(jnp.bfloat16)
    x_trans = jnp.dot(
        far_tile[0, 0],
        lefts[table[sizes.far_rows_at + slot]],
        preferred_element_type=jnp.float32,
    )
    pairs = factors[...]
    small = sum(
        lax.dot_general(part, pairs, across, preferred_element_type=jnp.float32)
        for part in halves(x_trans)
    )
    turned = pltpu.roll(small, sizes.far_all - 1, 1)
    lane = lax.broadcasted_iota(jnp.int32, turned.shape, 1)
    turned = jnp.where(lane % 2 == 0, turned, 0.0)
    change = sum(
        jnp.dot(part, pairs, preferred_element_type=jnp.float32) for part in halves(turned)
    )
    far_out[0] = (far_tile[0, 1].astype(jnp.float32) - change).astype(jnp.bfloat16)


def update(sizes, n, table, near_tiles, far_tiles, lefts, got, before):
    order, rank = near_tiles.shape[1], far_tiles.shape[2]

    def at_slot(*rest):
        return lambda x, table: (table[sizes.owner_at(n)] * sizes.inner + x,) + rest

    return pl.pallas_call(
        functools.partial(update_kernel, sizes, n),
        grid_spec=pltpu.PrefetchScalarGridSpec(
            num_scalar_prefetch=1,
            grid=(sizes.inner,),
            in_specs=[
                pl.BlockSpec((1, order, order), lambda x, table: (x, 0, 0)),
                pl.BlockSpec((1, 2, rank, order), lambda x, table: (x, 0, 0, 0)),
                VMEM,
                VMEM,
            ]
            + [KEPT] * len(before),
            out_specs=[
                pl.BlockSpec((1, order, order), at_slot(0, 0)),
                pl.BlockSpec((1, rank, order), at_slot(0, 0)),
            ],
            scratch_shapes=[
                pltpu.VMEM((order, order), jnp.bfloat16),
                pltpu.VMEM((sizes.far_all, order), jnp.bfloat16),
            ],
        ),
        out_shape=[
            jax.ShapeDtypeStruct((sizes.slots, order, order), jnp.bfloat16),
            jax.ShapeDtypeStruct((sizes.slots, rank, order), jnp.bfloat16),
        ],
        input_output_aliases={5 + k: k for k in range(len(before))},
        compiler_params=pltpu.CompilerParams(vmem_limit_bytes=VMEM_LIMIT),
        cost_estimate=pl.CostEstimate(flops=UPDATE_FLOPS, bytes_accessed=0, transcendentals=0),
    )(table, near_tiles, far_tiles, lefts, got, *before)


def shards(
    row_panel, col_near, col_far, near_tiles, near_rows, near_cols, far_tiles, far_rows, far_cols
):
    inner_size = lax.axis_size("inner")
    groups = lax.axis_size("gy") * lax.axis_size("core")
    outer, inner = lax.axis_index("outer"), lax.axis_index("inner")
    per_bucket, quarter, order = col_near.shape
    row_group, shard = row_panel.shape[:2]
    far_pairs = jnp.swapaxes(col_far, 1, 2).reshape(per_bucket, -1, order)
    far = -(-far_pairs.shape[1] // FAR_ALIGN) * FAR_ALIGN
    far_pairs = jnp.pad(far_pairs, ((0, 0), (0, far - far_pairs.shape[1]), (0, 0)))
    sizes = Sizes(groups, inner_size, per_bucket, quarter, far, shard)

    def along(value, pairs):
        return lax.ppermute(value, "outer", pairs)

    rows = [row_panel]
    for k in range(1, inner_size):
        turn = [((i + k) % inner_size, i) for i in range(inner_size)]
        rows.append(lax.ppermute(row_panel, "inner", turn))

    place = jnp.stack([outer, inner])
    table, own, send = first(
        sizes, place, near_cols, far_cols, near_rows, far_rows, col_near, far_pairs
    )
    held = {"own": own}
    held["pair"] = along(own, [(0, 1), (1, 0), (2, 3), (3, 2)])
    held["middle"] = along(own, [(1, 2), (2, 1)])
    held["cross"] = along(held["pair"], [(1, 2), (2, 1)])
    held["pass2"] = along(held["middle"], [(1, 0), (2, 3)])
    held["pass3"] = along(held["cross"], [(1, 0), (2, 3)])

    got, after = [], []
    for n in range(OUTER):
        if n > 0:
            send = pack(sizes, n, table, [held[name] for name in CHUNK_SOURCES[n]], after)
        got.append(lax.all_to_all(send, PLANE, split_axis=0, concat_axis=0, tiled=True))
        if n == 2:
            line, token = join_rows(rows, got[1])
            after = [token]

    parts = [line]
    for k in range(1, OUTER):
        parts.append(along(line, [(i, (i + k) % OUTER) for i in range(OUTER)]))
    lefts = make_lefts(sizes, table, parts)
    outs = ()
    for n in range(OUTER):
        at = jnp.asarray(CHUNK_OWNER[n], jnp.int32)[outer] * inner_size
        near = lax.dynamic_slice_in_dim(near_tiles, at, inner_size, 0)
        far_pair = lax.dynamic_slice_in_dim(far_tiles, at, inner_size, 0)
        outs = update(sizes, n, table, near, far_pair, lefts, got[n], outs)
    return tuple(outs)


def solution(mesh):
    groups, dev_count = mesh.shape["grp"], mesh.shape["dev"]
    fine = Mesh(
        mesh.devices.reshape(groups // 2, 2, OUTER, dev_count // OUTER),
        ("gy", "core", "outer", "inner"),
    )
    grp, dev = ("gy", "core"), ("outer", "inner")
    every = grp + dev
    placed = (
        P(grp, dev, None),
        P(dev, grp, None),
        P(dev, None, grp, None),
        P(every, None, None),
        P(every, None),
        P(),
        P(every, None, None, None),
        P(every, None),
        P(),
    )
    return jax.shard_map(
        shards,
        mesh=fine,
        in_specs=placed,
        out_specs=(P(every, None, None), P(every, None, None)),
        check_vma=False,
    )
```

```python
import functools

import jax
import jax.numpy as jnp
from jax import lax
from jax.experimental import pallas as pl
from jax.experimental.pallas import tpu as pltpu
from jax.sharding import Mesh, PartitionSpec as P

OUTER = 4
PLANE = ("gy", "core", "inner")
ROW_ALIGN = 16
FAR_ALIGN = 8
LANES = 128
VMEM_LIMIT = 16 * 1024 * 1024
WIDE_VMEM = 60 * 1024 * 1024
HBM = pl.BlockSpec(memory_space=pltpu.HBM)
CHUNK_OWNER = ((0, 1, 2, 3), (1, 0, 3, 2), (2, 2, 1, 1), (3, 3, 0, 0))
CHUNK_SOURCE = ((0, 0, 0, 0), (0, 0, 0, 0), (1, 0, 0, 1), (1, 0, 0, 1))
CHUNK_SOURCES = (("own",), ("pair",), ("middle", "pass2"), ("cross", "pass3"))
PACK_FLOPS = 10**10
UPDATE_FLOPS = 3 * 10**9
VMEM = pl.BlockSpec(memory_space=pltpu.VMEM)
SMEM = pl.BlockSpec(memory_space=pltpu.SMEM)
KEPT = pl.BlockSpec(memory_space=pl.ANY)


class Sizes:
    def __init__(self, groups, inner, per_bucket, quarter, far, shard):
        self.groups, self.inner, self.per_bucket = groups, inner, per_bucket
        self.quarter, self.far, self.shard = quarter, far, shard
        self.far_all = -(-groups * far // LANES) * LANES
        self.slots = OUTER * inner
        self.wanted = groups * inner
        self.stride = 2 * self.wanted + 2
        self.near_rows_at = OUTER * self.stride
        self.far_rows_at = self.near_rows_at + self.slots
        self.inner_at = self.far_rows_at + self.slots
        self.outer_at = self.inner_at + 1
        self.table = self.outer_at + 1

    def owner_at(self, n):
        return n * self.stride + 2 * self.wanted

    def source_at(self, n):
        return n * self.stride + 2 * self.wanted + 1


def by_position(values, position):
    result = jnp.int32(values[0])
    for k in range(1, len(values)):
        result = jnp.where(position == k, jnp.int32(values[k]), result)
    return result


def fill_table(sizes, place, near_cols, far_cols, near_rows, far_rows, table):
    outer, inner = place[0], place[1]
    table[sizes.inner_at] = inner
    table[sizes.outer_at] = outer
    for n in range(OUTER):
        owner = by_position(CHUNK_OWNER[n], outer)
        table[sizes.owner_at(n)] = owner
        table[sizes.source_at(n)] = by_position(CHUNK_SOURCE[n], outer)
        bucket = owner * sizes.inner + inner
        for g in range(sizes.groups):
            for x in range(sizes.inner):
                at = g * sizes.inner + x
                device = (g * OUTER + outer) * sizes.inner + x
                first = bucket * sizes.per_bucket
                table[n * sizes.stride + at] = near_cols[bucket, device] - first
                table[n * sizes.stride + sizes.wanted + at] = far_cols[bucket, device] - first
    for s in range(sizes.slots):
        table[sizes.near_rows_at + s] = near_rows[0, s]
        table[sizes.far_rows_at + s] = far_rows[0, s]


def pack_from(sizes, n, table, source, out, sent, sems):
    quarter, far = sizes.quarter, sizes.far
    far_at = sizes.per_bucket * quarter
    copies = []
    for at in range(sizes.wanted):
        near_pick = table[n * sizes.stride + at] * quarter
        out[at, 0:quarter, :] = source[pl.ds(pl.multiple_of(near_pick, ROW_ALIGN), quarter), :]
        far_pick = table[n * sizes.stride + sizes.wanted + at]
        picked = source[far_at : far_at + far, :]
        for j in range(1, sizes.per_bucket):
            other = source[far_at + j * far : far_at + (j + 1) * far, :]
            picked = jnp.where(far_pick == j, other, picked)
        out[at, quarter : quarter + far, :] = picked
        copies.append(pltpu.make_async_copy(out.at[at], sent.at[at], sems.at[at]))
        copies[at].start()
    for copy in copies:
        copy.wait()


def pack_scratch(sizes, order):
    return [
        pltpu.VMEM((sizes.wanted, sizes.quarter + sizes.far, order), jnp.bfloat16),
        pltpu.SemaphoreType.DMA((sizes.wanted,)),
    ]


def first_kernel(sizes, place, near_cols, far_cols, near_rows, far_rows, near, pairs, *outs):
    table, own, sent, out, sems = outs
    fill_table(sizes, place, near_cols, far_cols, near_rows, far_rows, table)
    quarter, far = sizes.quarter, sizes.far
    far_at = sizes.per_bucket * quarter
    for j in range(sizes.per_bucket):
        own[j * quarter : (j + 1) * quarter, :] = near[j]
        own[far_at + j * far : far_at + (j + 1) * far, :] = pairs[j]
    pack_from(sizes, 0, table, own, out, sent, sems)


def send_shape(sizes, order):
    return jax.ShapeDtypeStruct((sizes.wanted, sizes.quarter + sizes.far, order), jnp.bfloat16)


def first(sizes, place, near_cols, far_cols, near_rows, far_rows, near, pairs):
    order = near.shape[2]
    rows = sizes.per_bucket * (sizes.quarter + sizes.far)
    return pl.pallas_call(
        functools.partial(first_kernel, sizes),
        in_specs=[SMEM] * 5 + [VMEM] * 2,
        out_specs=[SMEM, VMEM, HBM],
        scratch_shapes=pack_scratch(sizes, order),
        out_shape=[
            jax.ShapeDtypeStruct((sizes.table,), jnp.int32),
            jax.ShapeDtypeStruct((rows, order), jnp.bfloat16),
            send_shape(sizes, order),
        ],
        compiler_params=pltpu.CompilerParams(vmem_limit_bytes=WIDE_VMEM),
        cost_estimate=pl.CostEstimate(flops=0, bytes_accessed=0, transcendentals=0),
    )(place, near_cols.T, far_cols.T, near_rows, far_rows, near, pairs)


def pack_kernel(sizes, n, table, *refs):
    sources, (sent, out, sems, held, held_sem) = refs[: len(CHUNK_SOURCES[n])], refs[-5:]
    for k, source in enumerate(sources):

        @pl.when(table[sizes.source_at(n)] == k)
        def _(source=source):
            load = pltpu.make_async_copy(source, held, held_sem.at[0])
            load.start()
            load.wait()

    pack_from(sizes, n, table, held, out, sent, sems)


def pack(sizes, n, table, sources, after):
    order = sources[0].shape[1]
    return pl.pallas_call(
        functools.partial(pack_kernel, sizes, n),
        in_specs=[SMEM] + [HBM] * len(sources) + [KEPT] * len(after),
        out_specs=HBM,
        out_shape=send_shape(sizes, order),
        scratch_shapes=pack_scratch(sizes, order)
        + [pltpu.VMEM(sources[0].shape, jnp.bfloat16), pltpu.SemaphoreType.DMA((1,))],
        compiler_params=pltpu.CompilerParams(vmem_limit_bytes=WIDE_VMEM),
        cost_estimate=pl.CostEstimate(flops=PACK_FLOPS, bytes_accessed=0, transcendentals=0),
    )(table, *sources, *after)


def rows_kernel(after, *refs):
    for k, part in enumerate(refs[:-1]):
        refs[-1][k] = part[...]


def join_rows(parts, after):
    return pl.pallas_call(
        rows_kernel,
        in_specs=[KEPT] + [VMEM] * len(parts),
        out_specs=VMEM,
        out_shape=jax.ShapeDtypeStruct((len(parts),) + parts[0].shape, jnp.bfloat16),
        compiler_params=pltpu.CompilerParams(vmem_limit_bytes=VMEM_LIMIT),
        cost_estimate=pl.CostEstimate(flops=PACK_FLOPS, bytes_accessed=0, transcendentals=0),
    )(after, *parts)


def lefts_kernel(sizes, table, *refs):
    parts, lefts = refs[:-1], refs[-1]
    shard = sizes.shard
    inner, outer = table[sizes.inner_at], table[sizes.outer_at]
    for step, part in enumerate(parts):
        z = lax.rem(outer + OUTER - step, OUTER)
        for k in range(sizes.inner):
            x = lax.rem(inner + k, sizes.inner)
            at = pl.multiple_of((z * sizes.inner + x) * shard, ROW_ALIGN)
            for r in range(lefts.shape[0]):
                lefts[r, pl.ds(at, shard), :] = part[k, r]


def make_lefts(sizes, table, parts):
    row_group, shard, order = parts[0].shape[1:]
    return pl.pallas_call(
        functools.partial(lefts_kernel, sizes),
        in_specs=[SMEM] + [VMEM] * len(parts),
        out_specs=VMEM,
        out_shape=jax.ShapeDtypeStruct((row_group, order, order), jnp.bfloat16),
        compiler_params=pltpu.CompilerParams(vmem_limit_bytes=VMEM_LIMIT),
        cost_estimate=pl.CostEstimate(flops=0, bytes_accessed=0, transcendentals=0),
    )(table, *parts)


def halves(value):
    high = value.astype(jnp.bfloat16)
    return high, (value - high.astype(jnp.float32)).astype(jnp.bfloat16)


def update_kernel(sizes, chunks, table, near_tile, far_tile, lefts, *refs):
    got, (near_out, far_out, panel, factors) = refs[: len(chunks)], refs[-4:]
    step = pl.program_id(0)
    x = step % sizes.inner
    slot = slot_of(sizes, chunks, step, table)
    quarter, far = sizes.quarter, sizes.far
    for k, part in enumerate(got):

        @pl.when(step // sizes.inner == k)
        def _(part=part):
            for g in range(sizes.groups):
                at = g * sizes.inner + x
                panel[g * quarter : (g + 1) * quarter, :] = part[at, 0:quarter, :]
                factors[g * far : (g + 1) * far, :] = part[at, quarter : quarter + far, :]

    filled = sizes.groups * far
    if filled < sizes.far_all:
        factors[filled:, :] = jnp.zeros_like(factors[filled:, :])
    across = (((1,), (1,)), ((), ()))
    product = lax.dot_general(
        lefts[table[sizes.near_rows_at + slot]],
        panel[...],
        across,
        preferred_element_type=jnp.float32,
    )
    near_out[0] = (near_tile[0].astype(jnp.float32) - product).astype(jnp.bfloat16)
    x_trans = jnp.dot(
        far_tile[0, 0],
        lefts[table[sizes.far_rows_at + slot]],
        preferred_element_type=jnp.float32,
    )
    pairs = factors[...]
    small = sum(
        lax.dot_general(part, pairs, across, preferred_element_type=jnp.float32)
        for part in halves(x_trans)
    )
    turned = pltpu.roll(small, sizes.far_all - 1, 1)
    lane = lax.broadcasted_iota(jnp.int32, turned.shape, 1)
    turned = jnp.where(lane % 2 == 0, turned, 0.0)
    change = sum(
        jnp.dot(part, pairs, preferred_element_type=jnp.float32) for part in halves(turned)
    )
    far_out[0] = (far_tile[0, 1].astype(jnp.float32) - change).astype(jnp.bfloat16)


def slot_of(sizes, chunks, step, table):
    k = step // sizes.inner
    owner = table[sizes.owner_at(chunks[0])]
    for j in range(1, len(chunks)):
        owner = jnp.where(k == j, table[sizes.owner_at(chunks[j])], owner)
    return owner * sizes.inner + step % sizes.inner


def update(sizes, chunks, table, near_tiles, far_tiles, lefts, got, before):
    order, rank = near_tiles.shape[1], far_tiles.shape[2]
    steps = len(chunks) * sizes.inner

    def at_slot(*rest):
        return lambda step, table: (slot_of(sizes, chunks, step, table),) + rest

    def at_step(*rest):
        return lambda step, table: (step,) + rest

    place_in = at_slot if near_tiles.shape[0] == sizes.slots else at_step
    return pl.pallas_call(
        functools.partial(update_kernel, sizes, chunks),
        grid_spec=pltpu.PrefetchScalarGridSpec(
            num_scalar_prefetch=1,
            grid=(steps,),
            in_specs=[
                pl.BlockSpec((1, order, order), place_in(0, 0)),
                pl.BlockSpec((1, 2, rank, order), place_in(0, 0, 0)),
                VMEM,
            ]
            + [VMEM] * len(got)
            + [KEPT] * len(before),
            out_specs=[
                pl.BlockSpec((1, order, order), at_slot(0, 0)),
                pl.BlockSpec((1, rank, order), at_slot(0, 0)),
            ],
            scratch_shapes=[
                pltpu.VMEM((order, order), jnp.bfloat16),
                pltpu.VMEM((sizes.far_all, order), jnp.bfloat16),
            ],
        ),
        out_shape=[
            jax.ShapeDtypeStruct((sizes.slots, order, order), jnp.bfloat16),
            jax.ShapeDtypeStruct((sizes.slots, rank, order), jnp.bfloat16),
        ],
        input_output_aliases={4 + len(got) + k: k for k in range(len(before))},
        compiler_params=pltpu.CompilerParams(vmem_limit_bytes=VMEM_LIMIT),
        cost_estimate=pl.CostEstimate(
            flops=UPDATE_FLOPS * len(chunks), bytes_accessed=0, transcendentals=0
        ),
    )(table, near_tiles, far_tiles, lefts, *got, *before)


def shards(
    row_panel, col_near, col_far, near_tiles, near_rows, near_cols, far_tiles, far_rows, far_cols
):
    inner_size = lax.axis_size("inner")
    groups = lax.axis_size("gy") * lax.axis_size("core")
    outer, inner = lax.axis_index("outer"), lax.axis_index("inner")
    per_bucket, quarter, order = col_near.shape
    row_group, shard = row_panel.shape[:2]
    far_pairs = jnp.swapaxes(col_far, 1, 2).reshape(per_bucket, -1, order)
    far = -(-far_pairs.shape[1] // FAR_ALIGN) * FAR_ALIGN
    far_pairs = jnp.pad(far_pairs, ((0, 0), (0, far - far_pairs.shape[1]), (0, 0)))
    sizes = Sizes(groups, inner_size, per_bucket, quarter, far, shard)

    def along(value, pairs):
        return lax.ppermute(value, "outer", pairs)

    rows = [row_panel]
    for k in range(1, inner_size):
        turn = [((i + k) % inner_size, i) for i in range(inner_size)]
        rows.append(lax.ppermute(row_panel, "inner", turn))

    place = jnp.stack([outer, inner])
    table, own, send = first(
        sizes, place, near_cols, far_cols, near_rows, far_rows, col_near, far_pairs
    )
    held = {"own": own}
    held["pair"] = along(own, [(0, 1), (1, 0), (2, 3), (3, 2)])
    held["middle"] = along(own, [(1, 2), (2, 1)])
    held["cross"] = along(held["pair"], [(1, 2), (2, 1)])
    held["pass2"] = along(held["middle"], [(1, 0), (2, 3)])
    held["pass3"] = along(held["cross"], [(1, 0), (2, 3)])

    got = []
    for n in range(OUTER):
        if n > 0:
            after = [held["cross"]] if n == 2 else []
            send = pack(sizes, n, table, [held[name] for name in CHUNK_SOURCES[n]], after)
        got.append(lax.all_to_all(send, PLANE, split_axis=0, concat_axis=0, tiled=True))

    line = join_rows(rows, held["pass3"])
    parts = [line]
    for k in range(1, OUTER):
        parts.append(along(line, [(i, (i + k) % OUTER) for i in range(OUTER)]))
    lefts = make_lefts(sizes, table, parts)
    outs = update(sizes, (0, 1, 2), table, near_tiles, far_tiles, lefts, got[:3], ())
    at = by_position(CHUNK_OWNER[3], outer) * inner_size
    near = lax.dynamic_slice_in_dim(near_tiles, at, inner_size, 0)
    far_pair = lax.dynamic_slice_in_dim(far_tiles, at, inner_size, 0)
    outs = update(sizes, (3,), table, near, far_pair, lefts, got[3:], outs)
    return tuple(outs)


def solution(mesh):
    groups, dev_count = mesh.shape["grp"], mesh.shape["dev"]
    fine = Mesh(
        mesh.devices.reshape(groups // 2, 2, OUTER, dev_count // OUTER),
        ("gy", "core", "outer", "inner"),
    )
    grp, dev = ("gy", "core"), ("outer", "inner")
    every = grp + dev
    placed = (
        P(grp, dev, None),
        P(dev, grp, None),
        P(dev, None, grp, None),
        P(every, None, None),
        P(every, None),
        P(),
        P(every, None, None, None),
        P(every, None),
        P(),
    )
    return jax.shard_map(
        shards,
        mesh=fine,
        in_specs=placed,
        out_specs=(P(every, None, None), P(every, None, None)),
        check_vma=False,
    )
```

```python
import functools

import jax
import jax.numpy as jnp
from jax import lax
from jax.experimental import pallas as pl
from jax.experimental.pallas import tpu as pltpu
from jax.sharding import Mesh, PartitionSpec as P

OUTER = 4
PLANE = ("gy", "core", "inner")
ROW_ALIGN = 16
FAR_ALIGN = 8
LANES = 128
VMEM_LIMIT = 16 * 1024 * 1024
WIDE_VMEM = 60 * 1024 * 1024
LEFTS_VMEM = 24 * 1024 * 1024
HBM = pl.BlockSpec(memory_space=pltpu.HBM)
CHUNK_OWNER = ((0, 1, 2, 3), (1, 0, 3, 2), (2, 2, 1, 1), (3, 3, 0, 0))
CHUNK_SOURCE = ((0, 0, 0, 0), (0, 0, 0, 0), (1, 0, 0, 1), (1, 0, 0, 1))
CHUNK_SOURCES = (("own",), ("pair",), ("middle", "pass2"), ("cross", "pass3"))
PACK_FLOPS = 10**10
UPDATE_FLOPS = 3 * 10**9
VMEM = pl.BlockSpec(memory_space=pltpu.VMEM)
SMEM = pl.BlockSpec(memory_space=pltpu.SMEM)
KEPT = pl.BlockSpec(memory_space=pl.ANY)


class Sizes:
    def __init__(self, groups, inner, per_bucket, quarter, far, shard):
        self.groups, self.inner, self.per_bucket = groups, inner, per_bucket
        self.quarter, self.far, self.shard = quarter, far, shard
        self.far_all = -(-groups * far // LANES) * LANES
        self.slots = OUTER * inner
        self.wanted = groups * inner
        self.stride = 2 * self.wanted + 2
        self.near_rows_at = OUTER * self.stride
        self.far_rows_at = self.near_rows_at + self.slots
        self.inner_at = self.far_rows_at + self.slots
        self.outer_at = self.inner_at + 1
        self.table = self.outer_at + 1

    def owner_at(self, n):
        return n * self.stride + 2 * self.wanted

    def source_at(self, n):
        return n * self.stride + 2 * self.wanted + 1


def by_position(values, position):
    result = jnp.int32(values[0])
    for k in range(1, len(values)):
        result = jnp.where(position == k, jnp.int32(values[k]), result)
    return result


def fill_table(sizes, near_cols, far_cols, near_rows, far_rows, table):
    outer, inner = lax.axis_index("outer"), lax.axis_index("inner")
    table[sizes.inner_at] = inner
    table[sizes.outer_at] = outer
    for n in range(OUTER):
        owner = by_position(CHUNK_OWNER[n], outer)
        table[sizes.owner_at(n)] = owner
        table[sizes.source_at(n)] = by_position(CHUNK_SOURCE[n], outer)
        bucket = owner * sizes.inner + inner
        for g in range(sizes.groups):
            for x in range(sizes.inner):
                at = g * sizes.inner + x
                device = (g * OUTER + outer) * sizes.inner + x
                first = bucket * sizes.per_bucket
                table[n * sizes.stride + at] = near_cols[bucket, device] - first
                table[n * sizes.stride + sizes.wanted + at] = far_cols[bucket, device] - first
    for s in range(sizes.slots):
        table[sizes.near_rows_at + s] = near_rows[0, s]
        table[sizes.far_rows_at + s] = far_rows[0, s]


def pack_from(sizes, n, table, source, out, sent, sems):
    quarter, far = sizes.quarter, sizes.far
    far_at = sizes.per_bucket * quarter
    copies = []
    for at in range(sizes.wanted):
        near_pick = table[n * sizes.stride + at] * quarter
        out[at, 0:quarter, :] = source[pl.ds(pl.multiple_of(near_pick, ROW_ALIGN), quarter), :]
        far_pick = table[n * sizes.stride + sizes.wanted + at]
        picked = source[far_at : far_at + far, :]
        for j in range(1, sizes.per_bucket):
            other = source[far_at + j * far : far_at + (j + 1) * far, :]
            picked = jnp.where(far_pick == j, other, picked)
        out[at, quarter : quarter + far, :] = picked
        copies.append(pltpu.make_async_copy(out.at[at], sent.at[at], sems.at[at]))
        copies[at].start()
    for copy in copies:
        copy.wait()


def pack_scratch(sizes, order):
    return [
        pltpu.VMEM((sizes.wanted, sizes.quarter + sizes.far, order), jnp.bfloat16),
        pltpu.SemaphoreType.DMA((sizes.wanted,)),
    ]


def first_kernel(sizes, near_cols, far_cols, near_rows, far_rows, near, pairs, *outs):
    table, own, sent, out, sems = outs
    fill_table(sizes, near_cols, far_cols, near_rows, far_rows, table)
    quarter, far = sizes.quarter, sizes.far
    far_at = sizes.per_bucket * quarter
    for j in range(sizes.per_bucket):
        own[j * quarter : (j + 1) * quarter, :] = near[j]
        at = far_at + j * far
        count = 2 * pairs.shape[1]
        for r in range(pairs.shape[1]):
            own[at + 2 * r : at + 2 * r + 2, :] = pairs[j, r]
        if count < far:
            own[at + count : at + far, :] = jnp.zeros((far - count, own.shape[1]), own.dtype)
    pack_from(sizes, 0, table, own, out, sent, sems)


def send_shape(sizes, order):
    return jax.ShapeDtypeStruct((sizes.wanted, sizes.quarter + sizes.far, order), jnp.bfloat16)


def first(sizes, near_cols, far_cols, near_rows, far_rows, near, pairs):
    order = near.shape[2]
    rows = sizes.per_bucket * (sizes.quarter + sizes.far)
    return pl.pallas_call(
        functools.partial(first_kernel, sizes),
        in_specs=[SMEM] * 4 + [VMEM] * 2,
        out_specs=[SMEM, VMEM, HBM],
        scratch_shapes=pack_scratch(sizes, order),
        out_shape=[
            jax.ShapeDtypeStruct((sizes.table,), jnp.int32),
            jax.ShapeDtypeStruct((rows, order), jnp.bfloat16),
            send_shape(sizes, order),
        ],
        compiler_params=pltpu.CompilerParams(vmem_limit_bytes=WIDE_VMEM),
        cost_estimate=pl.CostEstimate(flops=0, bytes_accessed=0, transcendentals=0),
    )(near_cols.T, far_cols.T, near_rows, far_rows, near, pairs)


def pack_kernel(sizes, n, table, *refs):
    sources, (sent, out, sems, held, held_sem) = refs[: len(CHUNK_SOURCES[n])], refs[-5:]
    for k, source in enumerate(sources):

        @pl.when(table[sizes.source_at(n)] == k)
        def _(source=source):
            load = pltpu.make_async_copy(source, held, held_sem.at[0])
            load.start()
            load.wait()

    pack_from(sizes, n, table, held, out, sent, sems)


def pack(sizes, n, table, sources, after):
    order = sources[0].shape[1]
    return pl.pallas_call(
        functools.partial(pack_kernel, sizes, n),
        in_specs=[SMEM] + [HBM] * len(sources) + [KEPT] * len(after),
        out_specs=HBM,
        out_shape=send_shape(sizes, order),
        scratch_shapes=pack_scratch(sizes, order)
        + [pltpu.VMEM(sources[0].shape, jnp.bfloat16), pltpu.SemaphoreType.DMA((1,))],
        compiler_params=pltpu.CompilerParams(vmem_limit_bytes=WIDE_VMEM),
        cost_estimate=pl.CostEstimate(flops=PACK_FLOPS, bytes_accessed=0, transcendentals=0),
    )(table, *sources, *after)


def rows_kernel(after, *refs):
    for k, part in enumerate(refs[:-1]):
        refs[-1][k] = part[...]


def join_rows(parts, after):
    return pl.pallas_call(
        rows_kernel,
        in_specs=[KEPT] + [VMEM] * len(parts),
        out_specs=VMEM,
        out_shape=jax.ShapeDtypeStruct((len(parts),) + parts[0].shape, jnp.bfloat16),
        compiler_params=pltpu.CompilerParams(vmem_limit_bytes=VMEM_LIMIT),
        cost_estimate=pl.CostEstimate(flops=PACK_FLOPS, bytes_accessed=0, transcendentals=0),
    )(after, *parts)


def lefts_kernel(sizes, table, far_tiles, *refs):
    parts, (lefts, x_halves) = refs[:-2], refs[-2:]
    shard = sizes.shard
    inner, outer = table[sizes.inner_at], table[sizes.outer_at]
    for step, part in enumerate(parts):
        z = lax.rem(outer + OUTER - step, OUTER)
        for k in range(sizes.inner):
            x = lax.rem(inner + k, sizes.inner)
            at = pl.multiple_of((z * sizes.inner + x) * shard, ROW_ALIGN)
            for r in range(lefts.shape[0]):
                lefts[r, pl.ds(at, shard), :] = part[k, r]
    rank = far_tiles.shape[2]
    bases = jnp.concatenate([far_tiles[s, 0] for s in range(sizes.slots)], axis=0)
    for r in range(lefts.shape[0]):
        x_trans = jnp.dot(bases, lefts[r], preferred_element_type=jnp.float32)
        for s in range(sizes.slots):

            @pl.when(table[sizes.far_rows_at + s] == r)
            def _(s=s, own=x_trans[s * rank : (s + 1) * rank]):
                x_halves[s] = halves(own)


def make_lefts(sizes, table, far_tiles, parts):
    row_group, shard, order = parts[0].shape[1:]
    rank = far_tiles.shape[2]
    return pl.pallas_call(
        functools.partial(lefts_kernel, sizes),
        in_specs=[SMEM, VMEM] + [VMEM] * len(parts),
        out_specs=[VMEM, VMEM],
        out_shape=[
            jax.ShapeDtypeStruct((row_group, order, order), jnp.bfloat16),
            jax.ShapeDtypeStruct((sizes.slots, 2 * rank, order), jnp.bfloat16),
        ],
        compiler_params=pltpu.CompilerParams(vmem_limit_bytes=LEFTS_VMEM),
        cost_estimate=pl.CostEstimate(flops=0, bytes_accessed=0, transcendentals=0),
    )(table, far_tiles, *parts)


def halves(value):
    high = value.astype(jnp.bfloat16)
    low = (value - high.astype(jnp.float32)).astype(jnp.bfloat16)
    return jnp.concatenate([high, low], axis=0)


ACROSS = (((1,), (1,)), ((), ()))


def near_update(tile, left, panel):
    product = lax.dot_general(left, panel, ACROSS, preferred_element_type=jnp.float32)
    return (tile.astype(jnp.float32) - product).astype(jnp.bfloat16)


def far_update(tile, x_halves, pairs):
    rank = tile.shape[0]
    both = lax.dot_general(x_halves, pairs, ACROSS, preferred_element_type=jnp.float32)
    small = both[:rank] + both[rank:]
    turned = pltpu.roll(small, small.shape[1] - 1, 1)
    lane = lax.broadcasted_iota(jnp.int32, turned.shape, 1)
    turned = jnp.where(lane % 2 == 0, turned, 0.0)
    change = jnp.dot(halves(turned), pairs, preferred_element_type=jnp.float32)
    return (tile.astype(jnp.float32) - (change[:rank] + change[rank:])).astype(jnp.bfloat16)


def clear_rest(sizes, factors):
    filled = sizes.groups * sizes.far
    if filled < sizes.far_all:
        factors[filled:, :] = jnp.zeros_like(factors[filled:, :])


def take_part(sizes, g, part, panel, factors):
    quarter, far = sizes.quarter, sizes.far
    panel[g * quarter : (g + 1) * quarter, :] = part[0:quarter, :]
    factors[g * far : (g + 1) * far, :] = part[quarter : quarter + far, :]


def update_kernel(sizes, chunks, table, near_tile, far_tile, lefts, x_halves, *refs):
    got, (near_out, far_out, panel, factors) = refs[: len(chunks)], refs[-4:]
    step = pl.program_id(0)
    x = step % sizes.inner
    slot = slot_of(sizes, chunks, step, table)
    for k, part in enumerate(got):

        @pl.when(step // sizes.inner == k)
        def _(part=part):
            for g in range(sizes.groups):
                take_part(sizes, g, part.at[g * sizes.inner + x], panel, factors)

    clear_rest(sizes, factors)
    left = lefts[table[sizes.near_rows_at + slot]]
    near_out[0] = near_update(near_tile[0], left, panel[...])
    far_out[0] = far_update(far_tile[0, 1], x_halves[slot], factors[...])


def slot_of(sizes, chunks, step, table):
    k = step // sizes.inner
    owner = table[sizes.owner_at(chunks[0])]
    for j in range(1, len(chunks)):
        owner = jnp.where(k == j, table[sizes.owner_at(chunks[j])], owner)
    return owner * sizes.inner + step % sizes.inner


def out_shapes(sizes, near_tiles, far_tiles):
    order, rank = near_tiles.shape[1], far_tiles.shape[2]
    return [
        jax.ShapeDtypeStruct((sizes.slots, order, order), jnp.bfloat16),
        jax.ShapeDtypeStruct((sizes.slots, rank, order), jnp.bfloat16),
    ]


def update(sizes, chunks, table, near_tiles, far_tiles, lefts, x_halves, got):
    order, rank = near_tiles.shape[1], far_tiles.shape[2]

    def at_slot(*rest):
        return lambda step, table: (slot_of(sizes, chunks, step, table),) + rest

    return pl.pallas_call(
        functools.partial(update_kernel, sizes, chunks),
        grid_spec=pltpu.PrefetchScalarGridSpec(
            num_scalar_prefetch=1,
            grid=(len(chunks) * sizes.inner,),
            in_specs=[
                pl.BlockSpec((1, order, order), at_slot(0, 0)),
                pl.BlockSpec((1, 2, rank, order), at_slot(0, 0, 0)),
                VMEM,
                VMEM,
            ]
            + [VMEM] * len(got),
            out_specs=[
                pl.BlockSpec((1, order, order), at_slot(0, 0)),
                pl.BlockSpec((1, rank, order), at_slot(0, 0)),
            ],
            scratch_shapes=[
                pltpu.VMEM((order, order), jnp.bfloat16),
                pltpu.VMEM((sizes.far_all, order), jnp.bfloat16),
            ],
        ),
        out_shape=out_shapes(sizes, near_tiles, far_tiles),
        compiler_params=pltpu.CompilerParams(vmem_limit_bytes=VMEM_LIMIT),
        cost_estimate=pl.CostEstimate(
            flops=UPDATE_FLOPS * len(chunks), bytes_accessed=0, transcendentals=0
        ),
    )(table, near_tiles, far_tiles, lefts, x_halves, *got)


def last_kernel(sizes, n, table, near_tiles, far_tiles, lefts, x_halves, got, *refs):
    near_out, far_out = refs[2:4]
    tile, far_tile, left, x_half, parts, near_done, far_done, panel, factors, sems = refs[4:]
    first = table[sizes.owner_at(n)] * sizes.inner
    loads = []
    for x in range(sizes.inner):
        slot = first + x
        pairs = [(got.at[g * sizes.inner + x], parts.at[x, g]) for g in range(sizes.groups)]
        pairs += [
            (lefts.at[table[sizes.near_rows_at + slot]], left.at[x]),
            (near_tiles.at[slot], tile.at[x]),
            (x_halves.at[slot], x_half.at[x]),
            (far_tiles.at[slot, 1], far_tile.at[x]),
        ]
        loads.append(
            [
                pltpu.make_async_copy(source, to, sems.at[x, k])
                for k, (source, to) in enumerate(pairs)
            ]
        )
        for load in loads[x]:
            load.start()
    clear_rest(sizes, factors)
    stores = []
    at = sizes.groups + 4
    for x in range(sizes.inner):
        for load in loads[x]:
            load.wait()
        for g in range(sizes.groups):
            take_part(sizes, g, parts.at[x, g], panel, factors)
        near_done[x] = near_update(tile[x], left[x], panel[...])
        stores.append(
            pltpu.make_async_copy(near_done.at[x], near_out.at[first + x], sems.at[x, at])
        )
        stores[-1].start()
        far_done[x] = far_update(far_tile[x], x_half[x], factors[...])
        stores.append(
            pltpu.make_async_copy(far_done.at[x], far_out.at[first + x], sems.at[x, at + 1])
        )
        stores[-1].start()
    for store in stores:
        store.wait()


def last_update(sizes, n, table, near_tiles, far_tiles, lefts, x_halves, got, before):
    order, rank = near_tiles.shape[1], far_tiles.shape[2]
    inner, groups = sizes.inner, sizes.groups
    return pl.pallas_call(
        functools.partial(last_kernel, sizes, n),
        in_specs=[SMEM] + [HBM] * 7,
        out_specs=[HBM, HBM],
        out_shape=out_shapes(sizes, near_tiles, far_tiles),
        scratch_shapes=[
            pltpu.VMEM((inner, order, order), jnp.bfloat16),
            pltpu.VMEM((inner, rank, order), jnp.bfloat16),
            pltpu.VMEM((inner, order, order), jnp.bfloat16),
            pltpu.VMEM((inner, 2 * rank, order), jnp.bfloat16),
            pltpu.VMEM((inner, groups, sizes.quarter + sizes.far, order), jnp.bfloat16),
            pltpu.VMEM((inner, order, order), jnp.bfloat16),
            pltpu.VMEM((inner, rank, order), jnp.bfloat16),
            pltpu.VMEM((order, order), jnp.bfloat16),
            pltpu.VMEM((sizes.far_all, order), jnp.bfloat16),
            pltpu.SemaphoreType.DMA((inner, groups + 6)),
        ],
        input_output_aliases={6: 0, 7: 1},
        compiler_params=pltpu.CompilerParams(vmem_limit_bytes=WIDE_VMEM),
        cost_estimate=pl.CostEstimate(flops=UPDATE_FLOPS, bytes_accessed=0, transcendentals=0),
    )(table, near_tiles, far_tiles, lefts, x_halves, got, *before)


def shards(
    row_panel, col_near, col_far, near_tiles, near_rows, near_cols, far_tiles, far_rows, far_cols
):
    inner_size = lax.axis_size("inner")
    groups = lax.axis_size("gy") * lax.axis_size("core")
    per_bucket, quarter, order = col_near.shape
    row_group, shard = row_panel.shape[:2]
    far_pairs = jnp.swapaxes(col_far, 1, 2)
    far = -(-2 * col_far.shape[2] // FAR_ALIGN) * FAR_ALIGN
    sizes = Sizes(groups, inner_size, per_bucket, quarter, far, shard)

    def along(value, pairs):
        return lax.ppermute(value, "outer", pairs)

    rows = [row_panel]
    for k in range(1, inner_size):
        turn = [((i + k) % inner_size, i) for i in range(inner_size)]
        rows.append(lax.ppermute(row_panel, "inner", turn))

    table, own, send = first(
        sizes, near_cols, far_cols, near_rows, far_rows, col_near, far_pairs
    )
    held = {"own": own}
    held["pair"] = along(own, [(0, 1), (1, 0), (2, 3), (3, 2)])
    held["middle"] = along(own, [(1, 2), (2, 1)])
    held["cross"] = along(held["pair"], [(1, 2), (2, 1)])
    held["pass2"] = along(held["middle"], [(1, 0), (2, 3)])
    held["pass3"] = along(held["cross"], [(1, 0), (2, 3)])

    got = []
    for n in range(OUTER):
        if n > 0:
            after = [held["cross"]] if n == 2 else []
            send = pack(sizes, n, table, [held[name] for name in CHUNK_SOURCES[n]], after)
        got.append(lax.all_to_all(send, PLANE, split_axis=0, concat_axis=0, tiled=True))

    line = join_rows(rows, held["pass3"])
    parts = [line]
    for k in range(1, OUTER):
        parts.append(along(line, [(i, (i + k) % OUTER) for i in range(OUTER)]))
    lefts, x_halves = make_lefts(sizes, table, far_tiles, parts)
    tiles = (near_tiles, far_tiles, lefts, x_halves)
    outs = update(sizes, (0, 1, 2), table, *tiles, got[:3])
    outs = last_update(sizes, 3, table, *tiles, got[3], outs)
    return tuple(outs)


def solution(mesh):
    groups, dev_count = mesh.shape["grp"], mesh.shape["dev"]
    fine = Mesh(
        mesh.devices.reshape(groups // 2, 2, OUTER, dev_count // OUTER),
        ("gy", "core", "outer", "inner"),
    )
    grp, dev = ("gy", "core"), ("outer", "inner")
    every = grp + dev
    placed = (
        P(grp, dev, None),
        P(dev, grp, None),
        P(dev, None, grp, None),
        P(every, None, None),
        P(every, None),
        P(),
        P(every, None, None, None),
        P(every, None),
        P(),
    )
    return jax.shard_map(
        shards,
        mesh=fine,
        in_specs=placed,
        out_specs=(P(every, None, None), P(every, None, None)),
        check_vma=False,
    )
```

```python
import functools

import jax
import jax.numpy as jnp
from jax import lax
from jax.experimental import pallas as pl
from jax.experimental.pallas import tpu as pltpu
from jax.sharding import Mesh, PartitionSpec as P

OUTER = 4
PLANE = ("gy", "core", "inner")
ROW_ALIGN = 16
FAR_ALIGN = 8
LANES = 128
VMEM_LIMIT = 16 * 1024 * 1024
WIDE_VMEM = 60 * 1024 * 1024
LEFTS_VMEM = 24 * 1024 * 1024
HBM = pl.BlockSpec(memory_space=pltpu.HBM)
CHUNK_OWNER = ((0, 1, 2, 3), (1, 0, 3, 2), (2, 2, 1, 1), (3, 3, 0, 0))
CHUNK_SOURCE = ((0, 0, 0, 0), (0, 0, 0, 0), (1, 0, 0, 1), (1, 0, 0, 1))
CHUNK_SOURCES = (("own",), ("pair",), ("middle", "pass2"), ("cross", "pass3"))
PACK_FLOPS = 10**10
UPDATE_FLOPS = 3 * 10**9
VMEM = pl.BlockSpec(memory_space=pltpu.VMEM)
SMEM = pl.BlockSpec(memory_space=pltpu.SMEM)
KEPT = pl.BlockSpec(memory_space=pl.ANY)


class Sizes:
    def __init__(self, groups, inner, per_bucket, quarter, far, shard):
        self.groups, self.inner, self.per_bucket = groups, inner, per_bucket
        self.quarter, self.far, self.shard = quarter, far, shard
        self.far_all = -(-groups * far // LANES) * LANES
        self.slots = OUTER * inner
        self.wanted = groups * inner
        self.stride = 2 * self.wanted + 2
        self.near_rows_at = OUTER * self.stride
        self.far_rows_at = self.near_rows_at + self.slots
        self.inner_at = self.far_rows_at + self.slots
        self.outer_at = self.inner_at + 1
        self.table = self.outer_at + 1

    def owner_at(self, n):
        return n * self.stride + 2 * self.wanted

    def source_at(self, n):
        return n * self.stride + 2 * self.wanted + 1


def by_position(values, position):
    result = jnp.int32(values[0])
    for k in range(1, len(values)):
        result = jnp.where(position == k, jnp.int32(values[k]), result)
    return result


def fill_table(sizes, near_cols, far_cols, near_rows, far_rows, table):
    outer, inner = lax.axis_index("outer"), lax.axis_index("inner")
    table[sizes.inner_at] = inner
    table[sizes.outer_at] = outer
    for n in range(OUTER):
        owner = by_position(CHUNK_OWNER[n], outer)
        table[sizes.owner_at(n)] = owner
        table[sizes.source_at(n)] = by_position(CHUNK_SOURCE[n], outer)
        bucket = owner * sizes.inner + inner
        for g in range(sizes.groups):
            for x in range(sizes.inner):
                at = g * sizes.inner + x
                device = (g * OUTER + outer) * sizes.inner + x
                first = bucket * sizes.per_bucket
                table[n * sizes.stride + at] = near_cols[bucket, device] - first
                table[n * sizes.stride + sizes.wanted + at] = far_cols[bucket, device] - first
    for s in range(sizes.slots):
        table[sizes.near_rows_at + s] = near_rows[0, s]
        table[sizes.far_rows_at + s] = far_rows[0, s]


def pack_from(sizes, n, table, source, out, sent, sems):
    quarter, far = sizes.quarter, sizes.far
    far_at = sizes.per_bucket * quarter
    copies = []
    for at in range(sizes.wanted):
        near_pick = table[n * sizes.stride + at] * quarter
        out[at, 0:quarter, :] = source[pl.ds(pl.multiple_of(near_pick, ROW_ALIGN), quarter), :]
        far_pick = table[n * sizes.stride + sizes.wanted + at]
        picked = source[far_at : far_at + far, :]
        for j in range(1, sizes.per_bucket):
            other = source[far_at + j * far : far_at + (j + 1) * far, :]
            picked = jnp.where(far_pick == j, other, picked)
        out[at, quarter : quarter + far, :] = picked
        copies.append(pltpu.make_async_copy(out.at[at], sent.at[at], sems.at[at]))
        copies[at].start()
    for copy in copies:
        copy.wait()


def pack_scratch(sizes, order):
    return [
        pltpu.VMEM((sizes.wanted, sizes.quarter + sizes.far, order), jnp.bfloat16),
        pltpu.SemaphoreType.DMA((sizes.wanted,)),
    ]


def first_kernel(sizes, near_cols, far_cols, near_rows, far_rows, near, pairs, *outs):
    table, own, sent, out, sems = outs
    fill_table(sizes, near_cols, far_cols, near_rows, far_rows, table)
    quarter, far = sizes.quarter, sizes.far
    far_at = sizes.per_bucket * quarter
    for j in range(sizes.per_bucket):
        own[j * quarter : (j + 1) * quarter, :] = near[j]
        at = far_at + j * far
        count = 2 * pairs.shape[1]
        for r in range(pairs.shape[1]):
            own[at + 2 * r : at + 2 * r + 2, :] = pairs[j, r]
        if count < far:
            own[at + count : at + far, :] = jnp.zeros((far - count, own.shape[1]), own.dtype)
    pack_from(sizes, 0, table, own, out, sent, sems)


def send_shape(sizes, order):
    return jax.ShapeDtypeStruct((sizes.wanted, sizes.quarter + sizes.far, order), jnp.bfloat16)


def first(sizes, near_cols, far_cols, near_rows, far_rows, near, pairs):
    order = near.shape[2]
    rows = sizes.per_bucket * (sizes.quarter + sizes.far)
    return pl.pallas_call(
        functools.partial(first_kernel, sizes),
        in_specs=[SMEM] * 4 + [VMEM] * 2,
        out_specs=[SMEM, VMEM, HBM],
        scratch_shapes=pack_scratch(sizes, order),
        out_shape=[
            jax.ShapeDtypeStruct((sizes.table,), jnp.int32),
            jax.ShapeDtypeStruct((rows, order), jnp.bfloat16),
            send_shape(sizes, order),
        ],
        compiler_params=pltpu.CompilerParams(vmem_limit_bytes=WIDE_VMEM),
        cost_estimate=pl.CostEstimate(flops=0, bytes_accessed=0, transcendentals=0),
    )(near_cols.T, far_cols.T, near_rows, far_rows, near, pairs)


def pack_kernel(sizes, n, table, *refs):
    sources, (sent, out, sems, held, held_sem) = refs[: len(CHUNK_SOURCES[n])], refs[-5:]
    for k, source in enumerate(sources):

        @pl.when(table[sizes.source_at(n)] == k)
        def _(source=source):
            load = pltpu.make_async_copy(source, held, held_sem.at[0])
            load.start()
            load.wait()

    pack_from(sizes, n, table, held, out, sent, sems)


def pack(sizes, n, table, sources, after):
    order = sources[0].shape[1]
    return pl.pallas_call(
        functools.partial(pack_kernel, sizes, n),
        in_specs=[SMEM] + [HBM] * len(sources) + [KEPT] * len(after),
        out_specs=HBM,
        out_shape=send_shape(sizes, order),
        scratch_shapes=pack_scratch(sizes, order)
        + [pltpu.VMEM(sources[0].shape, jnp.bfloat16), pltpu.SemaphoreType.DMA((1,))],
        compiler_params=pltpu.CompilerParams(vmem_limit_bytes=WIDE_VMEM),
        cost_estimate=pl.CostEstimate(flops=PACK_FLOPS, bytes_accessed=0, transcendentals=0),
    )(table, *sources, *after)


def rows_kernel(after, *refs):
    for k, part in enumerate(refs[:-1]):
        refs[-1][k] = part[...]


def join_rows(parts, after):
    return pl.pallas_call(
        rows_kernel,
        in_specs=[KEPT] + [VMEM] * len(parts),
        out_specs=VMEM,
        out_shape=jax.ShapeDtypeStruct((len(parts),) + parts[0].shape, jnp.bfloat16),
        compiler_params=pltpu.CompilerParams(vmem_limit_bytes=VMEM_LIMIT),
        cost_estimate=pl.CostEstimate(flops=PACK_FLOPS, bytes_accessed=0, transcendentals=0),
    )(after, *parts)


def lefts_kernel(sizes, table, far_tiles, line, near1, near2, near3, relayed, lefts, x_halves):
    shard = sizes.shard
    inner, outer = table[sizes.inner_at], table[sizes.outer_at]

    def place(z, part):
        for k in range(sizes.inner):
            x = lax.rem(inner + k, sizes.inner)
            at = pl.multiple_of((z * sizes.inner + x) * shard, ROW_ALIGN)
            for r in range(lefts.shape[0]):
                lefts[r, pl.ds(at, shard), :] = part[k, r]

    place(outer, line)
    amid = (outer == 1) | (outer == 2)
    for n, part in ((1, near1), (2, near2), (3, near3)):
        owner = table[sizes.owner_at(n)]
        pl.when(amid)(functools.partial(place, owner, part))
        pl.when(jnp.logical_not(amid))(functools.partial(place, owner, relayed.at[n - 1]))
    rank = far_tiles.shape[2]
    bases = jnp.concatenate([far_tiles[s, 0] for s in range(sizes.slots)], axis=0)
    for r in range(lefts.shape[0]):
        x_trans = jnp.dot(bases, lefts[r], preferred_element_type=jnp.float32)
        for s in range(sizes.slots):

            @pl.when(table[sizes.far_rows_at + s] == r)
            def _(s=s, own=x_trans[s * rank : (s + 1) * rank]):
                x_halves[s] = halves(own)


def make_lefts(sizes, table, far_tiles, parts):
    row_group, _, order = parts[0].shape[1:]
    rank = far_tiles.shape[2]
    return pl.pallas_call(
        functools.partial(lefts_kernel, sizes),
        in_specs=[SMEM, VMEM] + [VMEM] * len(parts),
        out_specs=[VMEM, VMEM],
        out_shape=[
            jax.ShapeDtypeStruct((row_group, order, order), jnp.bfloat16),
            jax.ShapeDtypeStruct((sizes.slots, 2 * rank, order), jnp.bfloat16),
        ],
        compiler_params=pltpu.CompilerParams(vmem_limit_bytes=LEFTS_VMEM),
        cost_estimate=pl.CostEstimate(flops=0, bytes_accessed=0, transcendentals=0),
    )(table, far_tiles, *parts)


def halves(value):
    high = value.astype(jnp.bfloat16)
    low = (value - high.astype(jnp.float32)).astype(jnp.bfloat16)
    return jnp.concatenate([high, low], axis=0)


ACROSS = (((1,), (1,)), ((), ()))


def near_update(tile, left, panel):
    product = lax.dot_general(left, panel, ACROSS, preferred_element_type=jnp.float32)
    return (tile.astype(jnp.float32) - product).astype(jnp.bfloat16)


def far_update(tile, x_halves, pairs):
    rank = tile.shape[0]
    both = lax.dot_general(x_halves, pairs, ACROSS, preferred_element_type=jnp.float32)
    small = both[:rank] + both[rank:]
    turned = pltpu.roll(small, small.shape[1] - 1, 1)
    lane = lax.broadcasted_iota(jnp.int32, turned.shape, 1)
    turned = jnp.where(lane % 2 == 0, turned, 0.0)
    change = jnp.dot(halves(turned), pairs, preferred_element_type=jnp.float32)
    return (tile.astype(jnp.float32) - (change[:rank] + change[rank:])).astype(jnp.bfloat16)


def clear_rest(sizes, factors):
    filled = sizes.groups * sizes.far
    if filled < sizes.far_all:
        factors[filled:, :] = jnp.zeros_like(factors[filled:, :])


def take_part(sizes, g, part, panel, factors):
    quarter, far = sizes.quarter, sizes.far
    panel[g * quarter : (g + 1) * quarter, :] = part[0:quarter, :]
    factors[g * far : (g + 1) * far, :] = part[quarter : quarter + far, :]


def out_shapes(sizes, near_tiles, far_tiles):
    order, rank = near_tiles.shape[1], far_tiles.shape[2]
    return [
        jax.ShapeDtypeStruct((sizes.slots, order, order), jnp.bfloat16),
        jax.ShapeDtypeStruct((sizes.slots, rank, order), jnp.bfloat16),
    ]


def update_kernel(sizes, chunks, table, near_tiles, far_tiles, lefts, x_halves, *refs):
    got, (near_out, far_out) = refs[: len(chunks)], refs[-12:-10]
    tile, far_tile, left, x_half, parts, near_done, far_done, panel, factors, sems = refs[-10:]
    left_loads = [
        pltpu.make_async_copy(lefts.at[r], left.at[r], sems.at[0, sizes.groups + 5 + r])
        for r in range(left.shape[0])
    ]
    slots, loads = [], []
    for k, n in enumerate(chunks):
        for x in range(sizes.inner):
            at = len(slots)
            slot = table[sizes.owner_at(n)] * sizes.inner + x
            pairs = [(got[k].at[g * sizes.inner + x], parts.at[at, g]) for g in range(sizes.groups)]
            pairs += [
                (near_tiles.at[slot], tile.at[at]),
                (x_halves.at[slot], x_half.at[at]),
                (far_tiles.at[slot, 1], far_tile.at[at]),
            ]
            slots.append(slot)
            loads.append(
                [
                    pltpu.make_async_copy(source, to, sems.at[at, j])
                    for j, (source, to) in enumerate(pairs)
                ]
            )
    for load in loads[0] + left_loads + sum(loads[1:], []):
        load.start()
    clear_rest(sizes, factors)
    for load in left_loads:
        load.wait()
    stores = []
    for at, slot in enumerate(slots):
        for load in loads[at]:
            load.wait()
        for g in range(sizes.groups):
            take_part(sizes, g, parts.at[at, g], panel, factors)
        own_left = left[table[sizes.near_rows_at + slot]]
        near_done[at] = near_update(tile[at], own_left, panel[...])
        far_done[at] = far_update(far_tile[at], x_half[at], factors[...])
        for j, (done, out) in enumerate(((near_done, near_out), (far_done, far_out))):
            copy = pltpu.make_async_copy(
                done.at[at], out.at[slot], sems.at[at, sizes.groups + 3 + j]
            )
            copy.start()
            stores.append(copy)
    for store in stores:
        store.wait()


def update(sizes, chunks, table, near_tiles, far_tiles, lefts, x_halves, got, before):
    order, rank = near_tiles.shape[1], far_tiles.shape[2]
    groups, row_group = sizes.groups, lefts.shape[0]
    count = len(chunks) * sizes.inner
    return pl.pallas_call(
        functools.partial(update_kernel, sizes, chunks),
        in_specs=[SMEM] + [HBM] * (4 + len(got) + len(before)),
        out_specs=[HBM, HBM],
        out_shape=out_shapes(sizes, near_tiles, far_tiles),
        scratch_shapes=[
            pltpu.VMEM((count, order, order), jnp.bfloat16),
            pltpu.VMEM((count, rank, order), jnp.bfloat16),
            pltpu.VMEM((row_group, order, order), jnp.bfloat16),
            pltpu.VMEM((count, 2 * rank, order), jnp.bfloat16),
            pltpu.VMEM((count, groups, sizes.quarter + sizes.far, order), jnp.bfloat16),
            pltpu.VMEM((count, order, order), jnp.bfloat16),
            pltpu.VMEM((count, rank, order), jnp.bfloat16),
            pltpu.VMEM((order, order), jnp.bfloat16),
            pltpu.VMEM((sizes.far_all, order), jnp.bfloat16),
            pltpu.SemaphoreType.DMA((count, groups + 5 + row_group)),
        ],
        input_output_aliases={5 + len(got) + k: k for k in range(len(before))},
        compiler_params=pltpu.CompilerParams(vmem_limit_bytes=WIDE_VMEM),
        cost_estimate=pl.CostEstimate(
            flops=UPDATE_FLOPS * len(chunks), bytes_accessed=0, transcendentals=0
        ),
    )(table, near_tiles, far_tiles, lefts, x_halves, *got, *before)


def shards(
    row_panel, col_near, col_far, near_tiles, near_rows, near_cols, far_tiles, far_rows, far_cols
):
    inner_size = lax.axis_size("inner")
    groups = lax.axis_size("gy") * lax.axis_size("core")
    per_bucket, quarter, order = col_near.shape
    row_group, shard = row_panel.shape[:2]
    far_pairs = jnp.swapaxes(col_far, 1, 2)
    far = -(-2 * col_far.shape[2] // FAR_ALIGN) * FAR_ALIGN
    sizes = Sizes(groups, inner_size, per_bucket, quarter, far, shard)

    def along(value, pairs):
        return lax.ppermute(value, "outer", pairs)

    rows = [row_panel]
    for k in range(1, inner_size):
        turn = [((i + k) % inner_size, i) for i in range(inner_size)]
        rows.append(lax.ppermute(row_panel, "inner", turn))

    table, own, send = first(
        sizes, near_cols, far_cols, near_rows, far_rows, col_near, far_pairs
    )
    held = {"own": own}
    held["pair"] = along(own, [(0, 1), (1, 0), (2, 3), (3, 2)])
    held["middle"] = along(own, [(1, 2), (2, 1)])
    held["cross"] = along(held["pair"], [(1, 2), (2, 1)])
    held["pass2"] = along(held["middle"], [(0, 1), (1, 0), (2, 3), (3, 2)])
    held["pass3"] = along(held["cross"], [(0, 1), (1, 0), (2, 3), (3, 2)])

    got = []
    for n in range(OUTER):
        if n > 0:
            after = [held["cross"]] if n == 2 else []
            send = pack(sizes, n, table, [held[name] for name in CHUNK_SOURCES[n]], after)
        got.append(lax.all_to_all(send, PLANE, split_axis=0, concat_axis=0, tiled=True))

    line = join_rows(rows, held["cross"])
    near1 = along(line, [(0, 1), (3, 2)])
    near2 = along(line, [(1, 2), (2, 1)])
    near3 = along(line, [(0, 2), (3, 1)])
    relayed = join_rows([line, near2, near3], held["pass3"])
    relayed = along(relayed, [(0, 1), (1, 0), (2, 3), (3, 2)])
    parts = [line, near1, near2, near3, relayed]
    lefts, x_halves = make_lefts(sizes, table, far_tiles, parts)
    tiles = (near_tiles, far_tiles, lefts, x_halves)
    outs = update(sizes, (0, 1, 2), table, *tiles, got[:3], ())
    outs = update(sizes, (3,), table, *tiles, got[3:], outs)
    return tuple(outs)


def solution(mesh):
    groups, dev_count = mesh.shape["grp"], mesh.shape["dev"]
    fine = Mesh(
        mesh.devices.reshape(groups // 2, 2, OUTER, dev_count // OUTER),
        ("gy", "core", "outer", "inner"),
    )
    grp, dev = ("gy", "core"), ("outer", "inner")
    every = grp + dev
    placed = (
        P(grp, dev, None),
        P(dev, grp, None),
        P(dev, None, grp, None),
        P(every, None, None),
        P(every, None),
        P(),
        P(every, None, None, None),
        P(every, None),
        P(),
    )
    return jax.shard_map(
        shards,
        mesh=fine,
        in_specs=placed,
        out_specs=(P(every, None, None), P(every, None, None)),
        check_vma=False,
    )
```

```python
import functools

import jax
import jax.numpy as jnp
from jax import lax
from jax.experimental import pallas as pl
from jax.experimental.pallas import tpu as pltpu
from jax.sharding import Mesh, PartitionSpec as P

OUTER = 4
PLANE = ("gy", "core", "inner")
ROW_ALIGN = 16
FAR_ALIGN = 8
LANES = 128
VMEM_LIMIT = 16 * 1024 * 1024
WIDE_VMEM = 60 * 1024 * 1024
LEFTS_VMEM = 24 * 1024 * 1024
HBM = pl.BlockSpec(memory_space=pltpu.HBM)
CHUNK_OWNER = ((0, 1, 2, 3), (1, 0, 3, 2), (2, 2, 1, 1), (3, 3, 0, 0))
CHUNK_SOURCE = ((0, 0, 0, 0), (0, 0, 0, 0), (1, 0, 0, 1), (1, 0, 0, 1))
CHUNK_SOURCES = (("own",), ("pair",), ("middle", "pass2"), ("cross", "pass3"))
PACK_FLOPS = (0, 5 * 10**9, 10**10, 10**10)
JOIN_FLOPS = 10**9
UPDATE_FLOPS = 3 * 10**9
VMEM = pl.BlockSpec(memory_space=pltpu.VMEM)
SMEM = pl.BlockSpec(memory_space=pltpu.SMEM)
KEPT = pl.BlockSpec(memory_space=pl.ANY)


class Sizes:
    def __init__(self, groups, inner, per_bucket, quarter, far, shard):
        self.groups, self.inner, self.per_bucket = groups, inner, per_bucket
        self.quarter, self.far, self.shard = quarter, far, shard
        self.far_all = -(-groups * far // LANES) * LANES
        self.slots = OUTER * inner
        self.wanted = groups * inner
        self.stride = 2 * self.wanted + 2
        self.near_rows_at = OUTER * self.stride
        self.far_rows_at = self.near_rows_at + self.slots
        self.inner_at = self.far_rows_at + self.slots
        self.outer_at = self.inner_at + 1
        self.table = self.outer_at + 1

    def owner_at(self, n):
        return n * self.stride + 2 * self.wanted

    def source_at(self, n):
        return n * self.stride + 2 * self.wanted + 1


def by_position(values, position):
    result = jnp.int32(values[0])
    for k in range(1, len(values)):
        result = jnp.where(position == k, jnp.int32(values[k]), result)
    return result


def fill_table(sizes, near_cols, far_cols, near_rows, far_rows, table):
    outer, inner = lax.axis_index("outer"), lax.axis_index("inner")
    table[sizes.inner_at] = inner
    table[sizes.outer_at] = outer
    for n in range(OUTER):
        owner = by_position(CHUNK_OWNER[n], outer)
        table[sizes.owner_at(n)] = owner
        table[sizes.source_at(n)] = by_position(CHUNK_SOURCE[n], outer)
        bucket = owner * sizes.inner + inner
        for g in range(sizes.groups):
            for x in range(sizes.inner):
                at = g * sizes.inner + x
                device = (g * OUTER + outer) * sizes.inner + x
                first = bucket * sizes.per_bucket
                table[n * sizes.stride + at] = near_cols[bucket, device] - first
                table[n * sizes.stride + sizes.wanted + at] = far_cols[bucket, device] - first
    for s in range(sizes.slots):
        table[sizes.near_rows_at + s] = near_rows[0, s]
        table[sizes.far_rows_at + s] = far_rows[0, s]


def pack_from(sizes, n, table, source, out, sent, sems):
    quarter, far = sizes.quarter, sizes.far
    far_at = sizes.per_bucket * quarter
    copies = []
    for at in range(sizes.wanted):
        near_pick = table[n * sizes.stride + at] * quarter
        out[at, 0:quarter, :] = source[pl.ds(pl.multiple_of(near_pick, ROW_ALIGN), quarter), :]
        far_pick = table[n * sizes.stride + sizes.wanted + at]
        picked = source[far_at : far_at + far, :]
        for j in range(1, sizes.per_bucket):
            other = source[far_at + j * far : far_at + (j + 1) * far, :]
            picked = jnp.where(far_pick == j, other, picked)
        out[at, quarter : quarter + far, :] = picked
        copies.append(pltpu.make_async_copy(out.at[at], sent.at[at], sems.at[at]))
        copies[at].start()
    for copy in copies:
        copy.wait()


def pack_scratch(sizes, order):
    return [
        pltpu.VMEM((sizes.wanted, sizes.quarter + sizes.far, order), jnp.bfloat16),
        pltpu.SemaphoreType.DMA((sizes.wanted,)),
    ]


def first_kernel(sizes, near_cols, far_cols, near_rows, far_rows, near, pairs, *outs):
    table, own, sent, out, sems = outs
    fill_table(sizes, near_cols, far_cols, near_rows, far_rows, table)
    quarter, far = sizes.quarter, sizes.far
    far_at = sizes.per_bucket * quarter
    for j in range(sizes.per_bucket):
        own[j * quarter : (j + 1) * quarter, :] = near[j]
        at = far_at + j * far
        count = 2 * pairs.shape[1]
        for r in range(pairs.shape[1]):
            own[at + 2 * r : at + 2 * r + 2, :] = pairs[j, r]
        if count < far:
            own[at + count : at + far, :] = jnp.zeros((far - count, own.shape[1]), own.dtype)
    pack_from(sizes, 0, table, own, out, sent, sems)


def send_shape(sizes, order):
    return jax.ShapeDtypeStruct((sizes.wanted, sizes.quarter + sizes.far, order), jnp.bfloat16)


def first(sizes, near_cols, far_cols, near_rows, far_rows, near, pairs):
    order = near.shape[2]
    rows = sizes.per_bucket * (sizes.quarter + sizes.far)
    return pl.pallas_call(
        functools.partial(first_kernel, sizes),
        in_specs=[SMEM] * 4 + [VMEM] * 2,
        out_specs=[SMEM, VMEM, HBM],
        scratch_shapes=pack_scratch(sizes, order),
        out_shape=[
            jax.ShapeDtypeStruct((sizes.table,), jnp.int32),
            jax.ShapeDtypeStruct((rows, order), jnp.bfloat16),
            send_shape(sizes, order),
        ],
        compiler_params=pltpu.CompilerParams(vmem_limit_bytes=WIDE_VMEM),
        cost_estimate=pl.CostEstimate(flops=0, bytes_accessed=0, transcendentals=0),
    )(near_cols.T, far_cols.T, near_rows, far_rows, near, pairs)


def pack_kernel(sizes, n, table, *refs):
    sources, (sent, out, sems, held, held_sem) = refs[: len(CHUNK_SOURCES[n])], refs[-5:]
    for k, source in enumerate(sources):

        @pl.when(table[sizes.source_at(n)] == k)
        def _(source=source):
            load = pltpu.make_async_copy(source, held, held_sem.at[0])
            load.start()
            load.wait()

    pack_from(sizes, n, table, held, out, sent, sems)


def pack(sizes, n, table, sources, after):
    order = sources[0].shape[1]
    return pl.pallas_call(
        functools.partial(pack_kernel, sizes, n),
        in_specs=[SMEM] + [HBM] * len(sources) + [KEPT] * len(after),
        out_specs=HBM,
        out_shape=send_shape(sizes, order),
        scratch_shapes=pack_scratch(sizes, order)
        + [pltpu.VMEM(sources[0].shape, jnp.bfloat16), pltpu.SemaphoreType.DMA((1,))],
        compiler_params=pltpu.CompilerParams(vmem_limit_bytes=WIDE_VMEM),
        cost_estimate=pl.CostEstimate(flops=PACK_FLOPS[n], bytes_accessed=0, transcendentals=0),
    )(table, *sources, *after)


def rows_kernel(after, *refs):
    for k, part in enumerate(refs[:-1]):
        refs[-1][k] = part[...]


def join_rows(parts, after):
    return pl.pallas_call(
        rows_kernel,
        in_specs=[KEPT] + [VMEM] * len(parts),
        out_specs=VMEM,
        out_shape=jax.ShapeDtypeStruct((len(parts),) + parts[0].shape, jnp.bfloat16),
        compiler_params=pltpu.CompilerParams(vmem_limit_bytes=VMEM_LIMIT),
        cost_estimate=pl.CostEstimate(flops=JOIN_FLOPS, bytes_accessed=0, transcendentals=0),
    )(after, *parts)


def lefts_kernel(sizes, table, far_tiles, line, near1, near2, near3, relayed, lefts, x_halves):
    shard = sizes.shard
    inner, outer = table[sizes.inner_at], table[sizes.outer_at]

    def place(z, part):
        for k in range(sizes.inner):
            x = lax.rem(inner + k, sizes.inner)
            at = pl.multiple_of((z * sizes.inner + x) * shard, ROW_ALIGN)
            for r in range(lefts.shape[0]):
                lefts[r, pl.ds(at, shard), :] = part[k, r]

    place(outer, line)
    amid = (outer == 1) | (outer == 2)
    for n, part in ((1, near1), (2, near2), (3, near3)):
        owner = table[sizes.owner_at(n)]
        pl.when(amid)(functools.partial(place, owner, part))
        pl.when(jnp.logical_not(amid))(functools.partial(place, owner, relayed.at[n - 1]))
    rank = far_tiles.shape[2]
    bases = jnp.concatenate([far_tiles[s, 0] for s in range(sizes.slots)], axis=0)
    for r in range(lefts.shape[0]):
        x_trans = jnp.dot(bases, lefts[r], preferred_element_type=jnp.float32)
        for s in range(sizes.slots):

            @pl.when(table[sizes.far_rows_at + s] == r)
            def _(s=s, own=x_trans[s * rank : (s + 1) * rank]):
                x_halves[s] = halves(own)


def make_lefts(sizes, table, far_tiles, parts):
    row_group, _, order = parts[0].shape[1:]
    rank = far_tiles.shape[2]
    return pl.pallas_call(
        functools.partial(lefts_kernel, sizes),
        in_specs=[SMEM, VMEM] + [VMEM] * len(parts),
        out_specs=[VMEM, VMEM],
        out_shape=[
            jax.ShapeDtypeStruct((row_group, order, order), jnp.bfloat16),
            jax.ShapeDtypeStruct((sizes.slots, 2 * rank, order), jnp.bfloat16),
        ],
        compiler_params=pltpu.CompilerParams(vmem_limit_bytes=LEFTS_VMEM),
        cost_estimate=pl.CostEstimate(flops=0, bytes_accessed=0, transcendentals=0),
    )(table, far_tiles, *parts)


def halves(value):
    high = value.astype(jnp.bfloat16)
    low = (value - high.astype(jnp.float32)).astype(jnp.bfloat16)
    return jnp.concatenate([high, low], axis=0)


ACROSS = (((1,), (1,)), ((), ()))


def near_update(tile, left, panel):
    product = lax.dot_general(left, panel, ACROSS, preferred_element_type=jnp.float32)
    return (tile.astype(jnp.float32) - product).astype(jnp.bfloat16)


def far_update(tile, x_halves, pairs):
    rank = tile.shape[0]
    both = lax.dot_general(x_halves, pairs, ACROSS, preferred_element_type=jnp.float32)
    small = both[:rank] + both[rank:]
    turned = pltpu.roll(small, small.shape[1] - 1, 1)
    lane = lax.broadcasted_iota(jnp.int32, turned.shape, 1)
    turned = jnp.where(lane % 2 == 0, turned, 0.0)
    change = jnp.dot(halves(turned), pairs, preferred_element_type=jnp.float32)
    return (tile.astype(jnp.float32) - (change[:rank] + change[rank:])).astype(jnp.bfloat16)


def clear_rest(sizes, factors):
    filled = sizes.groups * sizes.far
    if filled < sizes.far_all:
        factors[filled:, :] = jnp.zeros_like(factors[filled:, :])


def take_part(sizes, g, part, panel, factors):
    quarter, far = sizes.quarter, sizes.far
    panel[g * quarter : (g + 1) * quarter, :] = part[0:quarter, :]
    factors[g * far : (g + 1) * far, :] = part[quarter : quarter + far, :]


def out_shapes(sizes, near_tiles, far_tiles):
    order, rank = near_tiles.shape[1], far_tiles.shape[2]
    return [
        jax.ShapeDtypeStruct((sizes.slots, order, order), jnp.bfloat16),
        jax.ShapeDtypeStruct((sizes.slots, rank, order), jnp.bfloat16),
    ]


def update_kernel(sizes, chunks, table, near_tiles, far_tiles, lefts, x_halves, *refs):
    got, (near_out, far_out) = refs[: len(chunks)], refs[-12:-10]
    tile, far_tile, left, x_half, parts, near_done, far_done, panel, factors, sems = refs[-10:]
    left_loads = [
        pltpu.make_async_copy(lefts.at[r], left.at[r], sems.at[0, sizes.groups + 5 + r])
        for r in range(left.shape[0])
    ]
    slots, loads = [], []
    for k, n in enumerate(chunks):
        for x in range(sizes.inner):
            at = len(slots)
            slot = table[sizes.owner_at(n)] * sizes.inner + x
            pairs = [(got[k].at[g * sizes.inner + x], parts.at[at, g]) for g in range(sizes.groups)]
            pairs += [
                (near_tiles.at[slot], tile.at[at]),
                (x_halves.at[slot], x_half.at[at]),
                (far_tiles.at[slot, 1], far_tile.at[at]),
            ]
            slots.append(slot)
            loads.append(
                [
                    pltpu.make_async_copy(source, to, sems.at[at, j])
                    for j, (source, to) in enumerate(pairs)
                ]
            )
    for load in loads[0] + left_loads + sum(loads[1:], []):
        load.start()
    clear_rest(sizes, factors)
    for load in left_loads:
        load.wait()
    stores = []
    for at, slot in enumerate(slots):
        for load in loads[at]:
            load.wait()
        for g in range(sizes.groups):
            take_part(sizes, g, parts.at[at, g], panel, factors)
        own_left = left[table[sizes.near_rows_at + slot]]
        near_done[at] = near_update(tile[at], own_left, panel[...])
        far_done[at] = far_update(far_tile[at], x_half[at], factors[...])
        for j, (done, out) in enumerate(((near_done, near_out), (far_done, far_out))):
            copy = pltpu.make_async_copy(
                done.at[at], out.at[slot], sems.at[at, sizes.groups + 3 + j]
            )
            copy.start()
            stores.append(copy)
    for store in stores:
        store.wait()


def update(sizes, chunks, table, near_tiles, far_tiles, lefts, x_halves, got, before):
    order, rank = near_tiles.shape[1], far_tiles.shape[2]
    groups, row_group = sizes.groups, lefts.shape[0]
    count = len(chunks) * sizes.inner
    return pl.pallas_call(
        functools.partial(update_kernel, sizes, chunks),
        in_specs=[SMEM] + [HBM] * (4 + len(got) + len(before)),
        out_specs=[HBM, HBM],
        out_shape=out_shapes(sizes, near_tiles, far_tiles),
        scratch_shapes=[
            pltpu.VMEM((count, order, order), jnp.bfloat16),
            pltpu.VMEM((count, rank, order), jnp.bfloat16),
            pltpu.VMEM((row_group, order, order), jnp.bfloat16),
            pltpu.VMEM((count, 2 * rank, order), jnp.bfloat16),
            pltpu.VMEM((count, groups, sizes.quarter + sizes.far, order), jnp.bfloat16),
            pltpu.VMEM((count, order, order), jnp.bfloat16),
            pltpu.VMEM((count, rank, order), jnp.bfloat16),
            pltpu.VMEM((order, order), jnp.bfloat16),
            pltpu.VMEM((sizes.far_all, order), jnp.bfloat16),
            pltpu.SemaphoreType.DMA((count, groups + 5 + row_group)),
        ],
        input_output_aliases={5 + len(got) + k: k for k in range(len(before))},
        compiler_params=pltpu.CompilerParams(vmem_limit_bytes=WIDE_VMEM),
        cost_estimate=pl.CostEstimate(
            flops=UPDATE_FLOPS * len(chunks), bytes_accessed=0, transcendentals=0
        ),
    )(table, near_tiles, far_tiles, lefts, x_halves, *got, *before)


def shards(
    row_panel, col_near, col_far, near_tiles, near_rows, near_cols, far_tiles, far_rows, far_cols
):
    inner_size = lax.axis_size("inner")
    groups = lax.axis_size("gy") * lax.axis_size("core")
    per_bucket, quarter, order = col_near.shape
    row_group, shard = row_panel.shape[:2]
    far_pairs = jnp.swapaxes(col_far, 1, 2)
    far = -(-2 * col_far.shape[2] // FAR_ALIGN) * FAR_ALIGN
    sizes = Sizes(groups, inner_size, per_bucket, quarter, far, shard)

    def along(value, pairs):
        return lax.ppermute(value, "outer", pairs)

    rows = [row_panel]
    for k in range(1, inner_size):
        turn = [((i + k) % inner_size, i) for i in range(inner_size)]
        rows.append(lax.ppermute(row_panel, "inner", turn))

    table, own, send = first(
        sizes, near_cols, far_cols, near_rows, far_rows, col_near, far_pairs
    )
    held = {"own": own}
    held["pair"] = along(own, [(0, 1), (1, 0), (2, 3), (3, 2)])
    held["middle"] = along(own, [(1, 2), (2, 1)])
    held["cross"] = along(held["pair"], [(1, 2), (2, 1)])
    held["pass2"] = along(held["middle"], [(0, 1), (1, 0), (2, 3), (3, 2)])
    held["pass3"] = along(held["cross"], [(0, 1), (1, 0), (2, 3), (3, 2)])

    got = []
    for n in range(OUTER):
        if n > 0:
            after = [held["cross"]] if n == 2 else []
            send = pack(sizes, n, table, [held[name] for name in CHUNK_SOURCES[n]], after)
        got.append(lax.all_to_all(send, PLANE, split_axis=0, concat_axis=0, tiled=True))

    line = join_rows(rows, held["cross"])
    near1 = along(line, [(0, 1), (3, 2)])
    near2 = along(line, [(1, 2), (2, 1)])
    near3 = along(line, [(0, 2), (3, 1)])
    relayed = join_rows([line, near2, near3], held["pass3"])
    relayed = along(relayed, [(0, 1), (1, 0), (2, 3), (3, 2)])
    parts = [line, near1, near2, near3, relayed]
    lefts, x_halves = make_lefts(sizes, table, far_tiles, parts)
    tiles = (near_tiles, far_tiles, lefts, x_halves)
    outs = update(sizes, (0, 1, 2), table, *tiles, got[:3], ())
    outs = update(sizes, (3,), table, *tiles, got[3:], outs)
    return tuple(outs)


def solution(mesh):
    groups, dev_count = mesh.shape["grp"], mesh.shape["dev"]
    fine = Mesh(
        mesh.devices.reshape(groups // 2, 2, OUTER, dev_count // OUTER),
        ("gy", "core", "outer", "inner"),
    )
    grp, dev = ("gy", "core"), ("outer", "inner")
    every = grp + dev
    placed = (
        P(grp, dev, None),
        P(dev, grp, None),
        P(dev, None, grp, None),
        P(every, None, None),
        P(every, None),
        P(),
        P(every, None, None, None),
        P(every, None),
        P(),
    )
    return jax.shard_map(
        shards,
        mesh=fine,
        in_specs=placed,
        out_specs=(P(every, None, None), P(every, None, None)),
        check_vma=False,
    )
```

```python
import functools

import jax
import jax.numpy as jnp
from jax import lax
from jax.experimental import pallas as pl
from jax.experimental.pallas import tpu as pltpu
from jax.sharding import Mesh, PartitionSpec as P

OUTER = 4
PLANE = ("gy", "core", "inner")
ROW_ALIGN = 16
FAR_ALIGN = 8
LANES = 128
VMEM_LIMIT = 16 * 1024 * 1024
WIDE_VMEM = 60 * 1024 * 1024
LEFTS_VMEM = 24 * 1024 * 1024
HBM = pl.BlockSpec(memory_space=pltpu.HBM)
CHUNK_OWNER = ((0, 1, 2, 3), (1, 0, 3, 2), (2, 2, 1, 1), (3, 3, 0, 0))
CHUNK_SOURCE = ((0, 0, 0, 0), (0, 0, 0, 0), (1, 0, 0, 1), (1, 0, 0, 1))
CHUNK_SOURCES = (("own",), ("pair",), ("middle", "pass2"), ("cross", "pass3"))
PACK_FLOPS = (0, 2 * 10**9, 10**10, 10**10)
JOIN_FLOPS = 10**9
UPDATE_FLOPS = 3 * 10**9
VMEM = pl.BlockSpec(memory_space=pltpu.VMEM)
SMEM = pl.BlockSpec(memory_space=pltpu.SMEM)
KEPT = pl.BlockSpec(memory_space=pl.ANY)


class Sizes:
    def __init__(self, groups, inner, per_bucket, quarter, far, shard):
        self.groups, self.inner, self.per_bucket = groups, inner, per_bucket
        self.quarter, self.far, self.shard = quarter, far, shard
        self.far_all = -(-groups * far // LANES) * LANES
        self.slots = OUTER * inner
        self.wanted = groups * inner
        self.stride = 2 * self.wanted + 2
        self.near_rows_at = OUTER * self.stride
        self.far_rows_at = self.near_rows_at + self.slots
        self.inner_at = self.far_rows_at + self.slots
        self.outer_at = self.inner_at + 1
        self.table = self.outer_at + 1

    def owner_at(self, n):
        return n * self.stride + 2 * self.wanted

    def source_at(self, n):
        return n * self.stride + 2 * self.wanted + 1


def by_position(values, position):
    result = jnp.int32(values[0])
    for k in range(1, len(values)):
        result = jnp.where(position == k, jnp.int32(values[k]), result)
    return result


def fill_table(sizes, near_cols, far_cols, near_rows, far_rows, table):
    outer, inner = lax.axis_index("outer"), lax.axis_index("inner")
    table[sizes.inner_at] = inner
    table[sizes.outer_at] = outer
    for n in range(OUTER):
        owner = by_position(CHUNK_OWNER[n], outer)
        table[sizes.owner_at(n)] = owner
        table[sizes.source_at(n)] = by_position(CHUNK_SOURCE[n], outer)
        bucket = owner * sizes.inner + inner
        for g in range(sizes.groups):
            for x in range(sizes.inner):
                at = g * sizes.inner + x
                device = (g * OUTER + outer) * sizes.inner + x
                first = bucket * sizes.per_bucket
                table[n * sizes.stride + at] = near_cols[bucket, device] - first
                table[n * sizes.stride + sizes.wanted + at] = far_cols[bucket, device] - first
    for s in range(sizes.slots):
        table[sizes.near_rows_at + s] = near_rows[0, s]
        table[sizes.far_rows_at + s] = far_rows[0, s]


def pack_from(sizes, n, table, source, out, sent, sems):
    quarter, far = sizes.quarter, sizes.far
    far_at = sizes.per_bucket * quarter
    copies = []
    for at in range(sizes.wanted):
        near_pick = table[n * sizes.stride + at] * quarter
        out[at, 0:quarter, :] = source[pl.ds(pl.multiple_of(near_pick, ROW_ALIGN), quarter), :]
        far_pick = table[n * sizes.stride + sizes.wanted + at]
        picked = source[far_at : far_at + far, :]
        for j in range(1, sizes.per_bucket):
            other = source[far_at + j * far : far_at + (j + 1) * far, :]
            picked = jnp.where(far_pick == j, other, picked)
        out[at, quarter : quarter + far, :] = picked
        copies.append(pltpu.make_async_copy(out.at[at], sent.at[at], sems.at[at]))
        copies[at].start()
    for copy in copies:
        copy.wait()


def pack_scratch(sizes, order):
    return [
        pltpu.VMEM((sizes.wanted, sizes.quarter + sizes.far, order), jnp.bfloat16),
        pltpu.SemaphoreType.DMA((sizes.wanted,)),
    ]


def first_kernel(sizes, near_cols, far_cols, near_rows, far_rows, near, pairs, *outs):
    table, own, sent, out, sems = outs
    fill_table(sizes, near_cols, far_cols, near_rows, far_rows, table)
    quarter, far = sizes.quarter, sizes.far
    far_at = sizes.per_bucket * quarter
    for j in range(sizes.per_bucket):
        own[j * quarter : (j + 1) * quarter, :] = near[j]
        at = far_at + j * far
        count = 2 * pairs.shape[1]
        for r in range(pairs.shape[1]):
            own[at + 2 * r : at + 2 * r + 2, :] = pairs[j, r]
        if count < far:
            own[at + count : at + far, :] = jnp.zeros((far - count, own.shape[1]), own.dtype)
    pack_from(sizes, 0, table, own, out, sent, sems)


def send_shape(sizes, order):
    return jax.ShapeDtypeStruct((sizes.wanted, sizes.quarter + sizes.far, order), jnp.bfloat16)


def first(sizes, near_cols, far_cols, near_rows, far_rows, near, pairs):
    order = near.shape[2]
    rows = sizes.per_bucket * (sizes.quarter + sizes.far)
    return pl.pallas_call(
        functools.partial(first_kernel, sizes),
        in_specs=[SMEM] * 4 + [VMEM] * 2,
        out_specs=[SMEM, VMEM, HBM],
        scratch_shapes=pack_scratch(sizes, order),
        out_shape=[
            jax.ShapeDtypeStruct((sizes.table,), jnp.int32),
            jax.ShapeDtypeStruct((rows, order), jnp.bfloat16),
            send_shape(sizes, order),
        ],
        compiler_params=pltpu.CompilerParams(vmem_limit_bytes=WIDE_VMEM),
        cost_estimate=pl.CostEstimate(flops=0, bytes_accessed=0, transcendentals=0),
    )(near_cols.T, far_cols.T, near_rows, far_rows, near, pairs)


def pack_kernel(sizes, n, table, *refs):
    sources, (sent, out, sems, held, held_sem) = refs[: len(CHUNK_SOURCES[n])], refs[-5:]
    for k, source in enumerate(sources):

        @pl.when(table[sizes.source_at(n)] == k)
        def _(source=source):
            load = pltpu.make_async_copy(source, held, held_sem.at[0])
            load.start()
            load.wait()

    pack_from(sizes, n, table, held, out, sent, sems)


def pack(sizes, n, table, sources, after):
    order = sources[0].shape[1]
    return pl.pallas_call(
        functools.partial(pack_kernel, sizes, n),
        in_specs=[SMEM] + [HBM] * len(sources) + [KEPT] * len(after),
        out_specs=HBM,
        out_shape=send_shape(sizes, order),
        scratch_shapes=pack_scratch(sizes, order)
        + [pltpu.VMEM(sources[0].shape, jnp.bfloat16), pltpu.SemaphoreType.DMA((1,))],
        compiler_params=pltpu.CompilerParams(vmem_limit_bytes=WIDE_VMEM),
        cost_estimate=pl.CostEstimate(flops=PACK_FLOPS[n], bytes_accessed=0, transcendentals=0),
    )(table, *sources, *after)


def rows_kernel(after, *refs):
    for k, part in enumerate(refs[:-1]):
        refs[-1][k] = part[...]


def join_rows(parts, after):
    return pl.pallas_call(
        rows_kernel,
        in_specs=[KEPT] + [VMEM] * len(parts),
        out_specs=VMEM,
        out_shape=jax.ShapeDtypeStruct((len(parts),) + parts[0].shape, jnp.bfloat16),
        compiler_params=pltpu.CompilerParams(vmem_limit_bytes=VMEM_LIMIT),
        cost_estimate=pl.CostEstimate(flops=JOIN_FLOPS, bytes_accessed=0, transcendentals=0),
    )(after, *parts)


def lefts_kernel(sizes, table, far_tiles, line, near1, near2, near3, relayed, lefts, x_halves):
    shard = sizes.shard
    inner, outer = table[sizes.inner_at], table[sizes.outer_at]

    def place(z, part):
        for k in range(sizes.inner):
            x = lax.rem(inner + k, sizes.inner)
            at = pl.multiple_of((z * sizes.inner + x) * shard, ROW_ALIGN)
            for r in range(lefts.shape[0]):
                lefts[r, pl.ds(at, shard), :] = part[k, r]

    place(outer, line)
    amid = (outer == 1) | (outer == 2)
    for n, part in ((1, near1), (2, near2), (3, near3)):
        owner = table[sizes.owner_at(n)]
        pl.when(amid)(functools.partial(place, owner, part))
        pl.when(jnp.logical_not(amid))(functools.partial(place, owner, relayed.at[n - 1]))
    rank = far_tiles.shape[2]
    bases = jnp.concatenate([far_tiles[s, 0] for s in range(sizes.slots)], axis=0)
    for r in range(lefts.shape[0]):
        x_trans = jnp.dot(bases, lefts[r], preferred_element_type=jnp.float32)
        for s in range(sizes.slots):

            @pl.when(table[sizes.far_rows_at + s] == r)
            def _(s=s, own=x_trans[s * rank : (s + 1) * rank]):
                x_halves[s] = halves(own)


def make_lefts(sizes, table, far_tiles, parts):
    row_group, _, order = parts[0].shape[1:]
    rank = far_tiles.shape[2]
    return pl.pallas_call(
        functools.partial(lefts_kernel, sizes),
        in_specs=[SMEM, VMEM] + [VMEM] * len(parts),
        out_specs=[VMEM, VMEM],
        out_shape=[
            jax.ShapeDtypeStruct((row_group, order, order), jnp.bfloat16),
            jax.ShapeDtypeStruct((sizes.slots, 2 * rank, order), jnp.bfloat16),
        ],
        compiler_params=pltpu.CompilerParams(vmem_limit_bytes=LEFTS_VMEM),
        cost_estimate=pl.CostEstimate(flops=0, bytes_accessed=0, transcendentals=0),
    )(table, far_tiles, *parts)


def halves(value):
    high = value.astype(jnp.bfloat16)
    low = (value - high.astype(jnp.float32)).astype(jnp.bfloat16)
    return jnp.concatenate([high, low], axis=0)


ACROSS = (((1,), (1,)), ((), ()))


def near_update(tile, left, panel):
    product = lax.dot_general(left, panel, ACROSS, preferred_element_type=jnp.float32)
    return (tile.astype(jnp.float32) - product).astype(jnp.bfloat16)


def far_update(tile, x_halves, pairs):
    rank = tile.shape[0]
    both = lax.dot_general(x_halves, pairs, ACROSS, preferred_element_type=jnp.float32)
    small = both[:rank] + both[rank:]
    turned = pltpu.roll(small, small.shape[1] - 1, 1)
    lane = lax.broadcasted_iota(jnp.int32, turned.shape, 1)
    turned = jnp.where(lane % 2 == 0, turned, 0.0)
    change = jnp.dot(halves(turned), pairs, preferred_element_type=jnp.float32)
    return (tile.astype(jnp.float32) - (change[:rank] + change[rank:])).astype(jnp.bfloat16)


def clear_rest(sizes, factors):
    filled = sizes.groups * sizes.far
    if filled < sizes.far_all:
        factors[filled:, :] = jnp.zeros_like(factors[filled:, :])


def take_part(sizes, g, part, panel, factors):
    quarter, far = sizes.quarter, sizes.far
    panel[g * quarter : (g + 1) * quarter, :] = part[0:quarter, :]
    factors[g * far : (g + 1) * far, :] = part[quarter : quarter + far, :]


def out_shapes(sizes, near_tiles, far_tiles):
    order, rank = near_tiles.shape[1], far_tiles.shape[2]
    return [
        jax.ShapeDtypeStruct((sizes.slots, order, order), jnp.bfloat16),
        jax.ShapeDtypeStruct((sizes.slots, rank, order), jnp.bfloat16),
    ]


def update_kernel(sizes, chunks, table, near_tiles, far_tiles, lefts, x_halves, *refs):
    got, (near_out, far_out) = refs[: len(chunks)], refs[-12:-10]
    tile, far_tile, left, x_half, parts, near_done, far_done, panel, factors, sems = refs[-10:]
    left_loads = [
        pltpu.make_async_copy(lefts.at[r], left.at[r], sems.at[0, sizes.groups + 6 + r])
        for r in range(left.shape[0])
    ]
    slots, loads = [], []
    for k, n in enumerate(chunks):
        for x in range(sizes.inner):
            at = len(slots)
            slot = table[sizes.owner_at(n)] * sizes.inner + x
            pairs = [(got[k].at[g * sizes.inner + x], parts.at[at, g]) for g in range(sizes.groups)]
            pairs += [
                (near_tiles.at[slot], tile.at[at]),
                (x_halves.at[slot], x_half.at[at]),
                (far_tiles.at[slot, 1], far_tile.at[at]),
            ]
            slots.append(slot)
            loads.append(
                [
                    pltpu.make_async_copy(source, to, sems.at[at, j])
                    for j, (source, to) in enumerate(pairs)
                ]
            )
    for load in loads[0] + left_loads + sum(loads[1:], []):
        load.start()
    clear_rest(sizes, factors)
    for load in left_loads:
        load.wait()
    stores = []
    for at, slot in enumerate(slots):
        for load in loads[at]:
            load.wait()
        for g in range(sizes.groups):
            take_part(sizes, g, parts.at[at, g], panel, factors)
        own_row = table[sizes.near_rows_at + slot]
        far_done[at] = far_update(far_tile[at], x_half[at], factors[...])
        store_at = sizes.groups + 3
        stores.append(
            pltpu.make_async_copy(far_done.at[at], far_out.at[slot], sems.at[at, store_at])
        )
        stores[-1].start()
        half = tile.shape[1] // 2
        for h in range(2):
            rows = pl.ds(h * half, half)
            near_done[at, rows, :] = near_update(tile[at, rows, :], left[own_row, rows, :], panel[...])
            stores.append(
                pltpu.make_async_copy(
                    near_done.at[at, rows], near_out.at[slot, rows], sems.at[at, store_at + 1 + h]
                )
            )
            stores[-1].start()
    for store in stores:
        store.wait()


def update(sizes, chunks, table, near_tiles, far_tiles, lefts, x_halves, got, before):
    order, rank = near_tiles.shape[1], far_tiles.shape[2]
    groups, row_group = sizes.groups, lefts.shape[0]
    count = len(chunks) * sizes.inner
    return pl.pallas_call(
        functools.partial(update_kernel, sizes, chunks),
        in_specs=[SMEM] + [HBM] * (4 + len(got) + len(before)),
        out_specs=[HBM, HBM],
        out_shape=out_shapes(sizes, near_tiles, far_tiles),
        scratch_shapes=[
            pltpu.VMEM((count, order, order), jnp.bfloat16),
            pltpu.VMEM((count, rank, order), jnp.bfloat16),
            pltpu.VMEM((row_group, order, order), jnp.bfloat16),
            pltpu.VMEM((count, 2 * rank, order), jnp.bfloat16),
            pltpu.VMEM((count, groups, sizes.quarter + sizes.far, order), jnp.bfloat16),
            pltpu.VMEM((count, order, order), jnp.bfloat16),
            pltpu.VMEM((count, rank, order), jnp.bfloat16),
            pltpu.VMEM((order, order), jnp.bfloat16),
            pltpu.VMEM((sizes.far_all, order), jnp.bfloat16),
            pltpu.SemaphoreType.DMA((count, groups + 6 + row_group)),
        ],
        input_output_aliases={5 + len(got) + k: k for k in range(len(before))},
        compiler_params=pltpu.CompilerParams(vmem_limit_bytes=WIDE_VMEM),
        cost_estimate=pl.CostEstimate(
            flops=UPDATE_FLOPS * len(chunks), bytes_accessed=0, transcendentals=0
        ),
    )(table, near_tiles, far_tiles, lefts, x_halves, *got, *before)


def shards(
    row_panel, col_near, col_far, near_tiles, near_rows, near_cols, far_tiles, far_rows, far_cols
):
    inner_size = lax.axis_size("inner")
    groups = lax.axis_size("gy") * lax.axis_size("core")
    per_bucket, quarter, order = col_near.shape
    row_group, shard = row_panel.shape[:2]
    far_pairs = jnp.swapaxes(col_far, 1, 2)
    far = -(-2 * col_far.shape[2] // FAR_ALIGN) * FAR_ALIGN
    sizes = Sizes(groups, inner_size, per_bucket, quarter, far, shard)

    def along(value, pairs):
        return lax.ppermute(value, "outer", pairs)

    rows = [row_panel]
    for k in range(1, inner_size):
        turn = [((i + k) % inner_size, i) for i in range(inner_size)]
        rows.append(lax.ppermute(row_panel, "inner", turn))

    table, own, send = first(
        sizes, near_cols, far_cols, near_rows, far_rows, col_near, far_pairs
    )
    held = {"own": own}
    held["pair"] = along(own, [(0, 1), (1, 0), (2, 3), (3, 2)])
    held["middle"] = along(own, [(1, 2), (2, 1)])
    held["cross"] = along(held["pair"], [(1, 2), (2, 1)])
    held["pass2"] = along(held["middle"], [(0, 1), (1, 0), (2, 3), (3, 2)])
    held["pass3"] = along(held["cross"], [(0, 1), (1, 0), (2, 3), (3, 2)])

    got = []
    for n in range(OUTER):
        if n > 0:
            after = [held["cross"]] if n == 2 else []
            send = pack(sizes, n, table, [held[name] for name in CHUNK_SOURCES[n]], after)
        got.append(lax.all_to_all(send, PLANE, split_axis=0, concat_axis=0, tiled=True))

    line = join_rows(rows, held["cross"])
    near1 = along(line, [(0, 1), (3, 2)])
    near2 = along(line, [(1, 2), (2, 1)])
    near3 = along(line, [(0, 2), (3, 1)])
    relayed = join_rows([line, near2, near3], held["pass3"])
    relayed = along(relayed, [(0, 1), (1, 0), (2, 3), (3, 2)])
    parts = [line, near1, near2, near3, relayed]
    lefts, x_halves = make_lefts(sizes, table, far_tiles, parts)
    tiles = (near_tiles, far_tiles, lefts, x_halves)
    outs = update(sizes, (0, 1, 2), table, *tiles, got[:3], ())
    outs = update(sizes, (3,), table, *tiles, got[3:], outs)
    return tuple(outs)


def solution(mesh):
    groups, dev_count = mesh.shape["grp"], mesh.shape["dev"]
    fine = Mesh(
        mesh.devices.reshape(groups // 2, 2, OUTER, dev_count // OUTER),
        ("gy", "core", "outer", "inner"),
    )
    grp, dev = ("gy", "core"), ("outer", "inner")
    every = grp + dev
    placed = (
        P(grp, dev, None),
        P(dev, grp, None),
        P(dev, None, grp, None),
        P(every, None, None),
        P(every, None),
        P(),
        P(every, None, None, None),
        P(every, None),
        P(),
    )
    return jax.shard_map(
        shards,
        mesh=fine,
        in_specs=placed,
        out_specs=(P(every, None, None), P(every, None, None)),
        check_vma=False,
    )
```

```python
import functools

import jax
import jax.numpy as jnp
from jax import lax
from jax.experimental import pallas as pl
from jax.experimental.pallas import tpu as pltpu
from jax.sharding import Mesh, PartitionSpec as P

OUTER = 4
PLANE = ("gy", "core", "inner")
ROW_ALIGN = 16
FAR_ALIGN = 8
LANES = 128
VMEM_LIMIT = 16 * 1024 * 1024
WIDE_VMEM = 63 * 1024 * 1024
HBM = pl.BlockSpec(memory_space=pltpu.HBM)
CHUNK_OWNER = ((0, 1, 2, 3), (1, 0, 3, 2), (2, 2, 1, 1), (3, 3, 0, 0))
CHUNK_SOURCE = ((0, 0, 0, 0), (0, 0, 0, 0), (1, 0, 0, 1), (1, 0, 0, 1))
CHUNK_SOURCES = (("own",), ("pair",), ("middle", "pass2"), ("cross", "pass3"))
PACK_FLOPS = (0, 2 * 10**9, 10**10, 10**10)
JOIN_FLOPS = 10**9
UPDATE_FLOPS = 3 * 10**9
VMEM = pl.BlockSpec(memory_space=pltpu.VMEM)
SMEM = pl.BlockSpec(memory_space=pltpu.SMEM)
KEPT = pl.BlockSpec(memory_space=pl.ANY)


class Sizes:
    def __init__(self, groups, inner, per_bucket, quarter, far, shard):
        self.groups, self.inner, self.per_bucket = groups, inner, per_bucket
        self.quarter, self.far, self.shard = quarter, far, shard
        self.far_all = -(-groups * far // LANES) * LANES
        self.slots = OUTER * inner
        self.wanted = groups * inner
        self.stride = 2 * self.wanted + 2
        self.near_rows_at = OUTER * self.stride
        self.far_rows_at = self.near_rows_at + self.slots
        self.inner_at = self.far_rows_at + self.slots
        self.outer_at = self.inner_at + 1
        self.table = self.outer_at + 1

    def owner_at(self, n):
        return n * self.stride + 2 * self.wanted

    def source_at(self, n):
        return n * self.stride + 2 * self.wanted + 1


def by_position(values, position):
    result = jnp.int32(values[0])
    for k in range(1, len(values)):
        result = jnp.where(position == k, jnp.int32(values[k]), result)
    return result


def fill_table(sizes, near_cols, far_cols, near_rows, far_rows, table):
    outer, inner = lax.axis_index("outer"), lax.axis_index("inner")
    table[sizes.inner_at] = inner
    table[sizes.outer_at] = outer
    for n in range(OUTER):
        owner = by_position(CHUNK_OWNER[n], outer)
        table[sizes.owner_at(n)] = owner
        table[sizes.source_at(n)] = by_position(CHUNK_SOURCE[n], outer)
        bucket = owner * sizes.inner + inner
        for g in range(sizes.groups):
            for x in range(sizes.inner):
                at = g * sizes.inner + x
                device = (g * OUTER + outer) * sizes.inner + x
                first = bucket * sizes.per_bucket
                table[n * sizes.stride + at] = near_cols[bucket, device] - first
                table[n * sizes.stride + sizes.wanted + at] = far_cols[bucket, device] - first
    for s in range(sizes.slots):
        table[sizes.near_rows_at + s] = near_rows[0, s]
        table[sizes.far_rows_at + s] = far_rows[0, s]


def pack_from(sizes, n, table, source, out, sent, sems):
    quarter, far = sizes.quarter, sizes.far
    far_at = sizes.per_bucket * quarter
    copies = []
    for at in range(sizes.wanted):
        near_pick = table[n * sizes.stride + at] * quarter
        out[at, 0:quarter, :] = source[pl.ds(pl.multiple_of(near_pick, ROW_ALIGN), quarter), :]
        far_pick = table[n * sizes.stride + sizes.wanted + at]
        picked = source[far_at : far_at + far, :]
        for j in range(1, sizes.per_bucket):
            other = source[far_at + j * far : far_at + (j + 1) * far, :]
            picked = jnp.where(far_pick == j, other, picked)
        out[at, quarter : quarter + far, :] = picked
        copies.append(pltpu.make_async_copy(out.at[at], sent.at[at], sems.at[at]))
        copies[at].start()
    for copy in copies:
        copy.wait()


def pack_scratch(sizes, order):
    return [
        pltpu.VMEM((sizes.wanted, sizes.quarter + sizes.far, order), jnp.bfloat16),
        pltpu.SemaphoreType.DMA((sizes.wanted,)),
    ]


def first_kernel(sizes, near_cols, far_cols, near_rows, far_rows, near, pairs, *outs):
    table, own, sent, out, sems = outs
    fill_table(sizes, near_cols, far_cols, near_rows, far_rows, table)
    quarter, far = sizes.quarter, sizes.far
    far_at = sizes.per_bucket * quarter
    for j in range(sizes.per_bucket):
        own[j * quarter : (j + 1) * quarter, :] = near[j]
        at = far_at + j * far
        count = 2 * pairs.shape[1]
        for r in range(pairs.shape[1]):
            own[at + 2 * r : at + 2 * r + 2, :] = pairs[j, r]
        if count < far:
            own[at + count : at + far, :] = jnp.zeros((far - count, own.shape[1]), own.dtype)
    pack_from(sizes, 0, table, own, out, sent, sems)


def send_shape(sizes, order):
    return jax.ShapeDtypeStruct((sizes.wanted, sizes.quarter + sizes.far, order), jnp.bfloat16)


def first(sizes, near_cols, far_cols, near_rows, far_rows, near, pairs):
    order = near.shape[2]
    rows = sizes.per_bucket * (sizes.quarter + sizes.far)
    return pl.pallas_call(
        functools.partial(first_kernel, sizes),
        in_specs=[SMEM] * 4 + [VMEM] * 2,
        out_specs=[SMEM, VMEM, HBM],
        scratch_shapes=pack_scratch(sizes, order),
        out_shape=[
            jax.ShapeDtypeStruct((sizes.table,), jnp.int32),
            jax.ShapeDtypeStruct((rows, order), jnp.bfloat16),
            send_shape(sizes, order),
        ],
        compiler_params=pltpu.CompilerParams(vmem_limit_bytes=WIDE_VMEM),
        cost_estimate=pl.CostEstimate(flops=0, bytes_accessed=0, transcendentals=0),
    )(near_cols.T, far_cols.T, near_rows, far_rows, near, pairs)


def pack_kernel(sizes, n, table, *refs):
    sources, (sent, out, sems, held, held_sem) = refs[: len(CHUNK_SOURCES[n])], refs[-5:]
    for k, source in enumerate(sources):

        @pl.when(table[sizes.source_at(n)] == k)
        def _(source=source):
            load = pltpu.make_async_copy(source, held, held_sem.at[0])
            load.start()
            load.wait()

    pack_from(sizes, n, table, held, out, sent, sems)


def pack(sizes, n, table, sources, after):
    order = sources[0].shape[1]
    return pl.pallas_call(
        functools.partial(pack_kernel, sizes, n),
        in_specs=[SMEM] + [HBM] * len(sources) + [KEPT] * len(after),
        out_specs=HBM,
        out_shape=send_shape(sizes, order),
        scratch_shapes=pack_scratch(sizes, order)
        + [pltpu.VMEM(sources[0].shape, jnp.bfloat16), pltpu.SemaphoreType.DMA((1,))],
        compiler_params=pltpu.CompilerParams(vmem_limit_bytes=WIDE_VMEM),
        cost_estimate=pl.CostEstimate(flops=PACK_FLOPS[n], bytes_accessed=0, transcendentals=0),
    )(table, *sources, *after)


def rows_kernel(after, *refs):
    for k, part in enumerate(refs[:-1]):
        refs[-1][k] = part[...]


def join_rows(parts, after):
    return pl.pallas_call(
        rows_kernel,
        in_specs=[KEPT] + [VMEM] * len(parts),
        out_specs=VMEM,
        out_shape=jax.ShapeDtypeStruct((len(parts),) + parts[0].shape, jnp.bfloat16),
        compiler_params=pltpu.CompilerParams(vmem_limit_bytes=VMEM_LIMIT),
        cost_estimate=pl.CostEstimate(flops=JOIN_FLOPS, bytes_accessed=0, transcendentals=0),
    )(after, *parts)


def fill_lefts(sizes, table, far_tiles, parts, lefts, x_halves):
    line, near1, near2, near3, relayed = parts
    shard = sizes.shard
    inner, outer = table[sizes.inner_at], table[sizes.outer_at]

    def place(z, part):
        for k in range(sizes.inner):
            x = lax.rem(inner + k, sizes.inner)
            at = pl.multiple_of((z * sizes.inner + x) * shard, ROW_ALIGN)
            for r in range(lefts.shape[0]):
                lefts[r, pl.ds(at, shard), :] = part[k, r]

    place(outer, line)
    amid = (outer == 1) | (outer == 2)
    for n, part in ((1, near1), (2, near2), (3, near3)):
        owner = table[sizes.owner_at(n)]
        pl.when(amid)(functools.partial(place, owner, part))
        pl.when(jnp.logical_not(amid))(functools.partial(place, owner, relayed.at[n - 1]))
    rank = far_tiles.shape[2]
    bases = jnp.concatenate([far_tiles[s, 0] for s in range(sizes.slots)], axis=0)
    for r in range(lefts.shape[0]):
        x_trans = jnp.dot(bases, lefts[r], preferred_element_type=jnp.float32)
        for s in range(sizes.slots):

            @pl.when(table[sizes.far_rows_at + s] == r)
            def _(s=s, own=x_trans[s * rank : (s + 1) * rank]):
                x_halves[s] = halves(own)


def halves(value):
    high = value.astype(jnp.bfloat16)
    low = (value - high.astype(jnp.float32)).astype(jnp.bfloat16)
    return jnp.concatenate([high, low], axis=0)


ACROSS = (((1,), (1,)), ((), ()))


def near_update(tile, left, panel):
    product = lax.dot_general(left, panel, ACROSS, preferred_element_type=jnp.float32)
    return (tile.astype(jnp.float32) - product).astype(jnp.bfloat16)


def far_update(tile, x_halves, pairs):
    rank = tile.shape[0]
    both = lax.dot_general(x_halves, pairs, ACROSS, preferred_element_type=jnp.float32)
    small = both[:rank] + both[rank:]
    turned = pltpu.roll(small, small.shape[1] - 1, 1)
    lane = lax.broadcasted_iota(jnp.int32, turned.shape, 1)
    turned = jnp.where(lane % 2 == 0, turned, 0.0)
    change = jnp.dot(halves(turned), pairs, preferred_element_type=jnp.float32)
    return (tile.astype(jnp.float32) - (change[:rank] + change[rank:])).astype(jnp.bfloat16)


def clear_rest(sizes, factors):
    filled = sizes.groups * sizes.far
    if filled < sizes.far_all:
        factors[filled:, :] = jnp.zeros_like(factors[filled:, :])


def take_part(sizes, g, part, panel, factors):
    quarter, far = sizes.quarter, sizes.far
    panel[g * quarter : (g + 1) * quarter, :] = part[0:quarter, :]
    factors[g * far : (g + 1) * far, :] = part[quarter : quarter + far, :]


def out_shapes(sizes, near_tiles, far_tiles):
    order, rank = near_tiles.shape[1], far_tiles.shape[2]
    return [
        jax.ShapeDtypeStruct((sizes.slots, order, order), jnp.bfloat16),
        jax.ShapeDtypeStruct((sizes.slots, rank, order), jnp.bfloat16),
    ]


def slot_loads(sizes, chunks, table, got, near_tiles, parts, tile, sems):
    slots, loads = [], []
    for k, n in enumerate(chunks):
        for x in range(sizes.inner):
            at = len(slots)
            slots.append(table[sizes.owner_at(n)] * sizes.inner + x)
            pairs = [(got[k].at[g * sizes.inner + x], parts.at[at, g]) for g in range(sizes.groups)]
            pairs.append((near_tiles.at[slots[at]], tile.at[at]))
            loads.append(
                [
                    pltpu.make_async_copy(source, to, sems.at[at, j])
                    for j, (source, to) in enumerate(pairs)
                ]
            )
    return slots, loads


def slot_update(
    sizes, at, slot, table, tile, v_tile, left, x_half, parts, done, outs, panel, factors, sems
):
    (near_done, far_done), (near_out, far_out) = done, outs
    for g in range(sizes.groups):
        take_part(sizes, g, parts.at[at, g], panel, factors)
    far_done[at] = far_update(v_tile, x_half, factors[...])
    store_at = sizes.groups + 3
    stores = [pltpu.make_async_copy(far_done.at[at], far_out.at[slot], sems.at[at, store_at])]
    stores[0].start()
    own_row = table[sizes.near_rows_at + slot]
    half = tile.shape[1] // 2
    for h in range(2):
        rows = pl.ds(h * half, half)
        near_done[at, rows, :] = near_update(tile[at, rows, :], left[own_row, rows, :], panel[...])
        stores.append(
            pltpu.make_async_copy(
                near_done.at[at, rows], near_out.at[slot, rows], sems.at[at, store_at + 1 + h]
            )
        )
        stores[-1].start()
    return stores


def first_update_kernel(sizes, chunks, table, near_tiles, far_tiles, *refs):
    rows_in, got = refs[:5], refs[5 : 5 + len(chunks)]
    near_out, far_out, lefts, x_halves = refs[5 + len(chunks) : 9 + len(chunks)]
    rows, (far_all, left, x_all, tile, parts, near_done, far_done, panel, factors, sems, few) = (
        refs[-16:-11],
        refs[-11:],
    )
    early = [pltpu.make_async_copy(part, to, few.at[j]) for j, (part, to) in enumerate(zip(rows_in, rows))]
    early.append(pltpu.make_async_copy(far_tiles, far_all, few.at[5]))
    slots, loads = slot_loads(sizes, chunks, table, got, near_tiles, parts, tile, sems)
    for load in early + sum(loads, []):
        load.start()
    clear_rest(sizes, factors)
    for load in early:
        load.wait()
    fill_lefts(sizes, table, far_all, rows, left, x_all)
    stores = [
        pltpu.make_async_copy(left, lefts, few.at[6]),
        pltpu.make_async_copy(x_all, x_halves, few.at[7]),
    ]
    for store in stores:
        store.start()
    done, outs = (near_done, far_done), (near_out, far_out)
    for at, slot in enumerate(slots):
        for load in loads[at]:
            load.wait()
        stores += slot_update(
            sizes, at, slot, table, tile, far_all[slot, 1], left, x_all[slot], parts, done, outs,
            panel, factors, sems,
        )
    for store in stores:
        store.wait()


def update_kernel(sizes, chunks, table, near_tiles, far_tiles, lefts, x_halves, *refs):
    got, (near_out, far_out) = refs[: len(chunks)], refs[-12:-10]
    tile, far_tile, left, x_half, parts, near_done, far_done, panel, factors, sems = refs[-10:]
    slots, loads = slot_loads(sizes, chunks, table, got, near_tiles, parts, tile, sems)
    for at, slot in enumerate(slots):
        j = sizes.groups + 1
        loads[at] += [
            pltpu.make_async_copy(x_halves.at[slot], x_half.at[at], sems.at[at, j]),
            pltpu.make_async_copy(far_tiles.at[slot, 1], far_tile.at[at], sems.at[at, j + 1]),
        ]
    left_loads = [
        pltpu.make_async_copy(lefts.at[r], left.at[r], sems.at[0, sizes.groups + 6 + r])
        for r in range(left.shape[0])
    ]
    for load in loads[0] + left_loads + sum(loads[1:], []):
        load.start()
    clear_rest(sizes, factors)
    for load in left_loads:
        load.wait()
    stores = []
    done, outs = (near_done, far_done), (near_out, far_out)
    for at, slot in enumerate(slots):
        for load in loads[at]:
            load.wait()
        stores += slot_update(
            sizes, at, slot, table, tile, far_tile[at], left, x_half[at], parts, done, outs,
            panel, factors, sems,
        )
    for store in stores:
        store.wait()


def first_update(sizes, chunks, table, near_tiles, far_tiles, rows, got):
    order, rank = near_tiles.shape[1], far_tiles.shape[2]
    groups, row_group = sizes.groups, rows[0].shape[1]
    count = len(chunks) * sizes.inner
    lefts = (row_group, order, order)
    x_halves = (sizes.slots, 2 * rank, order)
    return pl.pallas_call(
        functools.partial(first_update_kernel, sizes, chunks),
        in_specs=[SMEM] + [HBM] * (2 + len(rows) + len(got)),
        out_specs=[HBM] * 4,
        out_shape=out_shapes(sizes, near_tiles, far_tiles)
        + [jax.ShapeDtypeStruct(shape, jnp.bfloat16) for shape in (lefts, x_halves)],
        scratch_shapes=[pltpu.VMEM(part.shape, jnp.bfloat16) for part in rows]
        + [
            pltpu.VMEM(far_tiles.shape, jnp.bfloat16),
            pltpu.VMEM(lefts, jnp.bfloat16),
            pltpu.VMEM(x_halves, jnp.bfloat16),
            pltpu.VMEM((count, order, order), jnp.bfloat16),
            pltpu.VMEM((count, groups, sizes.quarter + sizes.far, order), jnp.bfloat16),
            pltpu.VMEM((count, order, order), jnp.bfloat16),
            pltpu.VMEM((count, rank, order), jnp.bfloat16),
            pltpu.VMEM((order, order), jnp.bfloat16),
            pltpu.VMEM((sizes.far_all, order), jnp.bfloat16),
            pltpu.SemaphoreType.DMA((count, groups + 6)),
            pltpu.SemaphoreType.DMA((8,)),
        ],
        compiler_params=pltpu.CompilerParams(vmem_limit_bytes=WIDE_VMEM),
        cost_estimate=pl.CostEstimate(
            flops=UPDATE_FLOPS * len(chunks), bytes_accessed=0, transcendentals=0
        ),
    )(table, near_tiles, far_tiles, *rows, *got)


def update(sizes, chunks, table, near_tiles, far_tiles, lefts, x_halves, got, before):
    order, rank = near_tiles.shape[1], far_tiles.shape[2]
    groups, row_group = sizes.groups, lefts.shape[0]
    count = len(chunks) * sizes.inner
    return pl.pallas_call(
        functools.partial(update_kernel, sizes, chunks),
        in_specs=[SMEM] + [HBM] * (4 + len(got) + len(before)),
        out_specs=[HBM, HBM],
        out_shape=out_shapes(sizes, near_tiles, far_tiles),
        scratch_shapes=[
            pltpu.VMEM((count, order, order), jnp.bfloat16),
            pltpu.VMEM((count, rank, order), jnp.bfloat16),
            pltpu.VMEM((row_group, order, order), jnp.bfloat16),
            pltpu.VMEM((count, 2 * rank, order), jnp.bfloat16),
            pltpu.VMEM((count, groups, sizes.quarter + sizes.far, order), jnp.bfloat16),
            pltpu.VMEM((count, order, order), jnp.bfloat16),
            pltpu.VMEM((count, rank, order), jnp.bfloat16),
            pltpu.VMEM((order, order), jnp.bfloat16),
            pltpu.VMEM((sizes.far_all, order), jnp.bfloat16),
            pltpu.SemaphoreType.DMA((count, groups + 6 + row_group)),
        ],
        input_output_aliases={5 + len(got) + k: k for k in range(len(before))},
        compiler_params=pltpu.CompilerParams(vmem_limit_bytes=WIDE_VMEM),
        cost_estimate=pl.CostEstimate(
            flops=UPDATE_FLOPS * len(chunks), bytes_accessed=0, transcendentals=0
        ),
    )(table, near_tiles, far_tiles, lefts, x_halves, *got, *before)


def shards(
    row_panel, col_near, col_far, near_tiles, near_rows, near_cols, far_tiles, far_rows, far_cols
):
    inner_size = lax.axis_size("inner")
    groups = lax.axis_size("gy") * lax.axis_size("core")
    per_bucket, quarter, order = col_near.shape
    row_group, shard = row_panel.shape[:2]
    far_pairs = jnp.swapaxes(col_far, 1, 2)
    far = -(-2 * col_far.shape[2] // FAR_ALIGN) * FAR_ALIGN
    sizes = Sizes(groups, inner_size, per_bucket, quarter, far, shard)

    def along(value, pairs):
        return lax.ppermute(value, "outer", pairs)

    rows = [row_panel]
    for k in range(1, inner_size):
        turn = [((i + k) % inner_size, i) for i in range(inner_size)]
        rows.append(lax.ppermute(row_panel, "inner", turn))

    table, own, send = first(
        sizes, near_cols, far_cols, near_rows, far_rows, col_near, far_pairs
    )
    held = {"own": own}
    held["pair"] = along(own, [(0, 1), (1, 0), (2, 3), (3, 2)])
    held["middle"] = along(own, [(1, 2), (2, 1)])
    held["cross"] = along(held["pair"], [(1, 2), (2, 1)])
    held["pass2"] = along(held["middle"], [(0, 1), (1, 0), (2, 3), (3, 2)])
    held["pass3"] = along(held["cross"], [(0, 1), (1, 0), (2, 3), (3, 2)])

    got = []
    for n in range(OUTER):
        if n > 0:
            after = [held["cross"]] if n == 2 else []
            send = pack(sizes, n, table, [held[name] for name in CHUNK_SOURCES[n]], after)
        got.append(lax.all_to_all(send, PLANE, split_axis=0, concat_axis=0, tiled=True))

    line = join_rows(rows, held["cross"])
    near1 = along(line, [(0, 1), (3, 2)])
    near2 = along(line, [(1, 2), (2, 1)])
    near3 = along(line, [(0, 2), (3, 1)])
    relayed = join_rows([line, near2, near3], held["pass3"])
    relayed = along(relayed, [(0, 1), (1, 0), (2, 3), (3, 2)])
    parts = [line, near1, near2, near3, relayed]
    *outs, lefts, x_halves = first_update(
        sizes, (0, 1, 2), table, near_tiles, far_tiles, parts, got[:3]
    )
    outs = update(sizes, (3,), table, near_tiles, far_tiles, lefts, x_halves, got[3:], outs)
    return tuple(outs)


def solution(mesh):
    groups, dev_count = mesh.shape["grp"], mesh.shape["dev"]
    fine = Mesh(
        mesh.devices.reshape(groups // 2, 2, OUTER, dev_count // OUTER),
        ("gy", "core", "outer", "inner"),
    )
    grp, dev = ("gy", "core"), ("outer", "inner")
    every = grp + dev
    placed = (
        P(grp, dev, None),
        P(dev, grp, None),
        P(dev, None, grp, None),
        P(every, None, None),
        P(every, None),
        P(),
        P(every, None, None, None),
        P(every, None),
        P(),
    )
    return jax.shard_map(
        shards,
        mesh=fine,
        in_specs=placed,
        out_specs=(P(every, None, None), P(every, None, None)),
        check_vma=False,
    )
```

```python
import functools

import jax
import jax.numpy as jnp
from jax import lax
from jax.experimental import pallas as pl
from jax.experimental.pallas import tpu as pltpu
from jax.sharding import Mesh, PartitionSpec as P

OUTER = 4
PLANE = ("gy", "core", "inner")
ROW_ALIGN = 16
FAR_ALIGN = 8
LANES = 128
VMEM_LIMIT = 16 * 1024 * 1024
WIDE_VMEM = 60 * 1024 * 1024
FULL_VMEM = 63 * 1024 * 1024
HBM = pl.BlockSpec(memory_space=pltpu.HBM)
CHUNK_OWNER = ((0, 1, 2, 3), (1, 0, 3, 2), (2, 2, 1, 1), (3, 3, 0, 0))
CHUNK_SOURCE = ((0, 0, 0, 0), (0, 0, 0, 0), (1, 0, 0, 1), (1, 0, 0, 1))
CHUNK_SOURCES = (("own",), ("pair",), ("middle", "pass2"), ("cross", "pass3"))
PACK_FLOPS = (0, 2 * 10**9, 10**10, 10**10)
JOIN_FLOPS = 10**9
UPDATE_FLOPS = 3 * 10**9
VMEM = pl.BlockSpec(memory_space=pltpu.VMEM)
SMEM = pl.BlockSpec(memory_space=pltpu.SMEM)
KEPT = pl.BlockSpec(memory_space=pl.ANY)


class Sizes:
    def __init__(self, groups, inner, per_bucket, quarter, far, shard):
        self.groups, self.inner, self.per_bucket = groups, inner, per_bucket
        self.quarter, self.far, self.shard = quarter, far, shard
        self.far_all = -(-groups * far // LANES) * LANES
        self.slots = OUTER * inner
        self.wanted = groups * inner
        self.stride = 2 * self.wanted + 2
        self.near_rows_at = OUTER * self.stride
        self.far_rows_at = self.near_rows_at + self.slots
        self.inner_at = self.far_rows_at + self.slots
        self.outer_at = self.inner_at + 1
        self.table = self.outer_at + 1

    def owner_at(self, n):
        return n * self.stride + 2 * self.wanted

    def source_at(self, n):
        return n * self.stride + 2 * self.wanted + 1


def by_position(values, position):
    result = jnp.int32(values[0])
    for k in range(1, len(values)):
        result = jnp.where(position == k, jnp.int32(values[k]), result)
    return result


def fill_table(sizes, near_cols, far_cols, near_rows, far_rows, table):
    outer, inner = lax.axis_index("outer"), lax.axis_index("inner")
    table[sizes.inner_at] = inner
    table[sizes.outer_at] = outer
    for n in range(OUTER):
        owner = by_position(CHUNK_OWNER[n], outer)
        table[sizes.owner_at(n)] = owner
        table[sizes.source_at(n)] = by_position(CHUNK_SOURCE[n], outer)
        bucket = owner * sizes.inner + inner
        for g in range(sizes.groups):
            for x in range(sizes.inner):
                at = g * sizes.inner + x
                device = (g * OUTER + outer) * sizes.inner + x
                first = bucket * sizes.per_bucket
                table[n * sizes.stride + at] = near_cols[bucket, device] - first
                table[n * sizes.stride + sizes.wanted + at] = far_cols[bucket, device] - first
    for s in range(sizes.slots):
        table[sizes.near_rows_at + s] = near_rows[0, s]
        table[sizes.far_rows_at + s] = far_rows[0, s]


def pack_from(sizes, n, table, source, out, sent, sems):
    quarter, far = sizes.quarter, sizes.far
    far_at = sizes.per_bucket * quarter
    copies = []
    for at in range(sizes.wanted):
        near_pick = table[n * sizes.stride + at] * quarter
        out[at, 0:quarter, :] = source[pl.ds(pl.multiple_of(near_pick, ROW_ALIGN), quarter), :]
        far_pick = table[n * sizes.stride + sizes.wanted + at]
        picked = source[far_at : far_at + far, :]
        for j in range(1, sizes.per_bucket):
            other = source[far_at + j * far : far_at + (j + 1) * far, :]
            picked = jnp.where(far_pick == j, other, picked)
        out[at, quarter : quarter + far, :] = picked
        copies.append(pltpu.make_async_copy(out.at[at], sent.at[at], sems.at[at]))
        copies[at].start()
    for copy in copies:
        copy.wait()


def pack_scratch(sizes, order):
    return [
        pltpu.VMEM((sizes.wanted, sizes.quarter + sizes.far, order), jnp.bfloat16),
        pltpu.SemaphoreType.DMA((sizes.wanted,)),
    ]


def first_kernel(sizes, near_cols, far_cols, near_rows, far_rows, near, pairs, *outs):
    table, own, sent, out, sems = outs
    fill_table(sizes, near_cols, far_cols, near_rows, far_rows, table)
    quarter, far = sizes.quarter, sizes.far
    far_at = sizes.per_bucket * quarter
    for j in range(sizes.per_bucket):
        own[j * quarter : (j + 1) * quarter, :] = near[j]
        at = far_at + j * far
        count = 2 * pairs.shape[1]
        for r in range(pairs.shape[1]):
            own[at + 2 * r : at + 2 * r + 2, :] = pairs[j, r]
        if count < far:
            own[at + count : at + far, :] = jnp.zeros((far - count, own.shape[1]), own.dtype)
    pack_from(sizes, 0, table, own, out, sent, sems)


def send_shape(sizes, order):
    return jax.ShapeDtypeStruct((sizes.wanted, sizes.quarter + sizes.far, order), jnp.bfloat16)


def first(sizes, near_cols, far_cols, near_rows, far_rows, near, pairs):
    order = near.shape[2]
    rows = sizes.per_bucket * (sizes.quarter + sizes.far)
    return pl.pallas_call(
        functools.partial(first_kernel, sizes),
        in_specs=[SMEM] * 4 + [VMEM] * 2,
        out_specs=[SMEM, VMEM, HBM],
        scratch_shapes=pack_scratch(sizes, order),
        out_shape=[
            jax.ShapeDtypeStruct((sizes.table,), jnp.int32),
            jax.ShapeDtypeStruct((rows, order), jnp.bfloat16),
            send_shape(sizes, order),
        ],
        compiler_params=pltpu.CompilerParams(vmem_limit_bytes=WIDE_VMEM),
        cost_estimate=pl.CostEstimate(flops=0, bytes_accessed=0, transcendentals=0),
    )(near_cols.T, far_cols.T, near_rows, far_rows, near, pairs)


def pack_kernel(sizes, n, table, *refs):
    sources, (sent, out, sems, held, held_sem) = refs[: len(CHUNK_SOURCES[n])], refs[-5:]
    for k, source in enumerate(sources):

        @pl.when(table[sizes.source_at(n)] == k)
        def _(source=source):
            load = pltpu.make_async_copy(source, held, held_sem.at[0])
            load.start()
            load.wait()

    pack_from(sizes, n, table, held, out, sent, sems)


def pack(sizes, n, table, sources, after):
    order = sources[0].shape[1]
    return pl.pallas_call(
        functools.partial(pack_kernel, sizes, n),
        in_specs=[SMEM] + [HBM] * len(sources) + [KEPT] * len(after),
        out_specs=HBM,
        out_shape=send_shape(sizes, order),
        scratch_shapes=pack_scratch(sizes, order)
        + [pltpu.VMEM(sources[0].shape, jnp.bfloat16), pltpu.SemaphoreType.DMA((1,))],
        compiler_params=pltpu.CompilerParams(vmem_limit_bytes=WIDE_VMEM),
        cost_estimate=pl.CostEstimate(flops=PACK_FLOPS[n], bytes_accessed=0, transcendentals=0),
    )(table, *sources, *after)


def rows_kernel(after, *refs):
    for k, part in enumerate(refs[:-1]):
        refs[-1][k] = part[...]


def join_rows(parts, after):
    return pl.pallas_call(
        rows_kernel,
        in_specs=[KEPT] + [VMEM] * len(parts),
        out_specs=VMEM,
        out_shape=jax.ShapeDtypeStruct((len(parts),) + parts[0].shape, jnp.bfloat16),
        compiler_params=pltpu.CompilerParams(vmem_limit_bytes=VMEM_LIMIT),
        cost_estimate=pl.CostEstimate(flops=JOIN_FLOPS, bytes_accessed=0, transcendentals=0),
    )(after, *parts)


def fill_lefts(sizes, table, far_tiles, parts, lefts, x_halves):
    line, near1, near2, near3, relayed = parts
    shard = sizes.shard
    inner, outer = table[sizes.inner_at], table[sizes.outer_at]

    def place(z, part):
        for k in range(sizes.inner):
            x = lax.rem(inner + k, sizes.inner)
            at = pl.multiple_of((z * sizes.inner + x) * shard, ROW_ALIGN)
            for r in range(lefts.shape[0]):
                lefts[r, pl.ds(at, shard), :] = part[k, r]

    place(outer, line)
    amid = (outer == 1) | (outer == 2)
    for n, part in ((1, near1), (2, near2), (3, near3)):
        owner = table[sizes.owner_at(n)]
        pl.when(amid)(functools.partial(place, owner, part))
        pl.when(jnp.logical_not(amid))(functools.partial(place, owner, relayed.at[n - 1]))
    rank = far_tiles.shape[2]
    bases = jnp.concatenate([far_tiles[s, 0] for s in range(sizes.slots)], axis=0)
    for r in range(lefts.shape[0]):
        x_trans = jnp.dot(bases, lefts[r], preferred_element_type=jnp.float32)
        for s in range(sizes.slots):

            @pl.when(table[sizes.far_rows_at + s] == r)
            def _(s=s, own=x_trans[s * rank : (s + 1) * rank]):
                x_halves[s] = halves(own)


def halves(value):
    high = value.astype(jnp.bfloat16)
    low = (value - high.astype(jnp.float32)).astype(jnp.bfloat16)
    return jnp.concatenate([high, low], axis=0)


ACROSS = (((1,), (1,)), ((), ()))


def near_update(tile, left, panel):
    product = lax.dot_general(left, panel, ACROSS, preferred_element_type=jnp.float32)
    return (tile.astype(jnp.float32) - product).astype(jnp.bfloat16)


def far_update(tile, x_halves, pairs):
    rank = tile.shape[0]
    both = lax.dot_general(x_halves, pairs, ACROSS, preferred_element_type=jnp.float32)
    small = both[:rank] + both[rank:]
    turned = pltpu.roll(small, small.shape[1] - 1, 1)
    lane = lax.broadcasted_iota(jnp.int32, turned.shape, 1)
    turned = jnp.where(lane % 2 == 0, turned, 0.0)
    change = jnp.dot(halves(turned), pairs, preferred_element_type=jnp.float32)
    return (tile.astype(jnp.float32) - (change[:rank] + change[rank:])).astype(jnp.bfloat16)


def clear_rest(sizes, factors):
    filled = sizes.groups * sizes.far
    if filled < sizes.far_all:
        factors[filled:, :] = jnp.zeros_like(factors[filled:, :])


def take_part(sizes, g, part, panel, factors):
    quarter, far = sizes.quarter, sizes.far
    panel[g * quarter : (g + 1) * quarter, :] = part[0:quarter, :]
    factors[g * far : (g + 1) * far, :] = part[quarter : quarter + far, :]


def out_shapes(sizes, near_tiles, far_tiles):
    order, rank = near_tiles.shape[1], far_tiles.shape[2]
    return [
        jax.ShapeDtypeStruct((sizes.slots, order, order), jnp.bfloat16),
        jax.ShapeDtypeStruct((sizes.slots, rank, order), jnp.bfloat16),
    ]


def slot_loads(sizes, chunks, table, got, near_tiles, parts, tile, sems):
    slots, loads = [], []
    for k, n in enumerate(chunks):
        for x in range(sizes.inner):
            at = len(slots)
            slots.append(table[sizes.owner_at(n)] * sizes.inner + x)
            pairs = [(got[k].at[g * sizes.inner + x], parts.at[at, g]) for g in range(sizes.groups)]
            pairs.append((near_tiles.at[slots[at]], tile.at[at]))
            loads.append(
                [
                    pltpu.make_async_copy(source, to, sems.at[at, j])
                    for j, (source, to) in enumerate(pairs)
                ]
            )
    return slots, loads


def slot_update(
    sizes, at, slot, table, tile, v_tile, left, x_half, parts, done, outs, panel, factors, sems
):
    (near_done, far_done), (near_out, far_out) = done, outs
    for g in range(sizes.groups):
        take_part(sizes, g, parts.at[at, g], panel, factors)
    far_done[at] = far_update(v_tile, x_half, factors[...])
    store_at = sizes.groups + 3
    stores = [pltpu.make_async_copy(far_done.at[at], far_out.at[slot], sems.at[at, store_at])]
    stores[0].start()
    own_row = table[sizes.near_rows_at + slot]
    half = tile.shape[1] // 2
    for h in range(2):
        rows = pl.ds(h * half, half)
        near_done[at, rows, :] = near_update(tile[at, rows, :], left[own_row, rows, :], panel[...])
        stores.append(
            pltpu.make_async_copy(
                near_done.at[at, rows], near_out.at[slot, rows], sems.at[at, store_at + 1 + h]
            )
        )
        stores[-1].start()
    return stores


def first_update_kernel(sizes, chunks, table, near_tiles, far_tiles, *refs):
    rows_in, got = refs[:5], refs[5 : 5 + len(chunks)]
    near_out, far_out, lefts, x_halves = refs[5 + len(chunks) : 9 + len(chunks)]
    rows, (far_all, left, x_all, tile, parts, near_done, far_done, panel, factors, sems, few) = (
        refs[-16:-11],
        refs[-11:],
    )
    early = [pltpu.make_async_copy(part, to, few.at[j]) for j, (part, to) in enumerate(zip(rows_in, rows))]
    early.append(pltpu.make_async_copy(far_tiles, far_all, few.at[5]))
    slots, loads = slot_loads(sizes, chunks, table, got, near_tiles, parts, tile, sems)
    for load in early + sum(loads, []):
        load.start()
    clear_rest(sizes, factors)
    for load in early:
        load.wait()
    fill_lefts(sizes, table, far_all, rows, left, x_all)
    stores = [
        pltpu.make_async_copy(left, lefts, few.at[6]),
        pltpu.make_async_copy(x_all, x_halves, few.at[7]),
    ]
    for store in stores:
        store.start()
    done, outs = (near_done, far_done), (near_out, far_out)
    for at, slot in enumerate(slots):
        for load in loads[at]:
            load.wait()
        stores += slot_update(
            sizes, at, slot, table, tile, far_all[slot, 1], left, x_all[slot], parts, done, outs,
            panel, factors, sems,
        )
    for store in stores:
        store.wait()


def update_kernel(sizes, chunks, table, near_tiles, far_tiles, lefts, x_halves, *refs):
    got, (near_out, far_out) = refs[: len(chunks)], refs[-12:-10]
    tile, far_tile, left, x_half, parts, near_done, far_done, panel, factors, sems = refs[-10:]
    slots, loads = slot_loads(sizes, chunks, table, got, near_tiles, parts, tile, sems)
    for at, slot in enumerate(slots):
        j = sizes.groups + 1
        loads[at] += [
            pltpu.make_async_copy(x_halves.at[slot], x_half.at[at], sems.at[at, j]),
            pltpu.make_async_copy(far_tiles.at[slot, 1], far_tile.at[at], sems.at[at, j + 1]),
        ]
    left_loads = [
        pltpu.make_async_copy(lefts.at[r], left.at[r], sems.at[0, sizes.groups + 6 + r])
        for r in range(left.shape[0])
    ]
    for load in loads[0] + left_loads + sum(loads[1:], []):
        load.start()
    clear_rest(sizes, factors)
    for load in left_loads:
        load.wait()
    stores = []
    done, outs = (near_done, far_done), (near_out, far_out)
    for at, slot in enumerate(slots):
        for load in loads[at]:
            load.wait()
        stores += slot_update(
            sizes, at, slot, table, tile, far_tile[at], left, x_half[at], parts, done, outs,
            panel, factors, sems,
        )
    for store in stores:
        store.wait()


def first_update(sizes, chunks, table, near_tiles, far_tiles, rows, got):
    order, rank = near_tiles.shape[1], far_tiles.shape[2]
    groups, row_group = sizes.groups, rows[0].shape[1]
    count = len(chunks) * sizes.inner
    lefts = (row_group, order, order)
    x_halves = (sizes.slots, 2 * rank, order)
    return pl.pallas_call(
        functools.partial(first_update_kernel, sizes, chunks),
        in_specs=[SMEM] + [HBM] * (2 + len(rows) + len(got)),
        out_specs=[HBM] * 4,
        out_shape=out_shapes(sizes, near_tiles, far_tiles)
        + [jax.ShapeDtypeStruct(shape, jnp.bfloat16) for shape in (lefts, x_halves)],
        scratch_shapes=[pltpu.VMEM(part.shape, jnp.bfloat16) for part in rows]
        + [
            pltpu.VMEM(far_tiles.shape, jnp.bfloat16),
            pltpu.VMEM(lefts, jnp.bfloat16),
            pltpu.VMEM(x_halves, jnp.bfloat16),
            pltpu.VMEM((count, order, order), jnp.bfloat16),
            pltpu.VMEM((count, groups, sizes.quarter + sizes.far, order), jnp.bfloat16),
            pltpu.VMEM((count, order, order), jnp.bfloat16),
            pltpu.VMEM((count, rank, order), jnp.bfloat16),
            pltpu.VMEM((order, order), jnp.bfloat16),
            pltpu.VMEM((sizes.far_all, order), jnp.bfloat16),
            pltpu.SemaphoreType.DMA((count, groups + 6)),
            pltpu.SemaphoreType.DMA((8,)),
        ],
        compiler_params=pltpu.CompilerParams(vmem_limit_bytes=FULL_VMEM),
        cost_estimate=pl.CostEstimate(
            flops=UPDATE_FLOPS * len(chunks), bytes_accessed=0, transcendentals=0
        ),
    )(table, near_tiles, far_tiles, *rows, *got)


def update(sizes, chunks, table, near_tiles, far_tiles, lefts, x_halves, got, before):
    order, rank = near_tiles.shape[1], far_tiles.shape[2]
    groups, row_group = sizes.groups, lefts.shape[0]
    count = len(chunks) * sizes.inner
    return pl.pallas_call(
        functools.partial(update_kernel, sizes, chunks),
        in_specs=[SMEM] + [HBM] * (4 + len(got) + len(before)),
        out_specs=[HBM, HBM],
        out_shape=out_shapes(sizes, near_tiles, far_tiles),
        scratch_shapes=[
            pltpu.VMEM((count, order, order), jnp.bfloat16),
            pltpu.VMEM((count, rank, order), jnp.bfloat16),
            pltpu.VMEM((row_group, order, order), jnp.bfloat16),
            pltpu.VMEM((count, 2 * rank, order), jnp.bfloat16),
            pltpu.VMEM((count, groups, sizes.quarter + sizes.far, order), jnp.bfloat16),
            pltpu.VMEM((count, order, order), jnp.bfloat16),
            pltpu.VMEM((count, rank, order), jnp.bfloat16),
            pltpu.VMEM((order, order), jnp.bfloat16),
            pltpu.VMEM((sizes.far_all, order), jnp.bfloat16),
            pltpu.SemaphoreType.DMA((count, groups + 6 + row_group)),
        ],
        input_output_aliases={5 + len(got) + k: k for k in range(len(before))},
        compiler_params=pltpu.CompilerParams(vmem_limit_bytes=FULL_VMEM),
        cost_estimate=pl.CostEstimate(
            flops=UPDATE_FLOPS * len(chunks), bytes_accessed=0, transcendentals=0
        ),
    )(table, near_tiles, far_tiles, lefts, x_halves, *got, *before)


def shards(
    row_panel, col_near, col_far, near_tiles, near_rows, near_cols, far_tiles, far_rows, far_cols
):
    inner_size = lax.axis_size("inner")
    groups = lax.axis_size("gy") * lax.axis_size("core")
    per_bucket, quarter, order = col_near.shape
    row_group, shard = row_panel.shape[:2]
    far_pairs = jnp.swapaxes(col_far, 1, 2)
    far = -(-2 * col_far.shape[2] // FAR_ALIGN) * FAR_ALIGN
    sizes = Sizes(groups, inner_size, per_bucket, quarter, far, shard)

    def along(value, pairs):
        return lax.ppermute(value, "outer", pairs)

    rows = [row_panel]
    for k in range(1, inner_size):
        turn = [((i + k) % inner_size, i) for i in range(inner_size)]
        rows.append(lax.ppermute(row_panel, "inner", turn))

    table, own, send = first(
        sizes, near_cols, far_cols, near_rows, far_rows, col_near, far_pairs
    )
    held = {"own": own}
    held["pair"] = along(own, [(0, 1), (1, 0), (2, 3), (3, 2)])
    held["middle"] = along(own, [(1, 2), (2, 1)])
    held["cross"] = along(held["pair"], [(1, 2), (2, 1)])
    held["pass2"] = along(held["middle"], [(0, 1), (1, 0), (2, 3), (3, 2)])
    held["pass3"] = along(held["cross"], [(0, 1), (1, 0), (2, 3), (3, 2)])

    got = []
    for n in range(OUTER):
        if n > 0:
            after = [held["cross"]] if n == 2 else []
            send = pack(sizes, n, table, [held[name] for name in CHUNK_SOURCES[n]], after)
        got.append(lax.all_to_all(send, PLANE, split_axis=0, concat_axis=0, tiled=True))

    line = join_rows(rows, held["cross"])
    near1 = along(line, [(0, 1), (3, 2)])
    near2 = along(line, [(1, 2), (2, 1)])
    near3 = along(line, [(0, 2), (3, 1)])
    relayed = join_rows([line, near2, near3], held["pass2"])
    relayed = along(relayed, [(0, 1), (1, 0), (2, 3), (3, 2)])
    parts = [line, near1, near2, near3, relayed]
    *outs, lefts, x_halves = first_update(
        sizes, (0, 1, 2), table, near_tiles, far_tiles, parts, got[:3]
    )
    outs = update(sizes, (3,), table, near_tiles, far_tiles, lefts, x_halves, got[3:], outs)
    return tuple(outs)


def solution(mesh):
    groups, dev_count = mesh.shape["grp"], mesh.shape["dev"]
    fine = Mesh(
        mesh.devices.reshape(groups // 2, 2, OUTER, dev_count // OUTER),
        ("gy", "core", "outer", "inner"),
    )
    grp, dev = ("gy", "core"), ("outer", "inner")
    every = grp + dev
    placed = (
        P(grp, dev, None),
        P(dev, grp, None),
        P(dev, None, grp, None),
        P(every, None, None),
        P(every, None),
        P(),
        P(every, None, None, None),
        P(every, None),
        P(),
    )
    return jax.shard_map(
        shards,
        mesh=fine,
        in_specs=placed,
        out_specs=(P(every, None, None), P(every, None, None)),
        check_vma=False,
    )
```

```python
import functools

import jax
import jax.numpy as jnp
from jax import lax
from jax.experimental import pallas as pl
from jax.experimental.pallas import tpu as pltpu
from jax.sharding import Mesh, PartitionSpec as P

OUTER = 4
PLANE = ("gy", "core", "inner")
ROW_ALIGN = 16
FAR_ALIGN = 8
LANES = 128
VMEM_LIMIT = 16 * 1024 * 1024
WIDE_VMEM = 60 * 1024 * 1024
LEFTS_VMEM = 24 * 1024 * 1024
HBM = pl.BlockSpec(memory_space=pltpu.HBM)
CHUNK_OWNER = ((0, 1, 2, 3), (1, 0, 3, 2), (2, 2, 1, 1), (3, 3, 0, 0))
CHUNK_SOURCE = ((0, 0, 0, 0), (0, 0, 0, 0), (1, 0, 0, 1), (1, 0, 0, 1))
CHUNK_SOURCES = (("own",), ("pair",), ("middle", "pass2"), ("cross", "pass3"))
PACK_FLOPS = (0, 2 * 10**9, 10**10, 10**10)
JOIN_FLOPS = 10**9
UPDATE_FLOPS = 3 * 10**9
VMEM = pl.BlockSpec(memory_space=pltpu.VMEM)
SMEM = pl.BlockSpec(memory_space=pltpu.SMEM)
KEPT = pl.BlockSpec(memory_space=pl.ANY)


class Sizes:
    def __init__(self, groups, inner, per_bucket, quarter, far, shard):
        self.groups, self.inner, self.per_bucket = groups, inner, per_bucket
        self.quarter, self.far, self.shard = quarter, far, shard
        self.far_all = -(-groups * far // LANES) * LANES
        self.slots = OUTER * inner
        self.wanted = groups * inner
        self.stride = 2 * self.wanted + 2
        self.near_rows_at = OUTER * self.stride
        self.far_rows_at = self.near_rows_at + self.slots
        self.inner_at = self.far_rows_at + self.slots
        self.outer_at = self.inner_at + 1
        self.table = self.outer_at + 1

    def owner_at(self, n):
        return n * self.stride + 2 * self.wanted

    def source_at(self, n):
        return n * self.stride + 2 * self.wanted + 1


def by_position(values, position):
    result = jnp.int32(values[0])
    for k in range(1, len(values)):
        result = jnp.where(position == k, jnp.int32(values[k]), result)
    return result


def fill_table(sizes, near_cols, far_cols, near_rows, far_rows, table):
    outer, inner = lax.axis_index("outer"), lax.axis_index("inner")
    table[sizes.inner_at] = inner
    table[sizes.outer_at] = outer
    for n in range(OUTER):
        owner = by_position(CHUNK_OWNER[n], outer)
        table[sizes.owner_at(n)] = owner
        table[sizes.source_at(n)] = by_position(CHUNK_SOURCE[n], outer)
        bucket = owner * sizes.inner + inner
        for g in range(sizes.groups):
            for x in range(sizes.inner):
                at = g * sizes.inner + x
                device = (g * OUTER + outer) * sizes.inner + x
                first = bucket * sizes.per_bucket
                table[n * sizes.stride + at] = near_cols[bucket, device] - first
                table[n * sizes.stride + sizes.wanted + at] = far_cols[bucket, device] - first
    for s in range(sizes.slots):
        table[sizes.near_rows_at + s] = near_rows[0, s]
        table[sizes.far_rows_at + s] = far_rows[0, s]


def pack_from(sizes, n, table, source, out, sent, sems):
    quarter, far = sizes.quarter, sizes.far
    far_at = sizes.per_bucket * quarter
    copies = []
    for at in range(sizes.wanted):
        near_pick = table[n * sizes.stride + at] * quarter
        out[at, 0:quarter, :] = source[pl.ds(pl.multiple_of(near_pick, ROW_ALIGN), quarter), :]
        far_pick = table[n * sizes.stride + sizes.wanted + at]
        picked = source[far_at : far_at + far, :]
        for j in range(1, sizes.per_bucket):
            other = source[far_at + j * far : far_at + (j + 1) * far, :]
            picked = jnp.where(far_pick == j, other, picked)
        out[at, quarter : quarter + far, :] = picked
        copies.append(pltpu.make_async_copy(out.at[at], sent.at[at], sems.at[at]))
        copies[at].start()
    for copy in copies:
        copy.wait()


def pack_scratch(sizes, order):
    return [
        pltpu.VMEM((sizes.wanted, sizes.quarter + sizes.far, order), jnp.bfloat16),
        pltpu.SemaphoreType.DMA((sizes.wanted,)),
    ]


def first_kernel(sizes, near_cols, far_cols, near_rows, far_rows, near, pairs, *outs):
    table, own, sent, out, sems = outs
    fill_table(sizes, near_cols, far_cols, near_rows, far_rows, table)
    quarter, far = sizes.quarter, sizes.far
    far_at = sizes.per_bucket * quarter
    for j in range(sizes.per_bucket):
        own[j * quarter : (j + 1) * quarter, :] = near[j]
        at = far_at + j * far
        count = 2 * pairs.shape[1]
        for r in range(pairs.shape[1]):
            own[at + 2 * r : at + 2 * r + 2, :] = pairs[j, r]
        if count < far:
            own[at + count : at + far, :] = jnp.zeros((far - count, own.shape[1]), own.dtype)
    pack_from(sizes, 0, table, own, out, sent, sems)


def send_shape(sizes, order):
    return jax.ShapeDtypeStruct((sizes.wanted, sizes.quarter + sizes.far, order), jnp.bfloat16)


def first(sizes, near_cols, far_cols, near_rows, far_rows, near, pairs):
    order = near.shape[2]
    rows = sizes.per_bucket * (sizes.quarter + sizes.far)
    return pl.pallas_call(
        functools.partial(first_kernel, sizes),
        in_specs=[SMEM] * 4 + [VMEM] * 2,
        out_specs=[SMEM, VMEM, HBM],
        scratch_shapes=pack_scratch(sizes, order),
        out_shape=[
            jax.ShapeDtypeStruct((sizes.table,), jnp.int32),
            jax.ShapeDtypeStruct((rows, order), jnp.bfloat16),
            send_shape(sizes, order),
        ],
        compiler_params=pltpu.CompilerParams(vmem_limit_bytes=WIDE_VMEM),
        cost_estimate=pl.CostEstimate(flops=0, bytes_accessed=0, transcendentals=0),
    )(near_cols.T, far_cols.T, near_rows, far_rows, near, pairs)


def pack_kernel(sizes, n, table, *refs):
    sources, (sent, out, sems, held, held_sem) = refs[: len(CHUNK_SOURCES[n])], refs[-5:]
    for k, source in enumerate(sources):

        @pl.when(table[sizes.source_at(n)] == k)
        def _(source=source):
            load = pltpu.make_async_copy(source, held, held_sem.at[0])
            load.start()
            load.wait()

    pack_from(sizes, n, table, held, out, sent, sems)


def pack(sizes, n, table, sources, after):
    order = sources[0].shape[1]
    return pl.pallas_call(
        functools.partial(pack_kernel, sizes, n),
        in_specs=[SMEM] + [HBM] * len(sources) + [KEPT] * len(after),
        out_specs=HBM,
        out_shape=send_shape(sizes, order),
        scratch_shapes=pack_scratch(sizes, order)
        + [pltpu.VMEM(sources[0].shape, jnp.bfloat16), pltpu.SemaphoreType.DMA((1,))],
        compiler_params=pltpu.CompilerParams(vmem_limit_bytes=WIDE_VMEM),
        cost_estimate=pl.CostEstimate(flops=PACK_FLOPS[n], bytes_accessed=0, transcendentals=0),
    )(table, *sources, *after)


def rows_kernel(after, *refs):
    for k, part in enumerate(refs[:-1]):
        refs[-1][k] = part[...]


def join_rows(parts, after):
    return pl.pallas_call(
        rows_kernel,
        in_specs=[KEPT] + [VMEM] * len(parts),
        out_specs=VMEM,
        out_shape=jax.ShapeDtypeStruct((len(parts),) + parts[0].shape, jnp.bfloat16),
        compiler_params=pltpu.CompilerParams(vmem_limit_bytes=VMEM_LIMIT),
        cost_estimate=pl.CostEstimate(flops=JOIN_FLOPS, bytes_accessed=0, transcendentals=0),
    )(after, *parts)


def lefts_kernel(sizes, table, far_tiles, line, near1, near2, near3, relayed, lefts, x_halves):
    shard = sizes.shard
    inner, outer = table[sizes.inner_at], table[sizes.outer_at]

    def place(z, part):
        for k in range(sizes.inner):
            x = lax.rem(inner + k, sizes.inner)
            at = pl.multiple_of((z * sizes.inner + x) * shard, ROW_ALIGN)
            for r in range(lefts.shape[0]):
                lefts[r, pl.ds(at, shard), :] = part[k, r]

    place(outer, line)
    amid = (outer == 1) | (outer == 2)
    for n, part in ((1, near1), (2, near2), (3, near3)):
        owner = table[sizes.owner_at(n)]
        pl.when(amid)(functools.partial(place, owner, part))
        pl.when(jnp.logical_not(amid))(functools.partial(place, owner, relayed.at[n - 1]))
    rank = far_tiles.shape[2]
    bases = jnp.concatenate([far_tiles[s, 0] for s in range(sizes.slots)], axis=0)
    for r in range(lefts.shape[0]):
        x_trans = jnp.dot(bases, lefts[r], preferred_element_type=jnp.float32)
        for s in range(sizes.slots):

            @pl.when(table[sizes.far_rows_at + s] == r)
            def _(s=s, own=x_trans[s * rank : (s + 1) * rank]):
                x_halves[s] = halves(own)


def make_lefts(sizes, table, far_tiles, parts):
    row_group, _, order = parts[0].shape[1:]
    rank = far_tiles.shape[2]
    return pl.pallas_call(
        functools.partial(lefts_kernel, sizes),
        in_specs=[SMEM, VMEM] + [VMEM] * len(parts),
        out_specs=[VMEM, VMEM],
        out_shape=[
            jax.ShapeDtypeStruct((row_group, order, order), jnp.bfloat16),
            jax.ShapeDtypeStruct((sizes.slots, 2 * rank, order), jnp.bfloat16),
        ],
        compiler_params=pltpu.CompilerParams(vmem_limit_bytes=LEFTS_VMEM),
        cost_estimate=pl.CostEstimate(flops=0, bytes_accessed=0, transcendentals=0),
    )(table, far_tiles, *parts)


def halves(value):
    high = value.astype(jnp.bfloat16)
    low = (value - high.astype(jnp.float32)).astype(jnp.bfloat16)
    return jnp.concatenate([high, low], axis=0)


ACROSS = (((1,), (1,)), ((), ()))


def near_update(tile, left, panel):
    product = lax.dot_general(left, panel, ACROSS, preferred_element_type=jnp.float32)
    return (tile.astype(jnp.float32) - product).astype(jnp.bfloat16)


def far_update(tile, x_halves, pairs):
    rank = tile.shape[0]
    both = lax.dot_general(x_halves, pairs, ACROSS, preferred_element_type=jnp.float32)
    small = both[:rank] + both[rank:]
    turned = pltpu.roll(small, small.shape[1] - 1, 1)
    lane = lax.broadcasted_iota(jnp.int32, turned.shape, 1)
    turned = jnp.where(lane % 2 == 0, turned, 0.0)
    change = jnp.dot(halves(turned), pairs, preferred_element_type=jnp.float32)
    return (tile.astype(jnp.float32) - (change[:rank] + change[rank:])).astype(jnp.bfloat16)


def clear_rest(sizes, factors):
    filled = sizes.groups * sizes.far
    if filled < sizes.far_all:
        factors[filled:, :] = jnp.zeros_like(factors[filled:, :])


def take_part(sizes, g, part, panel, factors):
    quarter, far = sizes.quarter, sizes.far
    panel[g * quarter : (g + 1) * quarter, :] = part[0:quarter, :]
    factors[g * far : (g + 1) * far, :] = part[quarter : quarter + far, :]


def out_shapes(sizes, near_tiles, far_tiles):
    order, rank = near_tiles.shape[1], far_tiles.shape[2]
    return [
        jax.ShapeDtypeStruct((sizes.slots, order, order), jnp.bfloat16),
        jax.ShapeDtypeStruct((sizes.slots, rank, order), jnp.bfloat16),
    ]


def update_kernel(sizes, chunks, table, near_tiles, far_tiles, lefts, x_halves, *refs):
    got, (near_out, far_out) = refs[: len(chunks)], refs[-12:-10]
    tile, far_tile, left, x_half, parts, near_done, far_done, panel, factors, sems = refs[-10:]
    left_loads = [
        pltpu.make_async_copy(lefts.at[r], left.at[r], sems.at[0, sizes.groups + 5 + r])
        for r in range(left.shape[0])
    ]
    slots, loads = [], []
    for k, n in enumerate(chunks):
        for x in range(sizes.inner):
            at = len(slots)
            slot = table[sizes.owner_at(n)] * sizes.inner + x
            pairs = [(got[k].at[g * sizes.inner + x], parts.at[at, g]) for g in range(sizes.groups)]
            pairs += [
                (near_tiles.at[slot], tile.at[at]),
                (x_halves.at[slot], x_half.at[at]),
                (far_tiles.at[slot, 1], far_tile.at[at]),
            ]
            slots.append(slot)
            loads.append(
                [
                    pltpu.make_async_copy(source, to, sems.at[at, j])
                    for j, (source, to) in enumerate(pairs)
                ]
            )
    for load in loads[0] + left_loads + sum(loads[1:], []):
        load.start()
    clear_rest(sizes, factors)
    for load in left_loads:
        load.wait()
    stores = []
    for at, slot in enumerate(slots):
        for load in loads[at]:
            load.wait()
        for g in range(sizes.groups):
            take_part(sizes, g, parts.at[at, g], panel, factors)
        own_left = left[table[sizes.near_rows_at + slot]]
        near_done[at] = near_update(tile[at], own_left, panel[...])
        far_done[at] = far_update(far_tile[at], x_half[at], factors[...])
        for j, (done, out) in enumerate(((near_done, near_out), (far_done, far_out))):
            copy = pltpu.make_async_copy(
                done.at[at], out.at[slot], sems.at[at, sizes.groups + 3 + j]
            )
            copy.start()
            stores.append(copy)
    for store in stores:
        store.wait()


def update(sizes, chunks, table, near_tiles, far_tiles, lefts, x_halves, got, before):
    order, rank = near_tiles.shape[1], far_tiles.shape[2]
    groups, row_group = sizes.groups, lefts.shape[0]
    count = len(chunks) * sizes.inner
    return pl.pallas_call(
        functools.partial(update_kernel, sizes, chunks),
        in_specs=[SMEM] + [HBM] * (4 + len(got) + len(before)),
        out_specs=[HBM, HBM],
        out_shape=out_shapes(sizes, near_tiles, far_tiles),
        scratch_shapes=[
            pltpu.VMEM((count, order, order), jnp.bfloat16),
            pltpu.VMEM((count, rank, order), jnp.bfloat16),
            pltpu.VMEM((row_group, order, order), jnp.bfloat16),
            pltpu.VMEM((count, 2 * rank, order), jnp.bfloat16),
            pltpu.VMEM((count, groups, sizes.quarter + sizes.far, order), jnp.bfloat16),
            pltpu.VMEM((count, order, order), jnp.bfloat16),
            pltpu.VMEM((count, rank, order), jnp.bfloat16),
            pltpu.VMEM((order, order), jnp.bfloat16),
            pltpu.VMEM((sizes.far_all, order), jnp.bfloat16),
            pltpu.SemaphoreType.DMA((count, groups + 5 + row_group)),
        ],
        input_output_aliases={5 + len(got) + k: k for k in range(len(before))},
        compiler_params=pltpu.CompilerParams(vmem_limit_bytes=WIDE_VMEM),
        cost_estimate=pl.CostEstimate(
            flops=UPDATE_FLOPS * len(chunks), bytes_accessed=0, transcendentals=0
        ),
    )(table, near_tiles, far_tiles, lefts, x_halves, *got, *before)


def shards(
    row_panel, col_near, col_far, near_tiles, near_rows, near_cols, far_tiles, far_rows, far_cols
):
    inner_size = lax.axis_size("inner")
    groups = lax.axis_size("gy") * lax.axis_size("core")
    per_bucket, quarter, order = col_near.shape
    row_group, shard = row_panel.shape[:2]
    far_pairs = jnp.swapaxes(col_far, 1, 2)
    far = -(-2 * col_far.shape[2] // FAR_ALIGN) * FAR_ALIGN
    sizes = Sizes(groups, inner_size, per_bucket, quarter, far, shard)

    def along(value, pairs):
        return lax.ppermute(value, "outer", pairs)

    rows = [row_panel]
    for k in range(1, inner_size):
        turn = [((i + k) % inner_size, i) for i in range(inner_size)]
        rows.append(lax.ppermute(row_panel, "inner", turn))

    table, own, send = first(
        sizes, near_cols, far_cols, near_rows, far_rows, col_near, far_pairs
    )
    held = {"own": own}
    held["pair"] = along(own, [(0, 1), (1, 0), (2, 3), (3, 2)])
    held["middle"] = along(own, [(1, 2), (2, 1)])
    held["cross"] = along(held["pair"], [(1, 2), (2, 1)])
    held["pass2"] = along(held["middle"], [(0, 1), (1, 0), (2, 3), (3, 2)])
    held["pass3"] = along(held["cross"], [(0, 1), (1, 0), (2, 3), (3, 2)])

    got = []
    for n in range(OUTER):
        if n > 0:
            after = [held["cross"]] if n == 2 else []
            send = pack(sizes, n, table, [held[name] for name in CHUNK_SOURCES[n]], after)
        got.append(lax.all_to_all(send, PLANE, split_axis=0, concat_axis=0, tiled=True))

    line = join_rows(rows, held["cross"])
    near1 = along(line, [(0, 1), (3, 2)])
    near2 = along(line, [(1, 2), (2, 1)])
    near3 = along(line, [(0, 2), (3, 1)])
    relayed = join_rows([line, near2, near3], held["pass2"])
    relayed = along(relayed, [(0, 1), (1, 0), (2, 3), (3, 2)])
    parts = [line, near1, near2, near3, relayed]
    lefts, x_halves = make_lefts(sizes, table, far_tiles, parts)
    tiles = (near_tiles, far_tiles, lefts, x_halves)
    outs = update(sizes, (0, 1, 2), table, *tiles, got[:3], ())
    outs = update(sizes, (3,), table, *tiles, got[3:], outs)
    return tuple(outs)


def solution(mesh):
    groups, dev_count = mesh.shape["grp"], mesh.shape["dev"]
    fine = Mesh(
        mesh.devices.reshape(groups // 2, 2, OUTER, dev_count // OUTER),
        ("gy", "core", "outer", "inner"),
    )
    grp, dev = ("gy", "core"), ("outer", "inner")
    every = grp + dev
    placed = (
        P(grp, dev, None),
        P(dev, grp, None),
        P(dev, None, grp, None),
        P(every, None, None),
        P(every, None),
        P(),
        P(every, None, None, None),
        P(every, None),
        P(),
    )
    return jax.shard_map(
        shards,
        mesh=fine,
        in_specs=placed,
        out_specs=(P(every, None, None), P(every, None, None)),
        check_vma=False,
    )
```
